32 devices in a mesh: wide: 8 (over z, x), narrow: 4 (over y, core).
Axes of the slice: x: 2, y: 2, z: 4, core: 2. Of those that a mesh axis runs over, the one named last changes fastest.
Arguments:
- block_in: bfloat16 [128, 208, 768], P(('wide', 'narrow')), may hold values from -6 to 6
- out_grad: bfloat16 [128, 208, 768], P(('wide', 'narrow')), may hold values from -6 to 6
- lengths: int32 [128], P(('wide', 'narrow')), may hold values from 10 to 202, as said below
- feature_proj: float32 [12, 32, 64], replicated, may hold values from -5 to 5
- attn_in: float32 [3, 768, 768], P(None, 'wide'), may hold values from -0.21875 to 0.21875
- attn_out: float32 [768, 768], P('wide'), may hold values from -1.75 to 1.75
- ffn_in: float32 [768, 3072], P('wide'), may hold values from -0.21875 to 0.21875
- ffn_out: float32 [3072, 768], P('wide'), may hold values from -0.109375 to 0.109375
- norm_params: float32 [4, 768], P(None, 'wide')
- bias_in: float32 [3072], P('wide'), may hold values from -4 to 4
- bias_out: float32 [768], P('wide'), may hold values from -4 to 4
- mom_attn_in: float32 [3, 768, 768], P(None, 'wide', 'narrow')
- mom_attn_out: float32 [768, 768], P('wide', 'narrow')
- mom_ffn_in: float32 [768, 3072], P('wide', 'narrow')
- mom_ffn_out: float32 [3072, 768], P('wide', 'narrow')
- first_norms: float32 [4, 768], P(None, ('wide', 'narrow'))
- first_bias_in: float32 [3072], P(('wide', 'narrow'))
- first_bias_out: float32 [768], P(('wide', 'narrow'))
- second_norms: float32 [4, 768], P(None, ('wide', 'narrow'))
- second_bias_in: float32 [3072], P(('wide', 'narrow'))
- second_bias_out: float32 [768], P(('wide', 'narrow'))
Outputs:
- block_out: float32 [128, 208, 768], P(('wide', 'narrow'))
- input_grad: float32 [128, 208, 768], P(('wide', 'narrow'))
- grad_attn_in: float32 [3, 768, 768], P(None, 'wide', 'narrow')
- grad_attn_out: float32 [768, 768], P('wide', 'narrow')
- grad_ffn_in: float32 [768, 3072], P('wide', 'narrow')
- grad_ffn_out: float32 [3072, 768], P('wide', 'narrow')
- grad_norms: float32 [4, 768], P(None, ('wide', 'narrow'))
- grad_bias_in: float32 [3072], P(('wide', 'narrow'))
- grad_bias_out: float32 [768], P(('wide', 'narrow'))
- new_mom_attn_in: float32 [3, 768, 768], P(None, 'wide', 'narrow')
- new_mom_attn_out: float32 [768, 768], P('wide', 'narrow')
- new_mom_ffn_in: float32 [768, 3072], P('wide', 'narrow')
- new_mom_ffn_out: float32 [3072, 768], P('wide', 'narrow')
- new_attn_in: float32 [3, 768, 768], P(None, 'wide', 'narrow')
- new_attn_out: float32 [768, 768], P('wide', 'narrow')
- new_ffn_in: float32 [768, 3072], P('wide', 'narrow')
- new_ffn_out: float32 [3072, 768], P('wide', 'narrow')
- new_first_norms: float32 [4, 768], P(None, ('wide', 'narrow'))
- new_first_bias_in: float32 [3072], P(('wide', 'narrow'))
- new_first_bias_out: float32 [768], P(('wide', 'narrow'))
- new_second_norm_one: float32 [2, 768], P(None, ('wide', 'narrow'))
- new_second_norm_two: float32 [2, 768], P(None, ('wide', 'narrow'))
- new_second_bias_in: float32 [3072], P(('wide', 'narrow'))
- new_second_bias_out: float32 [768], P(('wide', 'narrow'))
- new_norm_params: float32 [4, 768], P(None, ('wide', 'narrow'))
- new_bias_in: float32 [3072], P(('wide', 'narrow'))
- new_bias_out: float32 [768], P(('wide', 'narrow'))
The draws below stay inside these ranges and needn't reach their ends.
Inputs may be any that keep to these rules, and one draw needn't show every extreme that they name: `lengths`: in each aligned group of four consecutive molecules (0 to 3, 4 to 7 and so on) at least one molecule has 202 tokens.
All inputs are finite; a program needn't handle non-finite values.
Results may differ from the reference program's by a relative error of at most 0.014.
The reference program's roundings to bfloat16 on the way count: a program that leaves them out, or rounds other values in their place, can miss the bound.
Values may be sent and summed in bfloat16 or wider, within the bound.
No kernel may reach another device: no remote copies, remote signals or barrier semaphores. Data moves between devices by JAX's collectives and lax.ppermute only.
A program may use at most 192 MiB of HBM per device.

```python
import math
import jax
import jax.numpy as jnp
from jax import lax

D = 768
FF = 3072
HEADS = 12
HDIM = 64
FEAT = 32
MINLEN = 10
MAXLEN = 202
PADLEN = 208
SEQ_DEV = 4
BATCH = 128
TOKENS = 26624
NS_ITERS = 5
ADAM_STEP = 10
N_WIDE = 8


def draw_lengths(key, part):
    count_key, slot_key = jax.random.split(key)
    drawn_lengths = jax.random.randint(count_key, (BATCH,), MINLEN, MAXLEN + 1, dtype=jnp.int32)
    slot_index = jax.random.randint(slot_key, (BATCH // 4,), 0, 4, dtype=jnp.int32)
    within = jnp.arange(BATCH, dtype=jnp.int32) % 4
    chosen = jnp.repeat(slot_index, 4)
    return jnp.where(within == chosen, MAXLEN, drawn_lengths).astype(jnp.int32)


def draw_norm_params(key, part):
    noise_vals = jnp.clip(jax.random.normal(key, (4, D), jnp.float32), -3.0, 3.0)
    parity = jnp.arange(4, dtype=jnp.int32)[:, None] % 2
    return jnp.where(parity == 0, 1.0 + 0.15 * noise_vals, 0.3 * noise_vals)


def moment_matrix(key, shape, size_scale, row_low, row_high):
    entry_key, row_key, col_key = jax.random.split(key, 3)
    entries = jnp.clip(jax.random.normal(entry_key, shape, jnp.float32), -4.0, 4.0)
    row_scale = jnp.exp(jax.random.uniform(row_key, shape[:-1] + (1,), jnp.float32, row_low, row_high))
    col_count = shape[-1]
    rising = jnp.exp(math.log(3.0) * (jnp.arange(col_count, dtype=jnp.float32) / max(col_count - 1, 1) - 0.5))
    col_scale = jnp.exp(jax.random.uniform(col_key, (col_count,), jnp.float32, -0.58, 0.58)) * rising
    return entries * row_scale * col_scale * size_scale * math.sqrt(TOKENS)


def draw_mom_attn_in(key, part):
    kinds = jnp.array([1.0, 1.0, 1.4], jnp.float32)[:, None, None]
    return moment_matrix(key, (3, D, D), 1.0, -0.58, 0.58) * kinds


def draw_mom_attn_out(key, part):
    return moment_matrix(key, (D, D), 3.0, math.log(0.01), 0.0)


def draw_mom_ffn_in(key, part):
    return moment_matrix(key, (D, FF), 0.3, -0.58, 0.58)


def draw_mom_ffn_out(key, part):
    return moment_matrix(key, (FF, D), 0.6, -0.58, 0.58)


def first_vector(key, shape, size_scale):
    noise_vals = jnp.clip(jax.random.normal(key, shape, jnp.float32), -3.0, 3.0)
    return noise_vals * size_scale * math.sqrt(TOKENS)


def second_vector(key, shape, size_scale):
    factor = jnp.exp(jax.random.uniform(key, shape, jnp.float32, 0.0, math.log(4.0)))
    return factor * size_scale * size_scale * TOKENS


def draw_first_norms(key, part):
    kinds = jnp.array([2.4, 2.4, 0.6, 0.6], jnp.float32)[:, None]
    return first_vector(key, (4, D), 1.0) * kinds


def draw_first_bias_in(key, part):
    return first_vector(key, (FF,), 0.3)


def draw_first_bias_out(key, part):
    return first_vector(key, (D,), 1.0)


def draw_second_norms(key, part):
    kinds = jnp.array([2.4, 2.4, 0.6, 0.6], jnp.float32)[:, None]
    return second_vector(key, (4, D), 1.0) * kinds * kinds


def draw_second_bias_in(key, part):
    return second_vector(key, (FF,), 0.3)


def draw_second_bias_out(key, part):
    return second_vector(key, (D,), 1.0)


def steps_of(rng, dims, cuts, smallest, top_value):
    gain = 1.0
    for axis_at, parts in cuts:
        heights = jax.random.uniform(jax.random.fold_in(jax.random.fold_in(rng, 6), axis_at), (parts,), jnp.float32, smallest / len(cuts), top_value / len(cuts))
        gain = gain * jnp.repeat(jnp.exp(heights), dims[axis_at] // parts).reshape((-1,) + (1,) * (len(dims) - 1 - axis_at))
    return gain


def gaussian(key, dims, spread, limit, cuts=(), held_as=jnp.bfloat16):
    drawn = spread * jax.random.normal(key, dims, jnp.float32)
    if cuts:
        drawn = drawn * steps_of(key, dims, cuts, -0.22, 0.18)
    return jnp.clip(drawn, -limit, limit).astype(held_as)


def setup_inputs(seed: int = 0) -> dict:
    key_list = jax.random.split(jax.random.key(seed), 22)
    return {
        "block_in": gaussian(key_list[0], (BATCH, PADLEN, D), 1.0, 6.0, ((0, 32),)),
        "out_grad": gaussian(key_list[1], (BATCH, PADLEN, D), 1.0, 6.0, ((0, 32),)),
        "lengths": draw_lengths(jax.random.fold_in(key_list[21], 71), 0),
        "feature_proj": gaussian(key_list[3], (HEADS, FEAT, HDIM), 1.0, 5.0, (), jnp.float32),
        "attn_in": gaussian(key_list[4], (3, D, D), D ** -0.5, 0.21875, ((1, 8),), jnp.float32),
        "attn_out": gaussian(key_list[5], (D, D), (D // 64) ** -0.5, 1.75, ((0, 8),), jnp.float32),
        "ffn_in": gaussian(key_list[6], (D, FF), D ** -0.5, 0.21875, ((0, 8),), jnp.float32),
        "ffn_out": gaussian(key_list[7], (FF, D), FF ** -0.5, 0.109375, ((0, 8),), jnp.float32),
        "norm_params": draw_norm_params(jax.random.fold_in(key_list[21], 71), 0),
        "bias_in": gaussian(key_list[9], (FF,), 0.3, 4.0, ((0, 8),), jnp.float32),
        "bias_out": gaussian(key_list[10], (D,), 0.3, 4.0, ((0, 8),), jnp.float32),
        "mom_attn_in": draw_mom_attn_in(jax.random.fold_in(key_list[21], 71), 0),
        "mom_attn_out": draw_mom_attn_out(jax.random.fold_in(key_list[21], 71), 0),
        "mom_ffn_in": draw_mom_ffn_in(jax.random.fold_in(key_list[21], 71), 0),
        "mom_ffn_out": draw_mom_ffn_out(jax.random.fold_in(key_list[21], 71), 0),
        "first_norms": draw_first_norms(jax.random.fold_in(key_list[21], 71), 0),
        "first_bias_in": draw_first_bias_in(jax.random.fold_in(key_list[21], 71), 0),
        "first_bias_out": draw_first_bias_out(jax.random.fold_in(key_list[21], 71), 0),
        "second_norms": draw_second_norms(jax.random.fold_in(key_list[21], 71), 0),
        "second_bias_in": draw_second_bias_in(jax.random.fold_in(key_list[21], 71), 0),
        "second_bias_out": draw_second_bias_out(jax.random.fold_in(key_list[21], 71), 0),
    }


PRECISE = lax.Precision.HIGHEST
NORM_EPS = 1e-05
ORTHO_EPS = 1e-07
ADAM_EPS = 1e-08
LINEAR_COEF = 3.4445
CUBIC_COEF = -4.775
QUINTIC_COEF = 2.0315
MOMENT_DECAY = 0.5
FIRST_DECAY = 0.5
SECOND_DECAY = 0.5
MUON_SCALE = 0.6
WEIGHT_DECAY = 0.01
VECTOR_RATE = 0.4

@jax.custom_vjp
def low(v):
    return lax.optimization_barrier(v.astype(jnp.bfloat16)).astype(jnp.float32)

@jax.custom_vjp
def low_back(v):
    return v

def low_keep(v):
    return (low(v), None)

def low_pass(kept, grad):
    return (grad,)

def back_keep(v):
    return (v, None)

def back_low(kept, grad):
    return (low(grad),)
low.defvjp(low_keep, low_pass)
low_back.defvjp(back_keep, back_low)

def product(left_mat, right_mat):
    return jnp.dot(left_mat, right_mat, precision=PRECISE, preferred_element_type=jnp.float32)

def layer_norm_apply(row_vals, gain_vals, shift_vals):
    centered = row_vals - lax.optimization_barrier(jnp.mean(row_vals, axis=-1, keepdims=True))
    inverse = lax.rsqrt(lax.optimization_barrier(jnp.mean(centered * centered, axis=-1, keepdims=True)) + NORM_EPS)
    return centered * inverse * gain_vals + shift_vals

def rotary_tables(length, head_width):
    half_width = head_width // 2
    frequency = jnp.exp(jnp.arange(half_width, dtype=jnp.float32) * (-2.0 * math.log(10000.0) / head_width))
    angles = jnp.arange(length, dtype=jnp.float32)[:, None] * frequency[None, :]
    return (jnp.cos(angles), jnp.sin(angles))

def rotate_heads(tensor, cosine_table, sine_table):
    half_width = tensor.shape[-1] // 2
    leading = tensor[..., :half_width]
    trailing = tensor[..., half_width:]
    cosine_wide = cosine_table[None, :, None, :]
    sine_wide = sine_table[None, :, None, :]
    return jnp.concatenate([leading * cosine_wide - trailing * sine_wide, trailing * cosine_wide + leading * sine_wide], axis=-1)

def feature_map(rotated, feature_proj):
    unit_heads = rotated * rotated.shape[-1] ** (-0.25)
    projected = jnp.einsum('slhe,hfe->slhf', unit_heads, feature_proj, precision=PRECISE)
    squared = 0.5 * lax.optimization_barrier(jnp.sum(unit_heads * unit_heads, axis=-1, keepdims=True))
    return jnp.exp(projected - squared) * feature_proj.shape[1] ** (-0.5)

def layer_forward(weights, group_rows, live_mask, cosine_table, sine_table, feature_proj):
    w_qkv, w_out, w_in, w_back, norm_vals, bias_inner, bias_final = weights
    seq_count, length, model_width = group_rows.shape
    head_shape = (seq_count, length, HEADS, HDIM)
    flat_in = group_rows.reshape(seq_count * length, model_width)
    hidden_one = low(layer_norm_apply(flat_in, norm_vals[0], norm_vals[1]))
    queries = low_back(product(hidden_one, w_qkv[0]))
    key_heads = low_back(product(hidden_one, w_qkv[1]))
    values = low(low_back(product(hidden_one, w_qkv[2]))).reshape(head_shape)
    query_feats = low(feature_map(rotate_heads(queries.reshape(head_shape), cosine_table, sine_table), feature_proj))
    key_feats = low(feature_map(rotate_heads(key_heads.reshape(head_shape), cosine_table, sine_table), feature_proj))
    key_feats = key_feats * live_mask[:, :, None, None]
    kv_state = low(jnp.einsum('slhf,slhe->shfe', key_feats, values, precision=PRECISE))
    key_total = lax.optimization_barrier(jnp.sum(key_feats, axis=1))
    numerator = jnp.einsum('slhf,shfe->slhe', query_feats, kv_state, precision=PRECISE)
    denominator = jnp.einsum('slhf,shf->slh', query_feats, key_total, precision=PRECISE)
    mixed_low = low((numerator / denominator[..., None]).reshape(seq_count * length, model_width))
    middle = flat_in + low_back(product(mixed_low, w_out))
    hidden_two = low(layer_norm_apply(middle, norm_vals[2], norm_vals[3]))
    inner_pre = low_back(product(hidden_two, w_in) + bias_inner)
    activated = low(jax.nn.gelu(inner_pre, approximate=False))
    result = middle + low_back(product(activated, w_back) + bias_final)
    return result.reshape(seq_count, length, model_width)

def newton_schulz(moment):
    iterate = moment / (jnp.sqrt(jnp.sum(moment * moment)) + ORTHO_EPS)
    for sweep_index in range(NS_ITERS):
        gram_mat = product(iterate, iterate.T)
        poly_mat = CUBIC_COEF * gram_mat + QUINTIC_COEF * product(gram_mat, gram_mat)
        iterate = LINEAR_COEF * iterate + product(poly_mat, iterate)
    return iterate

def muon_update(weight, moment, gradient, step_rate):
    row_count, col_count = weight.shape
    moment_new = MOMENT_DECAY * moment + gradient
    blocks = moment_new.reshape(N_WIDE, row_count // N_WIDE, col_count)
    ortho = jax.vmap(newton_schulz)(blocks).reshape(row_count, col_count)
    return (moment_new, weight * (1.0 - step_rate * WEIGHT_DECAY) - step_rate * ortho)

def adam_update(param, earlier_first, earlier_second, gradient):
    first_new = FIRST_DECAY * earlier_first + (1.0 - FIRST_DECAY) * gradient
    second_new = SECOND_DECAY * earlier_second + (1.0 - SECOND_DECAY) * gradient * gradient
    first_fix = 1.0 - FIRST_DECAY ** ADAM_STEP
    second_fix = 1.0 - SECOND_DECAY ** ADAM_STEP
    direction = first_new / first_fix / (jnp.sqrt(second_new / second_fix) + ADAM_EPS)
    return (first_new, second_new, param - VECTOR_RATE * (direction + WEIGHT_DECAY * param))

def reference(block_in, out_grad, lengths, feature_proj, attn_in, attn_out, ffn_in, ffn_out, norm_params, bias_in, bias_out, mom_attn_in, mom_attn_out, mom_ffn_in, mom_ffn_out, first_norms, first_bias_in, first_bias_out, second_norms, second_bias_in, second_bias_out):
    groups = BATCH // SEQ_DEV
    positions = jnp.arange(PADLEN, dtype=jnp.int32)
    live_mask = (positions[None, :] < lengths[:, None]).astype(jnp.float32).reshape(groups, SEQ_DEV, PADLEN)
    cosine_table, sine_table = rotary_tables(PADLEN, HDIM)
    inputs = block_in.astype(jnp.float32).reshape(groups, SEQ_DEV, PADLEN, D)
    params = (attn_in, attn_out, ffn_in, ffn_out, norm_params, bias_in, bias_out)

    def whole(weights, group_inputs):
        lowered = jax.tree.map(low, weights)

        def one_group(group_pair):
            return layer_forward(lowered, group_pair[0], group_pair[1], cosine_table, sine_table, feature_proj)
        return lax.map(jax.checkpoint(one_group), (group_inputs, live_mask))
    result, pull = jax.vjp(whole, params, inputs)
    gradients, grad_rows = pull(out_grad.astype(jnp.float32).reshape(groups, SEQ_DEV, PADLEN, D))
    grad_qkv, grad_out_w, grad_in_w, grad_back_w, grad_norm_vals, grad_bias_inner, grad_bias_final = gradients
    moments_qkv = []
    weights_qkv = []
    for matrix_index in range(3):
        moment_new, weight_new = muon_update(attn_in[matrix_index], mom_attn_in[matrix_index], grad_qkv[matrix_index], MUON_SCALE)
        moments_qkv.append(moment_new)
        weights_qkv.append(weight_new)
    mom_out_new, weight_out_new = muon_update(attn_out, mom_attn_out, grad_out_w, MUON_SCALE * math.sqrt(D / (D // 64)))
    mom_in_new, weight_in_new = muon_update(ffn_in, mom_ffn_in, grad_in_w, MUON_SCALE * math.sqrt(FF / D))
    mom_back_new, weight_back_new = muon_update(ffn_out, mom_ffn_out, grad_back_w, MUON_SCALE * math.sqrt(D / FF))
    norm_first, norm_second, norm_new = adam_update(norm_params, first_norms, second_norms, grad_norm_vals)
    inner_first, inner_second, inner_new = adam_update(bias_in, first_bias_in, second_bias_in, grad_bias_inner)
    final_first, final_second, final_new = adam_update(bias_out, first_bias_out, second_bias_out, grad_bias_final)
    return (result.reshape(BATCH, PADLEN, D), grad_rows.reshape(BATCH, PADLEN, D), grad_qkv, grad_out_w, grad_in_w, grad_back_w, grad_norm_vals, grad_bias_inner, grad_bias_final, jnp.stack(moments_qkv), mom_out_new, mom_in_new, mom_back_new, jnp.stack(weights_qkv), weight_out_new, weight_in_new, weight_back_new, norm_first, inner_first, final_first, norm_second[:2], norm_second[2:], inner_second, final_second, norm_new, inner_new, final_new)
```

```python
from functools import partial
import math

import jax
import jax.numpy as jnp
from jax import lax
from jax.sharding import PartitionSpec as P

D = 768
FF = 3072
HEADS = 12
HDIM = 64
NS_ITERS = 5
ADAM_STEP = 10


PRECISE = lax.Precision.HIGHEST
NORM_EPS = 1e-05
ORTHO_EPS = 1e-07
ADAM_EPS = 1e-08
LINEAR_COEF = 3.4445
CUBIC_COEF = -4.775
QUINTIC_COEF = 2.0315
MOMENT_DECAY = 0.5
FIRST_DECAY = 0.5
SECOND_DECAY = 0.5
MUON_SCALE = 0.6
WEIGHT_DECAY = 0.01
VECTOR_RATE = 0.4


def layer_norm_apply(row_vals, gain_vals, shift_vals):
    centered = row_vals - jnp.mean(row_vals, axis=-1, keepdims=True)
    inverse = lax.rsqrt(jnp.mean(centered * centered, axis=-1, keepdims=True) + NORM_EPS)
    return centered * inverse * gain_vals + shift_vals


def rotary_tables(length, head_width):
    half_width = head_width // 2
    frequency = jnp.exp(
        jnp.arange(half_width, dtype=jnp.float32) * (-2.0 * math.log(10000.0) / head_width)
    )
    angles = jnp.arange(length, dtype=jnp.float32)[:, None] * frequency[None, :]
    return (jnp.cos(angles), jnp.sin(angles))


def rotate_heads(tensor, cosine_table, sine_table):
    half_width = tensor.shape[-1] // 2
    leading = tensor[..., :half_width]
    trailing = tensor[..., half_width:]
    cosine_wide = cosine_table[None, :, None, :]
    sine_wide = sine_table[None, :, None, :]
    return jnp.concatenate(
        [
            leading * cosine_wide - trailing * sine_wide,
            trailing * cosine_wide + leading * sine_wide,
        ],
        axis=-1,
    )


def feature_map(rotated, feature_proj):
    unit_heads = rotated * rotated.shape[-1] ** (-0.25)
    projected = jnp.einsum("slhe,hfe->slhf", unit_heads, feature_proj, precision=PRECISE)
    squared = 0.5 * jnp.sum(unit_heads * unit_heads, axis=-1, keepdims=True)
    return jnp.exp(projected - squared) * feature_proj.shape[1] ** (-0.5)


def rotate_features(head_vals, cosine_table, sine_table, feature_proj):
    return feature_map(rotate_heads(head_vals, cosine_table, sine_table), feature_proj)


def forward(params, flat_in, live_mask, cosine_table, sine_table, feature_proj):
    w_qkv, w_out, w_in, w_back, norm_low, bias_inner_low, bias_final_low = params
    seq_count, length = live_mask.shape
    head_shape = (seq_count, length, HEADS, HDIM)
    norm_vals = norm_low.astype(jnp.float32)
    hidden_one = layer_norm_apply(flat_in, norm_vals[0], norm_vals[1]).astype(jnp.bfloat16)
    projected = jnp.einsum("td,jde->jte", hidden_one, w_qkv, preferred_element_type=jnp.float32)
    query_feats = rotate_features(
        projected[0].reshape(head_shape), cosine_table, sine_table, feature_proj
    )
    key_feats = rotate_features(
        projected[1].reshape(head_shape), cosine_table, sine_table, feature_proj
    )
    query_low = query_feats.astype(jnp.bfloat16)
    key_low = key_feats.astype(jnp.bfloat16) * live_mask[:, :, None, None].astype(jnp.bfloat16)
    value_low = projected[2].astype(jnp.bfloat16).reshape(head_shape)
    kv_state = jnp.einsum("slhf,slhe->shfe", key_low, value_low, preferred_element_type=jnp.float32)
    state_low = kv_state.astype(jnp.bfloat16)
    key_total = jnp.sum(key_low.astype(jnp.float32), axis=1)
    numerator = jnp.einsum(
        "slhf,shfe->slhe", query_low, state_low, preferred_element_type=jnp.float32
    )
    denominator = jnp.einsum(
        "slhf,shf->slh", query_low.astype(jnp.float32), key_total, precision=PRECISE
    )
    attended = numerator / denominator[..., None]
    mixed_low = attended.reshape(seq_count * length, D).astype(jnp.bfloat16)
    middle = flat_in + jnp.dot(mixed_low, w_out, preferred_element_type=jnp.float32)
    hidden_two = layer_norm_apply(middle, norm_vals[2], norm_vals[3]).astype(jnp.bfloat16)
    inner_pre = jnp.dot(
        hidden_two, w_in, preferred_element_type=jnp.float32
    ) + bias_inner_low.astype(jnp.float32)
    act_low = jax.nn.gelu(inner_pre, approximate=False).astype(jnp.bfloat16)
    result = middle + (
        jnp.dot(act_low, w_back, preferred_element_type=jnp.float32)
        + bias_final_low.astype(jnp.float32)
    )
    kept_values = (
        hidden_one,
        projected,
        query_low,
        key_low,
        value_low,
        state_low,
        key_total,
        denominator,
        attended,
        mixed_low,
        middle,
        hidden_two,
        inner_pre,
        act_low,
    )
    return (result, kept_values)


def backward(
    params, kept_values, flat_in, grad_final, live_mask, cosine_table, sine_table, feature_proj
):
    w_qkv, w_out, w_in, w_back, norm_low, bias_inner_low, bias_final_low = params
    (
        hidden_one,
        projected,
        query_low,
        key_low,
        value_low,
        state_low,
        key_total,
        denominator,
        attended,
        mixed_low,
        middle,
        hidden_two,
        inner_pre,
        act_low,
    ) = kept_values
    seq_count, length = live_mask.shape
    head_shape = (seq_count, length, HEADS, HDIM)
    norm_vals = norm_low.astype(jnp.float32)
    grad_bias_final = jnp.sum(grad_final.astype(jnp.float32), axis=0)
    grad_w_back = jnp.einsum("tf,td->fd", act_low, grad_final, preferred_element_type=jnp.float32)
    grad_act = jnp.einsum("td,fd->tf", grad_final, w_back, preferred_element_type=jnp.float32)
    unused_gelu, gelu_pull = jax.vjp(partial(jax.nn.gelu, approximate=False), inner_pre)
    grad_inner = gelu_pull(grad_act)[0].astype(jnp.bfloat16)
    grad_bias_inner = jnp.sum(grad_inner.astype(jnp.float32), axis=0)
    grad_w_in = jnp.einsum("td,tf->df", hidden_two, grad_inner, preferred_element_type=jnp.float32)
    grad_hidden_two = jnp.einsum("tf,df->td", grad_inner, w_in, preferred_element_type=jnp.float32)
    unused_two, norm_two_pull = jax.vjp(layer_norm_apply, middle, norm_vals[2], norm_vals[3])
    grad_mid_part, grad_gain_two, grad_shift_two = norm_two_pull(grad_hidden_two)
    grad_middle = grad_final.astype(jnp.float32) + grad_mid_part
    grad_branch = grad_middle.astype(jnp.bfloat16)
    grad_w_out = jnp.einsum("td,te->de", mixed_low, grad_branch, preferred_element_type=jnp.float32)
    grad_attended = jnp.einsum(
        "te,de->td", grad_branch, w_out, preferred_element_type=jnp.float32
    ).reshape(attended.shape)
    grad_numer = grad_attended / denominator[..., None]
    grad_denom = -jnp.sum(grad_attended * attended, axis=-1) / denominator
    query_vals = query_low.astype(jnp.float32)
    state_vals = state_low.astype(jnp.float32)
    grad_qfeat = (
        jnp.einsum("slhe,shfe->slhf", grad_numer, state_vals, precision=PRECISE)
        + grad_denom[..., None] * key_total[:, None]
    )
    grad_state = jnp.einsum("slhf,slhe->shfe", query_vals, grad_numer, precision=PRECISE)
    grad_total = jnp.einsum("slhf,slh->shf", query_vals, grad_denom, precision=PRECISE)
    grad_kfeat = (
        jnp.einsum("shfe,slhe->slhf", grad_state, value_low.astype(jnp.float32), precision=PRECISE)
        + grad_total[:, None]
    ) * live_mask[:, :, None, None]
    grad_values = jnp.einsum(
        "slhf,shfe->slhe", key_low.astype(jnp.float32), grad_state, precision=PRECISE
    )
    feature_fn = partial(
        rotate_features, cosine_table=cosine_table, sine_table=sine_table, feature_proj=feature_proj
    )
    unused_query, query_pull = jax.vjp(feature_fn, projected[0].reshape(head_shape))
    unused_key, key_pull = jax.vjp(feature_fn, projected[1].reshape(head_shape))
    grad_queries = query_pull(grad_qfeat)[0]
    grad_keys = key_pull(grad_kfeat)[0]
    row_total = seq_count * length
    grad_projected = jnp.stack(
        [
            grad_queries.reshape(row_total, D),
            grad_keys.reshape(row_total, D),
            grad_values.reshape(row_total, D),
        ]
    ).astype(jnp.bfloat16)
    grad_w_qkv = jnp.einsum(
        "td,jte->jde", hidden_one, grad_projected, preferred_element_type=jnp.float32
    )
    grad_hidden_one = jnp.einsum(
        "jte,jde->td", grad_projected, w_qkv, preferred_element_type=jnp.float32
    )
    unused_one, norm_one_pull = jax.vjp(layer_norm_apply, flat_in, norm_vals[0], norm_vals[1])
    grad_in_part, grad_gain_one, grad_shift_one = norm_one_pull(grad_hidden_one)
    grad_input = grad_middle + grad_in_part
    grad_norm_vals = jnp.stack([grad_gain_one, grad_shift_one, grad_gain_two, grad_shift_two])
    return (
        grad_input,
        (
            grad_w_qkv,
            grad_w_out,
            grad_w_in,
            grad_w_back,
            grad_norm_vals,
            grad_bias_inner,
            grad_bias_final,
        ),
    )


def xor_pairs(size, mask):
    return [(index, index ^ mask) for index in range(size)]


def swap(value, axis_name, mask):
    return lax.ppermute(value, axis_name, xor_pairs(lax.axis_size(axis_name), mask))


def gather_rows(piece):
    wide_size = lax.axis_size("wide")
    narrow_size = lax.axis_size("narrow")
    block = jnp.stack([piece] + [swap(piece, "wide", 2 * m) for m in range(1, wide_size // 2)])
    block = jnp.stack([block, swap(block, "wide", 1)])
    block = jnp.stack([block] + [swap(block, "narrow", 2 * m) for m in range(1, narrow_size // 2)])
    block = jnp.stack([block, swap(block, "narrow", 1)])
    flat = block.reshape((wide_size * narrow_size,) + piece.shape)
    my_wide = lax.axis_index("wide")
    my_narrow = lax.axis_index("narrow")
    ordered = []
    for wide_index in range(wide_size):
        for narrow_index in range(narrow_size):
            wide_mask = wide_index ^ my_wide
            narrow_mask = narrow_index ^ my_narrow
            place = (narrow_mask & 1) * (narrow_size // 2) + (narrow_mask >> 1)
            place = (place * 2 + (wide_mask & 1)) * (wide_size // 2) + (wide_mask >> 1)
            ordered.append(lax.dynamic_index_in_dim(flat, place, 0, keepdims=False))
    return jnp.concatenate(ordered, axis=0)


def pick(value, index, axis):
    return lax.dynamic_index_in_dim(value, index, axis, keepdims=False)


def fold(value, axis_name, masks, shift):
    place = lax.axis_index(axis_name)
    here = pick(value, (place >> shift) & (value.shape[0] - 1), 0).astype(jnp.float32)
    for mask in masks:
        other = ((place ^ mask) >> shift) & (value.shape[0] - 1)
        here = here + swap(pick(value, other, 0), axis_name, mask).astype(jnp.float32)
    return here


def scatter_blocks(parts, wire):
    wide_size = lax.axis_size("wide")
    narrow_size = lax.axis_size("narrow")
    rest = parts.shape[2:]
    value = parts.astype(wire).reshape((narrow_size // 2, 2, wide_size) + rest).swapaxes(0, 1)
    value = fold(value, "narrow", [1], 0).astype(wire)
    value = fold(value, "narrow", [2 * m for m in range(1, narrow_size // 2)], 1).astype(wire)
    value = value.reshape((wide_size // 2, 2) + rest).swapaxes(0, 1)
    value = fold(value, "wide", [1], 0).astype(wire)
    return fold(value, "wide", [2 * m for m in range(1, wide_size // 2)], 1)


def narrow_sum(value):
    mask = 1
    while mask < lax.axis_size("narrow"):
        value = value + swap(value, "narrow", mask)
        mask *= 2
    return value


def gram_of(matrices):
    return jnp.einsum("brc,bsc->brs", matrices, matrices, precision=PRECISE)


def bmm(left, right):
    return jnp.einsum("brs,bst->brt", left, right, precision=PRECISE)


def ortho_factor(gram_mat):
    count = gram_mat.shape[-1]
    identity = jnp.eye(count, dtype=jnp.float32)
    square_sum = jnp.trace(gram_mat, axis1=-2, axis2=-1)
    scale = (1.0 / (jnp.sqrt(square_sum) + ORTHO_EPS))[:, None, None]
    gram_mat = gram_mat * scale * scale
    factor = None
    for sweep_index in range(NS_ITERS):
        poly_mat = (
            LINEAR_COEF * identity + CUBIC_COEF * gram_mat + QUINTIC_COEF * bmm(gram_mat, gram_mat)
        )
        factor = poly_mat if factor is None else bmm(poly_mat, factor)
        if sweep_index < NS_ITERS - 1:
            gram_mat = bmm(poly_mat, bmm(gram_mat, poly_mat))
    return factor * scale


def adam_update(param, earlier_first, earlier_second, gradient):
    first_new = FIRST_DECAY * earlier_first + (1.0 - FIRST_DECAY) * gradient
    second_new = SECOND_DECAY * earlier_second + (1.0 - SECOND_DECAY) * gradient * gradient
    first_fix = 1.0 - FIRST_DECAY**ADAM_STEP
    second_fix = 1.0 - SECOND_DECAY**ADAM_STEP
    direction = first_new / first_fix / (jnp.sqrt(second_new / second_fix) + ADAM_EPS)
    return (first_new, second_new, param - VECTOR_RATE * (direction + WEIGHT_DECAY * param))


def per_device(
    block_in,
    out_grad,
    lengths,
    feature_proj,
    attn_in,
    attn_out,
    ffn_in,
    ffn_out,
    norm_params,
    bias_in,
    bias_out,
    mom_attn_in,
    mom_attn_out,
    mom_ffn_in,
    mom_ffn_out,
    first_norms,
    first_bias_in,
    first_bias_out,
    second_norms,
    second_bias_in,
    second_bias_out,
):
    seq_count, length, model_width = block_in.shape
    row_total = seq_count * length
    positions = jnp.arange(length, dtype=jnp.int32)
    live_mask = (positions[None, :] < lengths[:, None]).astype(jnp.float32)
    cosine_table, sine_table = rotary_tables(length, HDIM)
    flat_in = block_in.reshape(row_total, model_width).astype(jnp.float32)
    low_qkv = attn_in.astype(jnp.bfloat16)
    low_out = attn_out.astype(jnp.bfloat16)
    low_in = ffn_in.astype(jnp.bfloat16)
    low_back_w = ffn_out.astype(jnp.bfloat16)
    low_norms = norm_params.astype(jnp.bfloat16)
    low_bias_in = bias_in.astype(jnp.bfloat16)
    low_bias_out = bias_out.astype(jnp.bfloat16)
    narrow_size = lax.axis_size("narrow")
    wide_size = lax.axis_size("wide")
    column = lax.axis_index("narrow")

    def quarter(rows):
        part = rows.shape[0] // narrow_size
        return lax.dynamic_slice_in_dim(rows, column * part, part, axis=0)

    qkv_rows = low_qkv.transpose(1, 0, 2).reshape(-1, 3 * D)
    params = (
        gather_rows(quarter(qkv_rows)).reshape(D, 3, D).transpose(1, 0, 2),
        gather_rows(quarter(low_out)),
        gather_rows(quarter(low_in)),
        gather_rows(quarter(low_back_w)),
        lax.all_gather(low_norms, "wide", axis=1, tiled=True),
        lax.all_gather(low_bias_in, "wide", axis=0, tiled=True),
        lax.all_gather(low_bias_out, "wide", axis=0, tiled=True),
    )
    result, kept_values = forward(
        params, flat_in, live_mask, cosine_table, sine_table, feature_proj
    )
    grad_input, gradients = backward(
        params,
        kept_values,
        flat_in,
        out_grad.reshape(row_total, model_width),
        live_mask,
        cosine_table,
        sine_table,
        feature_proj,
    )
    def blocks_of(gradient):
        rows, columns = gradient.shape
        shape = (wide_size, rows // wide_size, narrow_size, columns // narrow_size)
        return gradient.astype(jnp.bfloat16).reshape(shape).transpose(2, 0, 1, 3)

    grad_back_w = scatter_blocks(blocks_of(gradients[3]), jnp.bfloat16)
    grad_in_w = scatter_blocks(blocks_of(gradients[2]), jnp.bfloat16)
    grad_out_w = scatter_blocks(blocks_of(gradients[1]), jnp.bfloat16)
    grad_qkv = scatter_blocks(
        jnp.stack([blocks_of(gradients[0][j]) for j in range(3)], axis=2), jnp.bfloat16
    )
    norm_sums, inner_sums, final_sums = lax.psum(gradients[4:], ("wide", "narrow"))
    place = lax.axis_index("wide") * narrow_size + column

    def own_part(vector):
        width = vector.shape[-1] // (wide_size * narrow_size)
        return lax.dynamic_slice_in_dim(vector, place * width, width, axis=vector.ndim - 1)

    grad_norm_vals = own_part(norm_sums)
    grad_bias_inner = own_part(inner_sums)
    grad_bias_final = own_part(final_sums)

    def own_columns(weight):
        block_width = weight.shape[-1] // narrow_size
        return lax.dynamic_slice_in_dim(
            weight, column * block_width, block_width, axis=weight.ndim - 1
        )

    mom_qkv_new = MOMENT_DECAY * mom_attn_in + grad_qkv
    mom_out_new = MOMENT_DECAY * mom_attn_out + grad_out_w
    mom_in_new = MOMENT_DECAY * mom_ffn_in + grad_in_w
    mom_back_new = MOMENT_DECAY * mom_ffn_out + grad_back_w
    stacks = (mom_qkv_new, mom_out_new[None], mom_in_new[None], mom_back_new[None])
    small = jnp.concatenate([gram_of(stacks[0]), gram_of(stacks[1]), gram_of(stacks[2])], axis=0)
    large = gram_of(stacks[3])
    small_factor = ortho_factor(narrow_sum(small))
    large_factor = ortho_factor(narrow_sum(large))
    iterates = (
        bmm(small_factor[:3], stacks[0]),
        bmm(small_factor[3:4], stacks[1]),
        bmm(small_factor[4:5], stacks[2]),
        bmm(large_factor, stacks[3]),
    )
    rate_qkv = MUON_SCALE
    rate_out = MUON_SCALE * math.sqrt(D / (D // 64))
    rate_in = MUON_SCALE * math.sqrt(FF / D)
    rate_back = MUON_SCALE * math.sqrt(D / FF)
    new_qkv = own_columns(attn_in) * (1.0 - rate_qkv * WEIGHT_DECAY) - rate_qkv * iterates[0]
    new_out = own_columns(attn_out) * (1.0 - rate_out * WEIGHT_DECAY) - rate_out * iterates[1][0]
    new_in = own_columns(ffn_in) * (1.0 - rate_in * WEIGHT_DECAY) - rate_in * iterates[2][0]
    new_back = own_columns(ffn_out) * (1.0 - rate_back * WEIGHT_DECAY) - rate_back * iterates[3][0]
    norm_first, norm_second, norm_new = adam_update(
        own_columns(norm_params), first_norms, second_norms, grad_norm_vals
    )
    inner_first, inner_second, inner_new = adam_update(
        own_columns(bias_in), first_bias_in, second_bias_in, grad_bias_inner
    )
    final_first, final_second, final_new = adam_update(
        own_columns(bias_out), first_bias_out, second_bias_out, grad_bias_final
    )
    return (
        result.reshape(seq_count, length, model_width),
        grad_input.reshape(seq_count, length, model_width),
        grad_qkv,
        grad_out_w,
        grad_in_w,
        grad_back_w,
        grad_norm_vals,
        grad_bias_inner,
        grad_bias_final,
        mom_qkv_new,
        mom_out_new,
        mom_in_new,
        mom_back_new,
        new_qkv,
        new_out,
        new_in,
        new_back,
        norm_first,
        inner_first,
        final_first,
        norm_second[:2],
        norm_second[2:],
        inner_second,
        final_second,
        norm_new,
        inner_new,
        final_new,
    )


def solution(mesh):
    in_specs = (
        P(("wide", "narrow"), None, None),
        P(("wide", "narrow"), None, None),
        P(("wide", "narrow")),
        P(),
        P(None, "wide", None),
        P("wide", None),
        P("wide", None),
        P("wide", None),
        P(None, "wide"),
        P("wide"),
        P("wide"),
        P(None, "wide", "narrow"),
        P("wide", "narrow"),
        P("wide", "narrow"),
        P("wide", "narrow"),
        P(None, ("wide", "narrow")),
        P(("wide", "narrow")),
        P(("wide", "narrow")),
        P(None, ("wide", "narrow")),
        P(("wide", "narrow")),
        P(("wide", "narrow")),
    )
    out_specs = (
        P(("wide", "narrow"), None, None),
        P(("wide", "narrow"), None, None),
        P(None, "wide", "narrow"),
        P("wide", "narrow"),
        P("wide", "narrow"),
        P("wide", "narrow"),
        P(None, ("wide", "narrow")),
        P(("wide", "narrow")),
        P(("wide", "narrow")),
        P(None, "wide", "narrow"),
        P("wide", "narrow"),
        P("wide", "narrow"),
        P("wide", "narrow"),
        P(None, "wide", "narrow"),
        P("wide", "narrow"),
        P("wide", "narrow"),
        P("wide", "narrow"),
        P(None, ("wide", "narrow")),
        P(("wide", "narrow")),
        P(("wide", "narrow")),
        P(None, ("wide", "narrow")),
        P(None, ("wide", "narrow")),
        P(("wide", "narrow")),
        P(("wide", "narrow")),
        P(None, ("wide", "narrow")),
        P(("wide", "narrow")),
        P(("wide", "narrow")),
    )
    return jax.shard_map(
        per_device, mesh=mesh, in_specs=in_specs, out_specs=out_specs, check_vma=False
    )
```

```python
from functools import partial
import math

import jax
import jax.numpy as jnp
from jax import lax
from jax.experimental import pallas as pl
from jax.experimental.pallas import tpu as pltpu
from jax.sharding import PartitionSpec as P

D = 768
FF = 3072
HEADS = 12
HDIM = 64
FEAT = 32
NS_ITERS = 5
ADAM_STEP = 10


PRECISE = lax.Precision.HIGHEST
NORM_EPS = 1e-05
ORTHO_EPS = 1e-07
ADAM_EPS = 1e-08
LINEAR_COEF = 3.4445
CUBIC_COEF = -4.775
QUINTIC_COEF = 2.0315
MOMENT_DECAY = 0.5
FIRST_DECAY = 0.5
SECOND_DECAY = 0.5
MUON_SCALE = 0.6
WEIGHT_DECAY = 0.01
VECTOR_RATE = 0.4
GROUP = 4
GROUPS = HEADS // GROUP
GE = GROUP * HDIM
GF = GROUP * FEAT


def mm(left, right):
    return jnp.dot(left, right, preferred_element_type=jnp.float32)


def mm_nt(left, right):
    return lax.dot_general(left, right, (((1,), (1,)), ((), ())), preferred_element_type=jnp.float32)


def mm_tn(left, right):
    return lax.dot_general(left, right, (((0,), (0,)), ((), ())), preferred_element_type=jnp.float32)


def halves(value):
    high = value.astype(jnp.bfloat16)
    return high, (value - high.astype(jnp.float32)).astype(jnp.bfloat16)


def normalise(rows):
    centered = rows - jnp.mean(rows, axis=-1, keepdims=True)
    inverse = lax.rsqrt(jnp.mean(centered * centered, axis=-1, keepdims=True) + NORM_EPS)
    return centered * inverse, inverse


def norm_pull(normed, inverse, grad, gain):
    scaled = grad * gain
    mean_plain = jnp.mean(scaled, axis=-1, keepdims=True)
    mean_prod = jnp.mean(scaled * normed, axis=-1, keepdims=True)
    return inverse * (scaled - mean_plain - normed * mean_prod)


def partner_of(values):
    lane = lax.broadcasted_iota(jnp.int32, (values.shape[0], 128), 1)
    first = (lane & (HDIM - 1)) < HDIM // 2
    parts = []
    for at in range(0, values.shape[1], 128):
        block = values[:, at : at + 128]
        ahead = pltpu.roll(block, 128 - HDIM // 2, 1)
        behind = pltpu.roll(block, HDIM // 2, 1)
        parts.append(jnp.where(first, ahead, behind))
    return jnp.concatenate(parts, axis=1)


def head_mask(rows, columns, row_width, column_width):
    row = lax.broadcasted_iota(jnp.int32, (rows, columns), 0) // row_width
    column = lax.broadcasted_iota(jnp.int32, (rows, columns), 1) // column_width
    return row == column


def store_columns(ref, values):
    width = ref.shape[3]
    for n in range(ref.shape[0]):
        ref[n, 0] = values[:, width * n : width * (n + 1)].astype(ref.dtype)


def load_columns(ref):
    return jnp.concatenate([ref[n, 0] for n in range(ref.shape[0])], axis=1)


def attend_kernel(
    lengths_ref, x_ref, w_ref, vec_ref, proj_ref, cos_ref, sin_ref,
    middle_ref, h1_ref, h2_ref, wq_ref, wk_ref, pq_ref, pk_ref, v_ref, state_ref, total_ref, att_ref, rden_ref, mixed_ref,
):
    rows = x_ref.shape[1]
    x = x_ref[0].astype(jnp.float32)
    h1 = (normalise(x)[0] * vec_ref[0:1, :] + vec_ref[1:2, :]).astype(jnp.bfloat16)
    h1_ref[0] = h1
    live = (lax.broadcasted_iota(jnp.int32, (rows, 1), 0) < lengths_ref[pl.program_id(0)]).astype(jnp.float32)
    cosine = jnp.concatenate([cos_ref[...]] * (D // 128), axis=1)
    sine = jnp.concatenate([sin_ref[...]] * (D // 128), axis=1)
    values = mm(h1, w_ref[2]).astype(jnp.bfloat16)
    v_ref[0] = values
    feats = []
    for j, (w_out, p_out) in enumerate(((wq_ref, pq_ref), (wk_ref, pk_ref))):
        heads = mm(h1, w_ref[j])
        unit = (heads * cosine + partner_of(heads) * sine) * HDIM ** (-0.25)
        w_out[0] = unit
        high, low = halves(unit)
        sq_high, sq_low = halves(unit * unit)
        parts = []
        for g in range(GROUPS):
            cut = slice(GE * g, GE * (g + 1))
            left = jnp.concatenate([high[:, cut], low[:, cut], high[:, cut], sq_high[:, cut], sq_low[:, cut]], axis=1)
            parts.append(jnp.exp(mm(left, proj_ref[g])) * FEAT ** (-0.5))
        phi = jnp.concatenate(parts, axis=1)
        p_out[0] = phi
        feats.append(phi)
    query_low = feats[0].astype(jnp.bfloat16)
    key_vals = feats[1].astype(jnp.bfloat16).astype(jnp.float32) * live
    key_low = key_vals.astype(jnp.bfloat16)
    total_ref[0] = jnp.sum(key_vals, axis=0, keepdims=True)
    mask = head_mask(GF, GE, FEAT, HDIM)
    ones = jnp.ones((rows, GE), jnp.bfloat16)
    attended, inverse_den = [], []
    for g in range(GROUPS):
        cut = slice(GE * g, GE * (g + 1))
        fcut = slice(GF * g, GF * (g + 1))
        both = mm_tn(key_low[:, fcut], jnp.concatenate([values[:, cut], ones], axis=1))
        state = jnp.where(mask, both[:, :GE], 0.0).astype(jnp.bfloat16)
        state_ref[0, g] = state
        tot_high, tot_low = halves(jnp.where(mask, both[:, GE:], 0.0))
        query = query_low[:, fcut]
        numer = mm(query, state)
        denom = mm(jnp.concatenate([query, query], axis=1), jnp.concatenate([tot_high, tot_low], axis=0))
        inverse = 1.0 / denom
        attended.append(numer * inverse)
        inverse_den.append(inverse)
    attended = jnp.concatenate(attended, axis=1)
    att_ref[0] = attended
    rden_ref[0] = jnp.concatenate(inverse_den, axis=1)
    mixed = attended.astype(jnp.bfloat16)
    mixed_ref[0] = mixed
    middle = x + mm(mixed, w_ref[3])
    middle_ref[0] = middle
    h2_ref[0] = (normalise(middle)[0] * vec_ref[2:3, :] + vec_ref[3:4, :]).astype(jnp.bfloat16)


def attend_back_kernel(
    lengths_ref, og_ref, gh2_ref, ffn_ref, middle_ref, w_ref, vec_ref, projt_ref, cos_ref, sin_ref,
    wq_ref, wk_ref, pq_ref, pk_ref, v_ref, state_ref, total_ref, att_ref, rden_ref,
    out_ref, gm_ref, gb_ref, gq_ref, gk_ref, gv_ref, sums_ref,
):
    rows = og_ref.shape[1]
    og = og_ref[0].astype(jnp.float32)
    middle = middle_ref[0]
    out_ref[0] = middle + (ffn_ref[0] + vec_ref[4:5, :])
    grad_h2 = gh2_ref[0]
    normed, inverse = normalise(middle)
    grad_middle = og + norm_pull(normed, inverse, grad_h2, vec_ref[2:3, :])
    gm_ref[0] = grad_middle

    @pl.when(pl.program_id(0) == 0)
    def _():
        sums_ref[...] = jnp.zeros_like(sums_ref)

    sums_ref[0:1, :] += jnp.sum(grad_h2 * normed, axis=0, keepdims=True)
    sums_ref[1:2, :] += jnp.sum(grad_h2, axis=0, keepdims=True)
    sums_ref[2:3, :] += jnp.sum(og, axis=0, keepdims=True)
    branch = grad_middle.astype(jnp.bfloat16)
    store_columns(gb_ref, grad_middle)
    grad_numer = mm_nt(branch, w_ref[3]) * rden_ref[0]
    gn_high, gn_low = halves(grad_numer)
    pr_high, pr_low = halves(grad_numer * att_ref[0])
    live = (lax.broadcasted_iota(jnp.int32, (rows, 1), 0) < lengths_ref[pl.program_id(0)]).astype(jnp.float32)
    query_low = pq_ref[0].astype(jnp.bfloat16)
    key_low = (pk_ref[0].astype(jnp.bfloat16).astype(jnp.float32) * live).astype(jnp.bfloat16)
    mask = head_mask(GF, GE, FEAT, HDIM)
    spread = head_mask(GE, GF, HDIM, FEAT).astype(jnp.float32).astype(jnp.bfloat16)
    spread2 = jnp.concatenate([spread, spread], axis=0)
    gather = mask.astype(jnp.float32).astype(jnp.bfloat16)
    gather2 = jnp.concatenate([gather, gather], axis=0)
    grad_u = ([], [])
    grad_v = []
    for g in range(GROUPS):
        cut = slice(GE * g, GE * (g + 1))
        fcut = slice(GF * g, GF * (g + 1))
        query, key, values = query_low[:, fcut], key_low[:, fcut], v_ref[0, :, cut]
        state = state_ref[0, g]
        grad_denom = -mm(jnp.concatenate([pr_high[:, cut], pr_low[:, cut]], axis=1), spread2)
        two = jnp.concatenate([gn_high[:, cut], gn_low[:, cut]], axis=1)
        grad_qfeat = mm_nt(two, jnp.concatenate([state, state], axis=1)) + grad_denom * total_ref[0, :, fcut]
        pair = mm_tn(query, two)
        grad_state = jnp.where(mask, pair[:, :GE] + pair[:, GE:], 0.0)
        grad_total = jnp.sum(grad_denom * query.astype(jnp.float32), axis=0, keepdims=True)
        gs_high, gs_low = halves(grad_state)
        grad_kfeat = mm_nt(
            jnp.concatenate([values, values], axis=1), jnp.concatenate([gs_high, gs_low], axis=1)
        )
        grad_kfeat = (grad_kfeat + grad_total) * live
        grad_v.append(mm(jnp.concatenate([key, key], axis=1), jnp.concatenate([gs_high, gs_low], axis=0)))
        for j, (grad_feat, p_in, w_in) in enumerate(((grad_qfeat, pq_ref, wq_ref), (grad_kfeat, pk_ref, wk_ref))):
            t_high, t_low = halves(grad_feat * p_in[0, :, fcut])
            pulled = mm(jnp.concatenate([t_high, t_low, t_high], axis=1), projt_ref[g])
            weight = mm(jnp.concatenate([t_high, t_low], axis=1), gather2)
            grad_u[j].append((pulled - weight * w_in[0, :, cut]) * HDIM ** (-0.25))
    cosine = jnp.concatenate([cos_ref[...]] * (D // 128), axis=1)
    sine = jnp.concatenate([sin_ref[...]] * (D // 128), axis=1)
    for grads, ref in zip(grad_u, (gq_ref, gk_ref)):
        turned = jnp.concatenate(grads, axis=1)
        store_columns(ref, turned * cosine - partner_of(turned) * sine)
    store_columns(gv_ref, jnp.concatenate(grad_v, axis=1))


def input_back_kernel(x_ref, gm_ref, gq_ref, gk_ref, gv_ref, w_ref, vec_ref, out_ref, sums_ref):
    grad_h1 = sum(mm_nt(load_columns(ref), w_ref[j]) for j, ref in enumerate((gq_ref, gk_ref, gv_ref)))
    normed, inverse = normalise(x_ref[0].astype(jnp.float32))
    out_ref[0] = gm_ref[0] + norm_pull(normed, inverse, grad_h1, vec_ref[0:1, :])

    @pl.when(pl.program_id(0) == 0)
    def _():
        sums_ref[...] = jnp.zeros_like(sums_ref)

    sums_ref[0:1, :] += jnp.sum(grad_h1 * normed, axis=0, keepdims=True)
    sums_ref[1:2, :] += jnp.sum(grad_h1, axis=0, keepdims=True)


def attn_weight_kernel(h1_ref, mixed_ref, gq_ref, gk_ref, gv_ref, gb_ref, out_ref):
    wide, rows = out_ref.shape[1], out_ref.shape[2] // 2
    h1 = h1_ref[...]
    left = mm_tn(h1, jnp.concatenate([gq_ref[...], gk_ref[...]], axis=1)).astype(jnp.bfloat16)
    right = jnp.concatenate([mm_tn(h1, gv_ref[...]), mm_tn(mixed_ref[...], gb_ref[...])], axis=1).astype(jnp.bfloat16)
    for w in range(wide):
        out_ref[0, w, :rows, :] = left[rows * w : rows * (w + 1)]
        out_ref[0, w, rows:, :] = right[rows * w : rows * (w + 1)]


def ffn_kernel(has_past, blocks, h2_ref, og_ref, win_ref, wback_ref, bias_ref, *rest):
    if has_past:
        out_past_ref, gh2_past_ref, out_ref, gh2_ref, gw_ref, bsum_ref, act_ref, gi_ref = rest
    else:
        out_ref, gh2_ref, gw_ref, bsum_ref, act_ref, gi_ref = rest
    seqs, rows = out_ref.shape[0], out_ref.shape[1]
    step = pl.program_id(0)
    win, wback = win_ref[...], wback_ref[...]
    bias = bias_ref[...]

    def part(s, carry):
        span = pl.ds(pl.multiple_of(s * rows, rows), rows)
        inner = mm(h2_ref[s], win) + bias
        grad_act = mm_nt(og_ref[s], wback)
        cdf = 0.5 * (1.0 + lax.erf(inner * (2.0**-0.5)))
        pdf = jnp.exp(-0.5 * inner * inner) * (2.0 * math.pi) ** -0.5
        act = (inner * cdf).astype(jnp.bfloat16)
        grad_inner = (grad_act * (cdf + inner * pdf)).astype(jnp.bfloat16)
        act_ref[span, :] = act
        gi_ref[span, :] = grad_inner
        out_part = mm(act, wback)
        gh2_part = mm_nt(grad_inner, win)

        @pl.when(step == 0)
        def _():
            if has_past:
                out_ref[s] = out_past_ref[s] + out_part
                gh2_ref[s] = gh2_past_ref[s] + gh2_part
            else:
                out_ref[s] = out_part
                gh2_ref[s] = gh2_part

        @pl.when(step > 0)
        def _():
            out_ref[s] += out_part
            gh2_ref[s] += gh2_part

        return carry + jnp.sum(grad_inner.astype(jnp.float32), axis=0, keepdims=True)

    bsum_ref[...] = lax.fori_loop(0, seqs, part, jnp.zeros(bias.shape, jnp.float32))
    h2 = h2_ref[...].reshape(seqs * rows, D)
    og = og_ref[...].reshape(seqs * rows, D)
    grad_in = mm_tn(h2, gi_ref[...]).astype(jnp.bfloat16)
    grad_back = mm_tn(og, act_ref[...]).astype(jnp.bfloat16)
    if not blocks:
        gw_ref[0] = grad_in
        gw_ref[1] = grad_back
        return
    narrow, wide = gw_ref.shape[0], gw_ref.shape[1]
    in_rows, in_cols = D // wide, gw_ref.shape[3]
    width = grad_in.shape[1]
    for k in range(width // in_cols):
        for w in range(wide):
            gw_ref[step * (width // in_cols) + k, w, :in_rows, :] = grad_in[
                in_rows * w : in_rows * (w + 1), in_cols * k : in_cols * (k + 1)
            ]
    back_rows = D // narrow
    half = back_rows // 2
    for k in range(width // 128):
        for n in range(narrow):
            for h in range(2):
                gw_ref[n, step * (width // 128) + k, in_rows:, 128 * h : 128 * (h + 1)] = grad_back[
                    back_rows * n + half * h : back_rows * n + half * (h + 1), 128 * k : 128 * (k + 1)
                ]


def spec(shape, index):
    return pl.BlockSpec(shape, index)


LIMIT = 60 * 1024 * 1024


def estimate(flops, moved, transcendentals=0):
    return pl.CostEstimate(flops=int(flops), bytes_accessed=int(moved), transcendentals=int(transcendentals))


def whole(array):
    rank = array.ndim
    return pl.BlockSpec(array.shape, lambda *unused: (0,) * rank)


def by_seq(shape):
    rank = len(shape)
    return pl.BlockSpec((1,) + tuple(shape[1:]), lambda s, *unused: (s,) + (0,) * (rank - 1))


def by_seq_second(shape):
    rank = len(shape)
    return pl.BlockSpec((shape[0], 1) + tuple(shape[2:]), lambda s, *unused: (0, s) + (0,) * (rank - 2))


def attend(lengths, x, weights, vectors, proj, cosine, sine):
    seqs, rows, unused_width = x.shape
    bf, f4 = jnp.bfloat16, jnp.float32
    shapes = [
        ((seqs, rows, D), f4), ((seqs, rows, D), bf), ((seqs, rows, D), bf), ((seqs, rows, D), f4), ((seqs, rows, D), f4),
        ((seqs, rows, HEADS * FEAT), f4), ((seqs, rows, HEADS * FEAT), f4), ((seqs, rows, D), bf),
        ((seqs, GROUPS, GF, GE), bf), ((seqs, 1, HEADS * FEAT), f4), ((seqs, rows, D), f4), ((seqs, rows, D), f4),
        ((seqs, rows, D), bf),
    ]
    return pl.pallas_call(
        attend_kernel,
        grid_spec=pltpu.PrefetchScalarGridSpec(
            num_scalar_prefetch=1,
            grid=(seqs,),
            in_specs=[by_seq(x.shape)] + [whole(a) for a in (weights, vectors, proj, cosine, sine)],
            out_specs=[by_seq(shape) for shape, unused in shapes],
        ),
        out_shape=[jax.ShapeDtypeStruct(shape, dtype) for shape, dtype in shapes],
        compiler_params=pltpu.CompilerParams(vmem_limit_bytes=LIMIT),
        cost_estimate=estimate(seqs * rows * D * D * 12, 40e6),
        name="attend",
    )(lengths, x, weights, vectors, proj, cosine, sine)


def attend_back(lengths, og, grad_h2, ffn, middle, weights, vectors, projt, cosine, sine, kept, narrow_size):
    seqs, rows, unused_width = og.shape
    bf, f4 = jnp.bfloat16, jnp.float32
    blocked = (narrow_size, seqs, rows, D // narrow_size)
    outs = [((seqs, rows, D), f4, by_seq), ((seqs, rows, D), f4, by_seq)]
    outs += [(blocked, bf, by_seq_second)] + [((seqs, rows, D), bf, by_seq)] * 0
    outs += [(blocked, bf, by_seq_second)] * 3
    out_shapes = [jax.ShapeDtypeStruct(shape, dtype) for shape, dtype, unused in outs]
    out_specs = [make(shape) for shape, unused, make in outs]
    out_shapes.append(jax.ShapeDtypeStruct((8, D), f4))
    out_specs.append(pl.BlockSpec((8, D), lambda s, *unused: (0, 0)))
    return pl.pallas_call(
        attend_back_kernel,
        grid_spec=pltpu.PrefetchScalarGridSpec(
            num_scalar_prefetch=1,
            grid=(seqs,),
            in_specs=[by_seq(a.shape) for a in (og, grad_h2, ffn, middle)]
            + [whole(a) for a in (weights, vectors, projt, cosine, sine)]
            + [by_seq(a.shape) for a in kept],
            out_specs=out_specs,
        ),
        out_shape=out_shapes,
        compiler_params=pltpu.CompilerParams(vmem_limit_bytes=LIMIT),
        cost_estimate=estimate(seqs * rows * D * D * 8, 50e6),
        name="attend_back",
    )(lengths, og, grad_h2, ffn, middle, weights, vectors, projt, cosine, sine, *kept)


def input_back(x, grad_middle, grads, weights, vectors):
    seqs, rows, unused_width = x.shape
    return pl.pallas_call(
        input_back_kernel,
        grid=(seqs,),
        in_specs=[by_seq(x.shape), by_seq(x.shape)] + [by_seq_second(a.shape) for a in grads] + [whole(weights), whole(vectors)],
        out_specs=[by_seq(x.shape), pl.BlockSpec((8, D), lambda s: (0, 0))],
        out_shape=[jax.ShapeDtypeStruct(x.shape, jnp.float32), jax.ShapeDtypeStruct((8, D), jnp.float32)],
        compiler_params=pltpu.CompilerParams(vmem_limit_bytes=LIMIT),
        cost_estimate=estimate(seqs * rows * D * D * 6, 15e6),
        name="input_back",
    )(x, grad_middle, *grads, weights, vectors)


def attn_weights(h1, mixed, grads, wide_size):
    narrow_size, seqs, rows, width = grads[0].shape
    tokens = seqs * rows
    flat = [a.reshape(narrow_size, tokens, width) for a in grads]
    h1, mixed = h1.reshape(tokens, D), mixed.reshape(tokens, D)
    shape = (narrow_size, wide_size, 2 * D // wide_size, 2 * width)
    return pl.pallas_call(
        attn_weight_kernel,
        grid=(narrow_size,),
        in_specs=[whole(h1), whole(mixed)] + [pl.BlockSpec((None, tokens, width), lambda n: (n, 0, 0))] * 4,
        out_specs=pl.BlockSpec((1,) + shape[1:], lambda n: (n, 0, 0, 0)),
        out_shape=jax.ShapeDtypeStruct(shape, jnp.bfloat16),
        compiler_params=pltpu.CompilerParams(vmem_limit_bytes=LIMIT),
        cost_estimate=estimate(tokens * D * D * 8, 15e6),
        name="attn_weights",
    )(h1, mixed, *flat)


def ffn_tile(tile, h2, og, w_in, w_back, bias, past, wide_size, narrow_size, blocks):
    seqs, rows, unused_width = h2.shape
    width = w_in.shape[2]
    step = 512 if width % 512 == 0 else width
    if blocks:
        shape = (narrow_size, wide_size, 2 * D // wide_size, width // narrow_size)
        gw_spec = pl.BlockSpec(shape, lambda i: (0, 0, 0, 0))
    else:
        shape = (2, D, width)
        gw_spec = pl.BlockSpec((2, D, step), lambda i: (0, 0, i))
    tokens = jax.ShapeDtypeStruct(h2.shape, jnp.float32)
    return pl.pallas_call(
        partial(ffn_kernel, past is not None, blocks),
        grid=(width // step,),
        in_specs=[
            whole(h2),
            whole(og),
            pl.BlockSpec((None, D, step), lambda i: (tile, 0, i)),
            pl.BlockSpec((None, step, D), lambda i: (tile, i, 0)),
            pl.BlockSpec((None, 1, step), lambda i: (tile, 0, i)),
        ]
        + [whole(a) for a in past or ()],
        out_specs=[whole(h2), whole(h2), gw_spec, pl.BlockSpec((1, step), lambda i: (0, i))],
        out_shape=[tokens, tokens, jax.ShapeDtypeStruct(shape, jnp.bfloat16), jax.ShapeDtypeStruct((1, width), jnp.float32)],
        scratch_shapes=[pltpu.VMEM((seqs * rows, step), jnp.bfloat16)] * 2,
        compiler_params=pltpu.CompilerParams(vmem_limit_bytes=LIMIT),
        cost_estimate=estimate(seqs * rows * D * width * 12, 20e6, seqs * rows * width * 2),
        name="ffn_tile",
    )(h2, og, w_in, w_back, bias, *(past or ()))


def rotary_blocks(length):
    half = HDIM // 2
    frequency = jnp.exp(jnp.arange(half, dtype=jnp.float32) * (-2.0 * math.log(10000.0) / HDIM))
    angles = jnp.arange(length, dtype=jnp.float32)[:, None] * frequency[None, :]
    cosine, sine = jnp.cos(angles), jnp.sin(angles)
    return jnp.tile(cosine, (1, 4)), jnp.tile(jnp.concatenate([-sine, sine], axis=1), (1, 2))


def projection_blocks(feature_proj):
    rows = jnp.arange(GF)[:, None] // FEAT
    columns = jnp.arange(GE)[None, :] // HDIM
    mask = (rows == columns).astype(jnp.float32)
    tall = jnp.tile(feature_proj.reshape(GROUPS, GF, HDIM), (1, 1, GROUP)) * mask
    high, low = halves(tall)
    square = jnp.broadcast_to(-0.5 * mask, tall.shape).astype(jnp.bfloat16)
    turned = [a.swapaxes(1, 2) for a in (high, high, low, square, square)]
    return jnp.concatenate(turned, axis=1), jnp.concatenate([high, high, low], axis=1)


def xor_pairs(size, mask):
    return [(index, index ^ mask) for index in range(size)]


def swap(value, axis_name, mask):
    return lax.ppermute(value, axis_name, xor_pairs(lax.axis_size(axis_name), mask))


def far_masks(axis_name):
    return [2 * m for m in range(1, lax.axis_size(axis_name) // 2)]


def gather_wide(piece):
    block = jnp.stack([piece] + [swap(piece, "wide", mask) for mask in far_masks("wide")])
    return jnp.stack([block, swap(block, "wide", 1)])


def gather_near(piece, far):
    block = gather_wide(piece)[None]
    if far:
        block = jnp.concatenate([block] + [swap(block, "narrow", mask) for mask in far_masks("narrow")])
    return block, swap(block, "narrow", 1)


def place_kernel(copies, me_ref, mine_ref, theirs_ref, out_ref, sems):
    started = []
    for side, ref in enumerate((mine_ref, theirs_ref)):
        for far in range(ref.shape[0]):
            for near in range(2):
                for m in range(ref.shape[2]):
                    wide = me_ref[0] ^ (2 * m + near)
                    narrow = me_ref[1] ^ (2 * far + side)
                    copy = pltpu.make_async_copy(
                        ref.at[far, near, m], copies(out_ref, wide, narrow), sems.at[len(started)]
                    )
                    copy.start()
                    started.append(copy)
    for copy in started:
        copy.wait()


def place(pair, target, shape, name):
    mine, theirs = pair
    me = jnp.stack([lax.axis_index("wide"), lax.axis_index("narrow")]).astype(jnp.int32)
    anywhere = pl.BlockSpec(memory_space=pl.ANY)
    return pl.pallas_call(
        partial(place_kernel, target),
        out_shape=jax.ShapeDtypeStruct(shape, mine.dtype),
        in_specs=[pl.BlockSpec(memory_space=pltpu.SMEM), anywhere, anywhere],
        out_specs=pl.BlockSpec(memory_space=pltpu.VMEM),
        compiler_params=pltpu.CompilerParams(vmem_limit_bytes=LIMIT),
        scratch_shapes=[pltpu.SemaphoreType.DMA((2 * math.prod(mine.shape[:3]),))],
        cost_estimate=pl.CostEstimate(flops=0, bytes_accessed=2 * math.prod(shape) * 2, transcendentals=0),
        name=name,
    )(me, mine, theirs)


def in_order(pair):
    both = jnp.stack(pair)
    sides, fars, unused_two, ms = both.shape[:4]
    piece = both.shape[4:]
    flat = both.reshape((sides * fars * 2 * ms,) + piece)
    my_wide, my_narrow = lax.axis_index("wide"), lax.axis_index("narrow")
    ordered = []
    for wide_index in range(2 * ms):
        for narrow_index in range(sides * fars):
            wide_mask = wide_index ^ my_wide
            narrow_mask = (narrow_index ^ my_narrow) & (sides * fars - 1)
            at = ((narrow_mask & 1) * fars + (narrow_mask >> 1)) * 2 + (wide_mask & 1)
            ordered.append(pick(flat, at * ms + (wide_mask >> 1), 0))
    return jnp.stack(ordered).reshape((2 * ms, sides * fars) + piece)


def pick(value, index, axis):
    return lax.dynamic_index_in_dim(value, index, axis, keepdims=False)


def fold(value, axis_name, masks, shift):
    place = lax.axis_index(axis_name)
    here = pick(value, (place >> shift) & (value.shape[0] - 1), 0).astype(jnp.float32)
    for mask in masks:
        other = ((place ^ mask) >> shift) & (value.shape[0] - 1)
        here = here + swap(pick(value, other, 0), axis_name, mask).astype(jnp.float32)
    return here


def scatter_blocks(parts, wire, far_last):
    wide_size = lax.axis_size("wide")
    narrow_size = lax.axis_size("narrow")
    rest = parts.shape[2:]
    value = parts.astype(wire).reshape((narrow_size // 2, 2, wide_size) + rest).swapaxes(0, 1)
    value = fold(value, "narrow", [1], 0).astype(wire)
    if not far_last:
        value = fold(value, "narrow", far_masks("narrow"), 1).astype(wire)[None]
    held = value.shape[0]
    value = value.reshape((held, wide_size // 2, 2) + rest)
    value = fold(jnp.moveaxis(value, 2, 0), "wide", [1], 0).astype(wire)
    value = fold(jnp.moveaxis(value, 1, 0), "wide", far_masks("wide"), 1)
    if not far_last:
        return value[0]
    return fold(value.astype(wire), "narrow", far_masks("narrow"), 1)


def narrow_sum(value):
    mask = 1
    while mask < lax.axis_size("narrow"):
        value = value + swap(value, "narrow", mask)
        mask *= 2
    return value


def gram_of(matrices):
    return jnp.einsum("brc,bsc->brs", matrices, matrices, precision=PRECISE)


def bmm(left, right):
    return jnp.einsum("brs,bst->brt", left, right, precision=PRECISE)


def ortho_factor(gram_mat):
    count = gram_mat.shape[-1]
    identity = jnp.eye(count, dtype=jnp.float32)
    square_sum = jnp.trace(gram_mat, axis1=-2, axis2=-1)
    scale = (1.0 / (jnp.sqrt(square_sum) + ORTHO_EPS))[:, None, None]
    gram_mat = gram_mat * scale * scale
    factor = None
    for sweep_index in range(NS_ITERS):
        poly_mat = (
            LINEAR_COEF * identity + CUBIC_COEF * gram_mat + QUINTIC_COEF * bmm(gram_mat, gram_mat)
        )
        factor = poly_mat if factor is None else bmm(poly_mat, factor)
        if sweep_index < NS_ITERS - 1:
            gram_mat = bmm(poly_mat, bmm(gram_mat, poly_mat))
    return factor * scale


def adam_update(param, earlier_first, earlier_second, gradient):
    first_new = FIRST_DECAY * earlier_first + (1.0 - FIRST_DECAY) * gradient
    second_new = SECOND_DECAY * earlier_second + (1.0 - SECOND_DECAY) * gradient * gradient
    first_fix = 1.0 - FIRST_DECAY**ADAM_STEP
    second_fix = 1.0 - SECOND_DECAY**ADAM_STEP
    direction = first_new / first_fix / (jnp.sqrt(second_new / second_fix) + ADAM_EPS)
    return (first_new, second_new, param - VECTOR_RATE * (direction + WEIGHT_DECAY * param))


def per_device(
    block_in,
    out_grad,
    lengths,
    feature_proj,
    attn_in,
    attn_out,
    ffn_in,
    ffn_out,
    norm_params,
    bias_in,
    bias_out,
    mom_attn_in,
    mom_attn_out,
    mom_ffn_in,
    mom_ffn_out,
    first_norms,
    first_bias_in,
    first_bias_out,
    second_norms,
    second_bias_in,
    second_bias_out,
):
    seqs, length, unused_width = block_in.shape
    wide_size, narrow_size = lax.axis_size("wide"), lax.axis_size("narrow")
    column = lax.axis_index("narrow")
    own_rows, own_cols = D // wide_size, D // narrow_size
    ffn_rows = FF // wide_size
    tiles = ffn_rows // 128 if ffn_rows % 128 == 0 else 1
    unit = ffn_rows // tiles
    width = unit * wide_size
    copied = narrow_size == 4 and own_rows % 16 == 0 and unit % 32 == 0 and (width // narrow_size) % 128 == 0
    blocks = unit == 128 and width // narrow_size == 256 and own_cols == 2 * own_rows
    bf = jnp.bfloat16

    four = jnp.concatenate([attn_in.astype(bf), attn_out.astype(bf)[None]])
    low_in = ffn_in.astype(bf).reshape(own_rows, wide_size, tiles, unit).transpose(2, 0, 1, 3).reshape(tiles, own_rows, width)
    low_back = ffn_out.astype(bf).reshape(tiles, unit, D)
    small = jnp.concatenate([norm_params.reshape(-1), bias_in, bias_out]).astype(bf).astype(jnp.float32)
    small_size = small.shape[0]
    small = jnp.pad(small, (0, -small_size % 1024)).reshape(-1, 128)
    part = 4 * D // narrow_size
    four_pair = gather_near(
        lax.dynamic_slice_in_dim(four.transpose(1, 0, 2).reshape(own_rows, 4 * D), column * part, part, 1)
        if part != D
        else pick(four, column, 0),
        True,
    )
    in_part = width // narrow_size
    in_pair = gather_near(lax.dynamic_slice_in_dim(low_in, column * in_part, in_part, 2), True)
    back_part = unit // 2
    back_pair = gather_near(lax.dynamic_slice_in_dim(low_back, (column & 1) * back_part, back_part, 1), False)
    small_all = in_order((gather_wide(small)[None],))[:, 0].reshape(wide_size, -1)[:, :small_size]
    norm_all = small_all[:, : 4 * own_rows].reshape(wide_size, 4, own_rows).transpose(1, 0, 2).reshape(4, D)
    bias_in_all = small_all[:, 4 * own_rows : 4 * own_rows + ffn_rows].reshape(wide_size, tiles, unit)
    bias_in_all = bias_in_all.transpose(1, 0, 2).reshape(tiles, 1, width)
    bias_out_all = small_all[:, 4 * own_rows + ffn_rows :].reshape(1, D)
    vectors = jnp.concatenate([norm_all, bias_out_all, jnp.zeros((3, D), jnp.float32)])
    if copied:
        weights = place(four_pair, lambda out, w, n: out.at[n, pl.ds(w * own_rows, own_rows)], (4, D, D), "place_four")
        w_in = place(
            in_pair,
            lambda out, w, n: out.at[:, pl.ds(w * own_rows, own_rows), pl.ds(n * in_part, in_part)],
            (tiles, D, width),
            "place_in",
        )
        w_back = place(
            back_pair,
            lambda out, w, n: out.at[:, pl.ds(w * unit + (n & 1) * back_part, back_part)],
            (tiles, width, D),
            "place_back",
        )
    else:
        weights = in_order(four_pair).transpose(0, 2, 1, 3).reshape(D, 4, D).transpose(1, 0, 2)
        w_in = in_order(in_pair).transpose(2, 0, 3, 1, 4).reshape(tiles, D, width)
        w_back = in_order(back_pair).transpose(2, 0, 1, 3, 4).reshape(tiles, width, D)

    cosine, sine = rotary_blocks(length)
    proj, projt = projection_blocks(feature_proj)
    middle, h1, h2, *kept, mixed = attend(lengths, block_in, weights, vectors, proj, cosine, sine)
    past = None
    ffn_sums, bias_sums = [], []
    for tile in range(tiles):
        ffn, grad_h2, grad_tile, bias_sum = ffn_tile(
            tile, h2, out_grad, w_in, w_back, bias_in_all, past, wide_size, narrow_size, blocks
        )
        past = (ffn, grad_h2)
        bias_sums.append(bias_sum)
        if blocks:
            ffn_sums.append(scatter_blocks(grad_tile, bf, tile == 1))
        else:
            grad_in = grad_tile[0].reshape(wide_size, own_rows, narrow_size, in_part).transpose(2, 0, 1, 3)
            grad_back = grad_tile[1].reshape(narrow_size, own_cols, wide_size, unit).transpose(0, 2, 1, 3)
            ffn_sums.append((scatter_blocks(grad_in, bf, False), scatter_blocks(grad_back, bf, False)))
    block_out, grad_middle, gb, gq, gk, gv, sums_two = attend_back(
        lengths, out_grad, grad_h2, ffn, middle, weights, vectors, projt, cosine, sine, kept, narrow_size
    )
    grad_four = attn_weights(h1, mixed, (gq, gk, gv, gb), wide_size)
    input_grad, sums_one = input_back(block_in, grad_middle, (gq, gk, gv), weights, vectors)

    four_sum = jnp.concatenate(
        [
            scatter_blocks(grad_four[:, :, own_rows:], bf, False),
            scatter_blocks(grad_four[:, :, :own_rows], bf, True),
        ]
    )
    grad_qkv = jnp.stack([four_sum[own_rows:, :own_cols], four_sum[own_rows:, own_cols:], four_sum[:own_rows, :own_cols]])
    grad_out_w = four_sum[:own_rows, own_cols:]
    in_parts, back_parts = [], []
    for found in ffn_sums:
        if blocks:
            in_parts.append(found[:own_rows])
            back_parts.append(found[own_rows:].reshape(own_rows, 2, 128).transpose(1, 0, 2).reshape(own_cols, 128))
        else:
            in_parts.append(found[0])
            back_parts.append(found[1])
    grad_in_w = jnp.stack([a.reshape(own_rows, wide_size // narrow_size, unit) for a in in_parts], axis=2).reshape(own_rows, -1)
    grad_back_w = jnp.concatenate(back_parts, axis=1).T
    norm_sums = jnp.concatenate([sums_one[:2], sums_two[:2], sums_two[2:3]])
    inner_sums = jnp.concatenate(bias_sums).reshape(tiles, wide_size, unit).transpose(1, 0, 2)
    inner_sums = inner_sums.reshape(wide_size, narrow_size, ffn_rows // narrow_size)
    norm_part = own_rows // narrow_size
    norm_sums = norm_sums.reshape(5, wide_size, narrow_size, norm_part).transpose(1, 2, 0, 3).reshape(wide_size, narrow_size, -1)
    vector_sums = scatter_blocks(jnp.concatenate([norm_sums, inner_sums], axis=2).swapaxes(0, 1), jnp.float32, False)
    grad_norm_vals = vector_sums[: 4 * norm_part].reshape(4, norm_part)
    grad_bias_final = vector_sums[4 * norm_part : 5 * norm_part]
    grad_bias_inner = vector_sums[5 * norm_part :]

    def own_columns(weight):
        block_width = weight.shape[-1] // narrow_size
        return lax.dynamic_slice_in_dim(
            weight, column * block_width, block_width, axis=weight.ndim - 1
        )

    mom_qkv_new = MOMENT_DECAY * mom_attn_in + grad_qkv
    mom_out_new = MOMENT_DECAY * mom_attn_out + grad_out_w
    mom_in_new = MOMENT_DECAY * mom_ffn_in + grad_in_w
    mom_back_new = MOMENT_DECAY * mom_ffn_out + grad_back_w
    stacks = (mom_qkv_new, mom_out_new[None], mom_in_new[None], mom_back_new[None])
    small = jnp.concatenate([gram_of(stacks[0]), gram_of(stacks[1]), gram_of(stacks[2])], axis=0)
    large = gram_of(stacks[3])
    small_factor = ortho_factor(narrow_sum(small))
    large_factor = ortho_factor(narrow_sum(large))
    iterates = (
        bmm(small_factor[:3], stacks[0]),
        bmm(small_factor[3:4], stacks[1]),
        bmm(small_factor[4:5], stacks[2]),
        bmm(large_factor, stacks[3]),
    )
    rate_qkv = MUON_SCALE
    rate_out = MUON_SCALE * math.sqrt(D / (D // 64))
    rate_in = MUON_SCALE * math.sqrt(FF / D)
    rate_back = MUON_SCALE * math.sqrt(D / FF)
    new_qkv = own_columns(attn_in) * (1.0 - rate_qkv * WEIGHT_DECAY) - rate_qkv * iterates[0]
    new_out = own_columns(attn_out) * (1.0 - rate_out * WEIGHT_DECAY) - rate_out * iterates[1][0]
    new_in = own_columns(ffn_in) * (1.0 - rate_in * WEIGHT_DECAY) - rate_in * iterates[2][0]
    new_back = own_columns(ffn_out) * (1.0 - rate_back * WEIGHT_DECAY) - rate_back * iterates[3][0]
    norm_first, norm_second, norm_new = adam_update(
        own_columns(norm_params), first_norms, second_norms, grad_norm_vals
    )
    inner_first, inner_second, inner_new = adam_update(
        own_columns(bias_in), first_bias_in, second_bias_in, grad_bias_inner
    )
    final_first, final_second, final_new = adam_update(
        own_columns(bias_out), first_bias_out, second_bias_out, grad_bias_final
    )
    return (
        block_out,
        input_grad,
        grad_qkv,
        grad_out_w,
        grad_in_w,
        grad_back_w,
        grad_norm_vals,
        grad_bias_inner,
        grad_bias_final,
        mom_qkv_new,
        mom_out_new,
        mom_in_new,
        mom_back_new,
        new_qkv,
        new_out,
        new_in,
        new_back,
        norm_first,
        inner_first,
        final_first,
        norm_second[:2],
        norm_second[2:],
        inner_second,
        final_second,
        norm_new,
        inner_new,
        final_new,
    )


def solution(mesh):
    in_specs = (
        P(("wide", "narrow"), None, None),
        P(("wide", "narrow"), None, None),
        P(("wide", "narrow")),
        P(),
        P(None, "wide", None),
        P("wide", None),
        P("wide", None),
        P("wide", None),
        P(None, "wide"),
        P("wide"),
        P("wide"),
        P(None, "wide", "narrow"),
        P("wide", "narrow"),
        P("wide", "narrow"),
        P("wide", "narrow"),
        P(None, ("wide", "narrow")),
        P(("wide", "narrow")),
        P(("wide", "narrow")),
        P(None, ("wide", "narrow")),
        P(("wide", "narrow")),
        P(("wide", "narrow")),
    )
    out_specs = (
        P(("wide", "narrow"), None, None),
        P(("wide", "narrow"), None, None),
        P(None, "wide", "narrow"),
        P("wide", "narrow"),
        P("wide", "narrow"),
        P("wide", "narrow"),
        P(None, ("wide", "narrow")),
        P(("wide", "narrow")),
        P(("wide", "narrow")),
        P(None, "wide", "narrow"),
        P("wide", "narrow"),
        P("wide", "narrow"),
        P("wide", "narrow"),
        P(None, "wide", "narrow"),
        P("wide", "narrow"),
        P("wide", "narrow"),
        P("wide", "narrow"),
        P(None, ("wide", "narrow")),
        P(("wide", "narrow")),
        P(("wide", "narrow")),
        P(None, ("wide", "narrow")),
        P(None, ("wide", "narrow")),
        P(("wide", "narrow")),
        P(("wide", "narrow")),
        P(None, ("wide", "narrow")),
        P(("wide", "narrow")),
        P(("wide", "narrow")),
    )
    return jax.shard_map(
        per_device, mesh=mesh, in_specs=in_specs, out_specs=out_specs, check_vma=False
    )
```

```python
from functools import partial
import math

import jax
import jax.numpy as jnp
from jax import lax
from jax.experimental import pallas as pl
from jax.experimental.pallas import tpu as pltpu
from jax.sharding import PartitionSpec as P

D = 768
FF = 3072
HEADS = 12
HDIM = 64
FEAT = 32
NS_ITERS = 5
ADAM_STEP = 10


PRECISE = lax.Precision.HIGHEST
NORM_EPS = 1e-05
ORTHO_EPS = 1e-07
ADAM_EPS = 1e-08
LINEAR_COEF = 3.4445
CUBIC_COEF = -4.775
QUINTIC_COEF = 2.0315
MOMENT_DECAY = 0.5
FIRST_DECAY = 0.5
SECOND_DECAY = 0.5
MUON_SCALE = 0.6
WEIGHT_DECAY = 0.01
VECTOR_RATE = 0.4
GROUP = 4
GROUPS = HEADS // GROUP
GE = GROUP * HDIM
GF = GROUP * FEAT


def mm(left, right):
    return jnp.dot(left, right, preferred_element_type=jnp.float32)


def mm_nt(left, right):
    return lax.dot_general(left, right, (((1,), (1,)), ((), ())), preferred_element_type=jnp.float32)


def mm_tn(left, right):
    return lax.dot_general(left, right, (((0,), (0,)), ((), ())), preferred_element_type=jnp.float32)


def halves(value):
    high = value.astype(jnp.bfloat16)
    return high, (value - high.astype(jnp.float32)).astype(jnp.bfloat16)


def normalise(rows):
    centered = rows - jnp.mean(rows, axis=-1, keepdims=True)
    inverse = lax.rsqrt(jnp.mean(centered * centered, axis=-1, keepdims=True) + NORM_EPS)
    return centered * inverse, inverse


def norm_pull(normed, inverse, grad, gain):
    scaled = grad * gain
    mean_plain = jnp.mean(scaled, axis=-1, keepdims=True)
    mean_prod = jnp.mean(scaled * normed, axis=-1, keepdims=True)
    return inverse * (scaled - mean_plain - normed * mean_prod)


def partner_of(values):
    lane = lax.broadcasted_iota(jnp.int32, (values.shape[0], 128), 1)
    first = (lane & (HDIM - 1)) < HDIM // 2
    parts = []
    for at in range(0, values.shape[1], 128):
        block = values[:, at : at + 128]
        ahead = pltpu.roll(block, 128 - HDIM // 2, 1)
        behind = pltpu.roll(block, HDIM // 2, 1)
        parts.append(jnp.where(first, ahead, behind))
    return jnp.concatenate(parts, axis=1)


def head_mask(rows, columns, row_width, column_width):
    row = lax.broadcasted_iota(jnp.int32, (rows, columns), 0) // row_width
    column = lax.broadcasted_iota(jnp.int32, (rows, columns), 1) // column_width
    return row == column


def store_columns(ref, values):
    width = ref.shape[3]
    for n in range(ref.shape[0]):
        ref[n, 0] = values[:, width * n : width * (n + 1)].astype(ref.dtype)


def load_columns(ref):
    return jnp.concatenate([ref[n, 0] for n in range(ref.shape[0])], axis=1)


def attend_kernel(
    first, lengths_ref, x_ref, w_ref, vec_ref, proj_ref, cos_ref, sin_ref,
    middle_ref, h1_ref, h2_ref, wq_ref, wk_ref, pq_ref, pk_ref, v_ref, state_ref, total_ref, att_ref, rden_ref, mixed_ref,
):
    rows = x_ref.shape[1]
    x = x_ref[0].astype(jnp.float32)
    h1 = (normalise(x)[0] * vec_ref[0:1, :] + vec_ref[1:2, :]).astype(jnp.bfloat16)
    h1_ref[0] = h1
    live = lax.broadcasted_iota(jnp.int32, (rows, 1), 0) < lengths_ref[pl.program_id(0) + first]
    live = live.astype(jnp.float32)
    cosine = jnp.concatenate([cos_ref[...]] * (D // 128), axis=1)
    sine = jnp.concatenate([sin_ref[...]] * (D // 128), axis=1)
    values = mm(h1, w_ref[2]).astype(jnp.bfloat16)
    v_ref[0] = values
    feats = []
    for j, (w_out, p_out) in enumerate(((wq_ref, pq_ref), (wk_ref, pk_ref))):
        heads = mm(h1, w_ref[j])
        unit = (heads * cosine + partner_of(heads) * sine) * HDIM ** (-0.25)
        w_out[0] = unit
        high, low = halves(unit)
        sq_high, sq_low = halves(unit * unit)
        parts = []
        for g in range(GROUPS):
            cut = slice(GE * g, GE * (g + 1))
            left = jnp.concatenate([high[:, cut], low[:, cut], high[:, cut], sq_high[:, cut], sq_low[:, cut]], axis=1)
            parts.append(jnp.exp(mm(left, proj_ref[g])) * FEAT ** (-0.5))
        phi = jnp.concatenate(parts, axis=1)
        p_out[0] = phi
        feats.append(phi)
    query_low = feats[0].astype(jnp.bfloat16)
    key_vals = feats[1].astype(jnp.bfloat16).astype(jnp.float32) * live
    key_low = key_vals.astype(jnp.bfloat16)
    total_ref[0] = jnp.sum(key_vals, axis=0, keepdims=True)
    mask = head_mask(GF, GE, FEAT, HDIM)
    ones = jnp.ones((rows, GE), jnp.bfloat16)
    attended, inverse_den = [], []
    for g in range(GROUPS):
        cut = slice(GE * g, GE * (g + 1))
        fcut = slice(GF * g, GF * (g + 1))
        both = mm_tn(key_low[:, fcut], jnp.concatenate([values[:, cut], ones], axis=1))
        state = jnp.where(mask, both[:, :GE], 0.0).astype(jnp.bfloat16)
        state_ref[0, g] = state
        tot_high, tot_low = halves(jnp.where(mask, both[:, GE:], 0.0))
        query = query_low[:, fcut]
        numer = mm(query, state)
        denom = mm(jnp.concatenate([query, query], axis=1), jnp.concatenate([tot_high, tot_low], axis=0))
        inverse = 1.0 / denom
        attended.append(numer * inverse)
        inverse_den.append(inverse)
    attended = jnp.concatenate(attended, axis=1)
    att_ref[0] = attended
    rden_ref[0] = jnp.concatenate(inverse_den, axis=1)
    mixed = attended.astype(jnp.bfloat16)
    mixed_ref[0] = mixed
    middle = x + mm(mixed, w_ref[3])
    middle_ref[0] = middle
    h2_ref[0] = (normalise(middle)[0] * vec_ref[2:3, :] + vec_ref[3:4, :]).astype(jnp.bfloat16)


def middle_back_kernel(og_ref, gh2_ref, ffn_ref, middle_ref, vec_ref, out_ref, gm_ref, gb_ref, sums_ref):
    og = og_ref[0].astype(jnp.float32)
    middle = middle_ref[0]
    out_ref[0] = middle + (ffn_ref[0] + vec_ref[4:5, :])
    grad_h2 = gh2_ref[0]
    normed, inverse = normalise(middle)
    grad_middle = og + norm_pull(normed, inverse, grad_h2, vec_ref[2:3, :])
    gm_ref[0] = grad_middle
    store_columns(gb_ref, grad_middle)

    @pl.when(pl.program_id(0) == 0)
    def _():
        sums_ref[...] = jnp.zeros_like(sums_ref)

    sums_ref[0:1, :] += jnp.sum(grad_h2 * normed, axis=0, keepdims=True)
    sums_ref[1:2, :] += jnp.sum(grad_h2, axis=0, keepdims=True)
    sums_ref[2:3, :] += jnp.sum(og, axis=0, keepdims=True)


def attend_back_kernel(
    lengths_ref, gm_ref, w_ref, projt_ref, cos_ref, sin_ref,
    wq_ref, wk_ref, pq_ref, pk_ref, v_ref, state_ref, total_ref, att_ref, rden_ref,
    gq_ref, gk_ref, gv_ref,
):
    rows = gm_ref.shape[1]
    branch = gm_ref[0].astype(jnp.bfloat16)
    grad_numer = mm_nt(branch, w_ref[0]) * rden_ref[0]
    gn_high, gn_low = halves(grad_numer)
    pr_high, pr_low = halves(grad_numer * att_ref[0])
    live = (lax.broadcasted_iota(jnp.int32, (rows, 1), 0) < lengths_ref[pl.program_id(0)]).astype(jnp.float32)
    query_low = pq_ref[0].astype(jnp.bfloat16)
    key_low = (pk_ref[0].astype(jnp.bfloat16).astype(jnp.float32) * live).astype(jnp.bfloat16)
    mask = head_mask(GF, GE, FEAT, HDIM)
    spread = head_mask(GE, GF, HDIM, FEAT).astype(jnp.float32).astype(jnp.bfloat16)
    spread2 = jnp.concatenate([spread, spread], axis=0)
    gather = mask.astype(jnp.float32).astype(jnp.bfloat16)
    gather2 = jnp.concatenate([gather, gather], axis=0)
    grad_u = ([], [])
    grad_v = []
    for g in range(GROUPS):
        cut = slice(GE * g, GE * (g + 1))
        fcut = slice(GF * g, GF * (g + 1))
        query, key, values = query_low[:, fcut], key_low[:, fcut], v_ref[0, :, cut]
        state = state_ref[0, g]
        grad_denom = -mm(jnp.concatenate([pr_high[:, cut], pr_low[:, cut]], axis=1), spread2)
        two = jnp.concatenate([gn_high[:, cut], gn_low[:, cut]], axis=1)
        grad_qfeat = mm_nt(two, jnp.concatenate([state, state], axis=1)) + grad_denom * total_ref[0, :, fcut]
        pair = mm_tn(query, two)
        grad_state = jnp.where(mask, pair[:, :GE] + pair[:, GE:], 0.0)
        grad_total = jnp.sum(grad_denom * query.astype(jnp.float32), axis=0, keepdims=True)
        gs_high, gs_low = halves(grad_state)
        grad_kfeat = mm_nt(
            jnp.concatenate([values, values], axis=1), jnp.concatenate([gs_high, gs_low], axis=1)
        )
        grad_kfeat = (grad_kfeat + grad_total) * live
        grad_v.append(mm(jnp.concatenate([key, key], axis=1), jnp.concatenate([gs_high, gs_low], axis=0)))
        for j, (grad_feat, p_in, w_in) in enumerate(((grad_qfeat, pq_ref, wq_ref), (grad_kfeat, pk_ref, wk_ref))):
            t_high, t_low = halves(grad_feat * p_in[0, :, fcut])
            pulled = mm(jnp.concatenate([t_high, t_low, t_high], axis=1), projt_ref[g])
            weight = mm(jnp.concatenate([t_high, t_low], axis=1), gather2)
            grad_u[j].append((pulled - weight * w_in[0, :, cut]) * HDIM ** (-0.25))
    cosine = jnp.concatenate([cos_ref[...]] * (D // 128), axis=1)
    sine = jnp.concatenate([sin_ref[...]] * (D // 128), axis=1)
    for grads, ref in zip(grad_u, (gq_ref, gk_ref)):
        turned = jnp.concatenate(grads, axis=1)
        store_columns(ref, turned * cosine - partner_of(turned) * sine)
    store_columns(gv_ref, jnp.concatenate(grad_v, axis=1))


def input_back_kernel(x_ref, gm_ref, gq_ref, gk_ref, gv_ref, w_ref, vec_ref, out_ref, sums_ref):
    grad_h1 = sum(mm_nt(load_columns(ref), w_ref[j]) for j, ref in enumerate((gq_ref, gk_ref, gv_ref)))
    normed, inverse = normalise(x_ref[0].astype(jnp.float32))
    out_ref[0] = gm_ref[0] + norm_pull(normed, inverse, grad_h1, vec_ref[0:1, :])

    @pl.when(pl.program_id(0) == 0)
    def _():
        sums_ref[...] = jnp.zeros_like(sums_ref)

    sums_ref[0:1, :] += jnp.sum(grad_h1 * normed, axis=0, keepdims=True)
    sums_ref[1:2, :] += jnp.sum(grad_h1, axis=0, keepdims=True)


def attn_weight_kernel(me_ref, h1_ref, mixed_ref, gq_ref, gk_ref, gv_ref, gb_ref, *out_refs):
    width, rows = out_refs[0].shape[1], out_refs[0].shape[2] // 2
    h1 = h1_ref[...]
    left = mm_tn(h1, jnp.concatenate([gq_ref[...], gk_ref[...]], axis=1)).astype(jnp.bfloat16)
    right = jnp.concatenate([mm_tn(h1, gv_ref[...]), mm_tn(mixed_ref[...], gb_ref[...])], axis=1).astype(jnp.bfloat16)
    for w in range(width * len(out_refs)):
        out_refs[w // width][0, w % width, :rows] = left[rows * w : rows * (w + 1)]
        out_refs[w // width][0, w % width, rows:] = right[rows * w : rows * (w + 1)]


def ffn_kernel(has_past, blocks, h2_ref, og_ref, win_ref, wback_ref, bias_ref, me_ref, *rest):
    if has_past:
        out_past_ref, gh2_past_ref, *rest = rest
    if blocks:
        out_ref, gh2_ref, bsum_ref, keep_ref, *send_refs, act_ref, gi_ref, gw_ref = rest
    else:
        out_ref, gh2_ref, bsum_ref, gw_ref, act_ref, gi_ref = rest
    seqs, rows = out_ref.shape[0], out_ref.shape[1]
    step = pl.program_id(0)
    win, wback = win_ref[...], wback_ref[...]
    bias = bias_ref[...]

    def part(s, carry):
        span = pl.ds(pl.multiple_of(s * rows, rows), rows)
        inner = mm(h2_ref[s], win) + bias
        grad_act = mm_nt(og_ref[s], wback)
        cdf = 0.5 * (1.0 + lax.erf(inner * (2.0**-0.5)))
        pdf = jnp.exp(-0.5 * inner * inner) * (2.0 * math.pi) ** -0.5
        act = (inner * cdf).astype(jnp.bfloat16)
        grad_inner = (grad_act * (cdf + inner * pdf)).astype(jnp.bfloat16)
        act_ref[span, :] = act
        gi_ref[span, :] = grad_inner
        out_part = mm(act, wback)
        gh2_part = mm_nt(grad_inner, win)

        @pl.when(step == 0)
        def _():
            if has_past:
                out_ref[s] = out_past_ref[s] + out_part
                gh2_ref[s] = gh2_past_ref[s] + gh2_part
            else:
                out_ref[s] = out_part
                gh2_ref[s] = gh2_part

        @pl.when(step > 0)
        def _():
            out_ref[s] += out_part
            gh2_ref[s] += gh2_part

        return carry + jnp.sum(grad_inner.astype(jnp.float32), axis=0, keepdims=True)

    bsum_ref[...] = lax.fori_loop(0, seqs, part, jnp.zeros(bias.shape, jnp.float32))
    h2 = h2_ref[...].reshape(seqs * rows, D)
    og = og_ref[...].reshape(seqs * rows, D)
    grad_in = mm_tn(h2, gi_ref[...]).astype(jnp.bfloat16)
    grad_back = mm_tn(og, act_ref[...]).astype(jnp.bfloat16)
    if not blocks:
        gw_ref[0] = grad_in
        gw_ref[1] = grad_back
        return
    narrow, wide = gw_ref.shape[0], gw_ref.shape[1]
    in_rows, in_cols = D // wide, gw_ref.shape[3]
    width = grad_in.shape[1]
    for k in range(width // in_cols):
        for w in range(wide):
            gw_ref[step * (width // in_cols) + k, w, :in_rows, :] = grad_in[
                in_rows * w : in_rows * (w + 1), in_cols * k : in_cols * (k + 1)
            ]
    back_rows = D // narrow
    half = back_rows // 2
    for k in range(width // 128):
        for n in range(narrow):
            for h in range(2):
                gw_ref[n, step * (width // 128) + k, in_rows:, 128 * h : 128 * (h + 1)] = grad_back[
                    back_rows * n + half * h : back_rows * n + half * (h + 1), 128 * k : 128 * (k + 1)
                ]

    @pl.when(step == pl.num_programs(0) - 1)
    def _():
        side = me_ref[1] & 1
        for far in range(narrow // 2):
            for w in range(wide):
                keep_ref[far, w] = gw_ref[2 * far + side, w]
                width = wide // len(send_refs)
                send_refs[w // width][far, w % width] = gw_ref[2 * far + (1 - side), w]


def spec(shape, index):
    return pl.BlockSpec(shape, index)


LIMIT = 60 * 1024 * 1024
ANYWHERE = pl.BlockSpec(memory_space=pl.ANY)


def skipping(kernel, before, extra):
    def run(*refs):
        return kernel(*refs[:before], *refs[before + extra :])

    return run


def estimate(flops, moved, transcendentals=0):
    return pl.CostEstimate(flops=int(flops), bytes_accessed=int(moved), transcendentals=int(transcendentals))


def whole(array):
    rank = array.ndim
    return pl.BlockSpec(array.shape, lambda *unused: (0,) * rank)


def by_seq(shape):
    rank = len(shape)
    return pl.BlockSpec((1,) + tuple(shape[1:]), lambda s, *unused: (s,) + (0,) * (rank - 1))


def by_seq_second(shape):
    rank = len(shape)
    return pl.BlockSpec((shape[0], 1) + tuple(shape[2:]), lambda s, *unused: (0, s) + (0,) * (rank - 2))


def attend(lengths, x, weights, vectors, proj, cosine, sine, before, after):
    seqs, rows, unused_width = x.shape
    bf, f4 = jnp.bfloat16, jnp.float32
    shapes = [
        ((seqs, rows, D), f4), ((seqs, rows, D), bf), ((seqs, rows, D), bf), ((seqs, rows, D), f4), ((seqs, rows, D), f4),
        ((seqs, rows, HEADS * FEAT), f4), ((seqs, rows, HEADS * FEAT), f4), ((seqs, rows, D), bf),
        ((seqs, GROUPS, GF, GE), bf), ((seqs, 1, HEADS * FEAT), f4), ((seqs, rows, D), f4), ((seqs, rows, D), f4),
        ((seqs, rows, D), bf),
    ]
    half = seqs // 2
    first = 0 if before is None else half
    before = list(before or [])

    def part(shape):
        rank = len(shape)
        return pl.BlockSpec((1,) + tuple(shape[1:]), lambda s, *unused: (s + first,) + (0,) * (rank - 1))

    return pl.pallas_call(
        skipping(partial(attend_kernel, first), 7, len(after) + len(before)),
        grid_spec=pltpu.PrefetchScalarGridSpec(
            num_scalar_prefetch=1,
            grid=(half if first == 0 else seqs - half,),
            in_specs=[part(x.shape)] + [whole(a) for a in (weights, vectors, proj, cosine, sine)]
            + [ANYWHERE] * (len(after) + len(before)),
            out_specs=[part(shape) for shape, unused in shapes],
        ),
        out_shape=[jax.ShapeDtypeStruct(shape, dtype) for shape, dtype in shapes],
        input_output_aliases={7 + len(after) + k: k for k in range(len(before))},
        compiler_params=pltpu.CompilerParams(vmem_limit_bytes=LIMIT),
        cost_estimate=estimate(seqs * rows * D * D * 6, 20e6),
        name="attend",
    )(lengths, x, weights, vectors, proj, cosine, sine, *after, *before)


def middle_back(og, grad_h2, ffn, middle, vectors, narrow_size):
    seqs, rows, unused_width = og.shape
    blocked = (narrow_size, seqs, rows, D // narrow_size)
    full = jax.ShapeDtypeStruct(og.shape, jnp.float32)
    return pl.pallas_call(
        middle_back_kernel,
        grid=(seqs,),
        in_specs=[by_seq(og.shape)] * 4 + [whole(vectors)],
        out_specs=[by_seq(og.shape)] * 2 + [by_seq_second(blocked), pl.BlockSpec((8, D), lambda s: (0, 0))],
        out_shape=[full, full, jax.ShapeDtypeStruct(blocked, jnp.bfloat16), jax.ShapeDtypeStruct((8, D), jnp.float32)],
        compiler_params=pltpu.CompilerParams(vmem_limit_bytes=LIMIT),
        cost_estimate=estimate(1e7, 16e6),
        name="middle_back",
    )(og, grad_h2, ffn, middle, vectors)


def attend_back(lengths, grad_middle, weights, projt, cosine, sine, kept, narrow_size, after):
    seqs, rows, unused_width = grad_middle.shape
    blocked = (narrow_size, seqs, rows, D // narrow_size)
    count = 6 + len(kept)
    return pl.pallas_call(
        skipping(attend_back_kernel, count, len(after)),
        grid_spec=pltpu.PrefetchScalarGridSpec(
            num_scalar_prefetch=1,
            grid=(seqs,),
            in_specs=[by_seq(grad_middle.shape), pl.BlockSpec((1, D, D), lambda s, *unused: (3, 0, 0))]
            + [whole(a) for a in (projt, cosine, sine)]
            + [by_seq(a.shape) for a in kept]
            + [ANYWHERE] * len(after),
            out_specs=[by_seq_second(blocked)] * 3,
        ),
        out_shape=[jax.ShapeDtypeStruct(blocked, jnp.bfloat16)] * 3,
        compiler_params=pltpu.CompilerParams(vmem_limit_bytes=LIMIT),
        cost_estimate=estimate(seqs * rows * D * D * 8, 40e6),
        name="attend_back",
    )(lengths, grad_middle, weights, projt, cosine, sine, *kept, *after)


def input_back(x, grad_middle, grads, weights, vectors, after):
    seqs, rows, unused_width = x.shape
    return pl.pallas_call(
        skipping(input_back_kernel, 4 + len(grads), len(after)),
        grid=(seqs,),
        in_specs=[by_seq(x.shape), by_seq(x.shape)] + [by_seq_second(a.shape) for a in grads] + [whole(weights), whole(vectors)] + [ANYWHERE] * len(after),
        out_specs=[by_seq(x.shape), pl.BlockSpec((8, D), lambda s: (0, 0))],
        out_shape=[jax.ShapeDtypeStruct(x.shape, jnp.float32), jax.ShapeDtypeStruct((8, D), jnp.float32)],
        compiler_params=pltpu.CompilerParams(vmem_limit_bytes=LIMIT),
        cost_estimate=estimate(seqs * rows * D * D * 6, 15e6),
        name="input_back",
    )(x, grad_middle, *grads, weights, vectors, *after)


def attn_weights(me, h1, mixed, grads, wide_size, side, after):
    narrow_size, seqs, rows, width = grads[0].shape
    tokens = seqs * rows
    flat = [a.reshape(narrow_size, tokens, width) for a in grads]
    h1, mixed = h1.reshape(tokens, D), mixed.reshape(tokens, D)
    count = min(4, wide_size // 2) if side else 1
    shape = (narrow_size // 2, wide_size // count, 2 * D // wide_size, 2 * width)

    def block_at(i, me_ref):
        return (2 * i + ((me_ref[1] & 1) ^ side), 0, 0)

    return pl.pallas_call(
        skipping(attn_weight_kernel, 7, len(after)),
        grid_spec=pltpu.PrefetchScalarGridSpec(
            num_scalar_prefetch=1,
            grid=(narrow_size // 2,),
            in_specs=[whole(h1), whole(mixed)] + [pl.BlockSpec((None, tokens, width), block_at)] * 4 + [ANYWHERE] * len(after),
            out_specs=[pl.BlockSpec((1,) + shape[1:], lambda i, *unused: (i, 0, 0, 0))] * count,
        ),
        out_shape=[jax.ShapeDtypeStruct(shape, jnp.bfloat16)] * count,
        compiler_params=pltpu.CompilerParams(vmem_limit_bytes=LIMIT),
        cost_estimate=estimate(tokens * D * D * 4, 8e6),
        name="attn_weights",
    )(me, h1, mixed, *flat, *after)


def ffn_tile(tile, h2, og, w_in, w_back, bias, me, past, wide_size, narrow_size, blocks, after):
    seqs, rows, unused_width = h2.shape
    width = w_in.shape[2]
    step = 512 if width % 512 == 0 else width
    tokens = jax.ShapeDtypeStruct(h2.shape, jnp.float32)
    out_specs = [whole(h2), whole(h2), pl.BlockSpec((1, step), lambda i: (0, i))]
    out_shape = [tokens, tokens, jax.ShapeDtypeStruct((1, width), jnp.float32)]
    scratch = [pltpu.VMEM((seqs * rows, step), jnp.bfloat16)] * 2
    if blocks:
        block = (2 * D // wide_size, width // narrow_size)
        half = jax.ShapeDtypeStruct((narrow_size // 2, wide_size) + block, jnp.bfloat16)
        part = jax.ShapeDtypeStruct((narrow_size // 2, wide_size // 4) + block, jnp.bfloat16)
        out_specs += [whole(half)] + [whole(part)] * 4
        out_shape += [half] + [part] * 4
        scratch.append(pltpu.VMEM((narrow_size, wide_size) + block, jnp.bfloat16))
    else:
        out_specs.append(pl.BlockSpec((2, D, step), lambda i: (0, 0, i)))
        out_shape.append(jax.ShapeDtypeStruct((2, D, width), jnp.bfloat16))
    return pl.pallas_call(
        skipping(partial(ffn_kernel, past is not None, blocks), 6 + len(past or ()), len(after)),
        grid=(width // step,),
        in_specs=[
            whole(h2),
            whole(og),
            pl.BlockSpec((None, D, step), lambda i: (tile, 0, i)),
            pl.BlockSpec((None, step, D), lambda i: (tile, i, 0)),
            pl.BlockSpec((None, 1, step), lambda i: (0, 0, i)),
            pl.BlockSpec(memory_space=pltpu.SMEM),
        ]
        + [whole(a) for a in past or ()]
        + [ANYWHERE] * len(after),
        out_specs=out_specs,
        out_shape=out_shape,
        scratch_shapes=scratch,
        compiler_params=pltpu.CompilerParams(vmem_limit_bytes=LIMIT),
        cost_estimate=estimate(seqs * rows * D * width * 12, 20e6, seqs * rows * width * 2),
        name="ffn_tile",
    )(h2, og, w_in, w_back, bias, me, *(past or ()), *after)


def rotary_blocks(length):
    half = HDIM // 2
    frequency = jnp.exp(jnp.arange(half, dtype=jnp.float32) * (-2.0 * math.log(10000.0) / HDIM))
    angles = jnp.arange(length, dtype=jnp.float32)[:, None] * frequency[None, :]
    cosine, sine = jnp.cos(angles), jnp.sin(angles)
    return jnp.tile(cosine, (1, 4)), jnp.tile(jnp.concatenate([-sine, sine], axis=1), (1, 2))


def projection_blocks(feature_proj):
    rows = jnp.arange(GF)[:, None] // FEAT
    columns = jnp.arange(GE)[None, :] // HDIM
    mask = (rows == columns).astype(jnp.float32)
    tall = jnp.tile(feature_proj.reshape(GROUPS, GF, HDIM), (1, 1, GROUP)) * mask
    high, low = halves(tall)
    square = jnp.broadcast_to(-0.5 * mask, tall.shape).astype(jnp.bfloat16)
    turned = [a.swapaxes(1, 2) for a in (high, high, low, square, square)]
    return jnp.concatenate(turned, axis=1), jnp.concatenate([high, high, low], axis=1)


def xor_pairs(size, mask):
    return [(index, index ^ mask) for index in range(size)]


def tie(value, *earlier):
    return lax.optimization_barrier((value, earlier))[0]


def swap(value, axis_name, mask):
    return lax.ppermute(value, axis_name, xor_pairs(lax.axis_size(axis_name), mask))


def far_masks(axis_name):
    return [2 * m for m in range(1, lax.axis_size(axis_name) // 2)]


class Gather:
    def __init__(self, pieces, cut):
        self.cut = cut
        self.pieces = pieces

    def near(self, *earlier):
        self.pieces = [tie(piece, *earlier) for piece in self.pieces] if earlier else self.pieces
        self.first = jnp.stack([piece[..., : -self.cut, :] for piece in self.pieces])
        self.second = jnp.stack([piece[..., -self.cut :, :] for piece in self.pieces])
        self.first_in = swap(self.first, "wide", 1)
        self.second_in = [swap(self.second, "narrow", mask) for mask in far_masks("narrow")]
        return [self.first_in] + self.second_in

    def far(self, *earlier):
        if earlier:
            self.first_in = tie(self.first_in, *earlier)
        self.first = jnp.stack([self.first, self.first_in])
        self.extra = self.first[..., self.cut :, :]
        self.first = self.first[..., : self.cut, :]
        self.second = jnp.stack([self.second] + (list(tie(tuple(self.second_in), *earlier)) if earlier else self.second_in))
        self.first_in = [swap(self.first, "narrow", mask) for mask in far_masks("narrow")]
        self.second_in = swap(self.second, "wide", 1)
        return self.first_in + [self.second_in]

    def core(self):
        self.mine = [self.first] + self.first_in + [self.second, self.second_in]
        self.theirs = [swap(part, "narrow", 1) for part in self.mine]
        return self.theirs


def far_wide(piece):
    return [piece] + [swap(piece, "wide", mask) for mask in far_masks("wide")]


def gathered_at(part, index, side, fars, ms):
    m, index = index % ms, index // ms
    half, near, far = (0, index, part) if part < fars else (1, part - fars, index)
    return half, 2 * m + near, 2 * far + side


def place_kernel(copies, fars, ms, me_ref, *rest):
    count = 2 * (fars + 2)
    refs, outs, sems = rest[:count], rest[count:-1], rest[-1]
    started = []
    for k, ref in enumerate(refs):
        side, part = divmod(k, count // 2)
        for index in range(ref.shape[0] * ms):
            half, wide_mask, narrow_mask = gathered_at(part, index, side, fars, ms)
            wide, narrow = me_ref[0] ^ wide_mask, me_ref[1] ^ narrow_mask
            for source, target in copies(ref.at[index // ms, index % ms], outs, half, wide, narrow):
                copy = pltpu.make_async_copy(source, target, sems.at[len(started)])
                copy.start()
                started.append(copy)
    for copy in started:
        copy.wait()


def place(me, parts, copies, shapes, each, name):
    fars, ms = lax.axis_size("narrow") // 2, lax.axis_size("wide") // 2
    return pl.pallas_call(
        partial(place_kernel, copies, fars, ms),
        out_shape=[jax.ShapeDtypeStruct(shape, parts[0].dtype) for shape in shapes],
        in_specs=[pl.BlockSpec(memory_space=pltpu.SMEM)] + [ANYWHERE] * len(parts),
        out_specs=[pl.BlockSpec(memory_space=pltpu.VMEM)] * len(shapes),
        compiler_params=pltpu.CompilerParams(vmem_limit_bytes=LIMIT),
        scratch_shapes=[pltpu.SemaphoreType.DMA((4 * fars * ms * (1 + each),))],
        cost_estimate=estimate(0, 4 * sum(math.prod(shape) for shape in shapes)),
        name=name,
    )(me, *parts)


def in_order(parts, wide_size, narrow_size, place_of):
    my_wide, my_narrow = lax.axis_index("wide"), lax.axis_index("narrow")
    ordered = [
        pick(parts, place_of(w ^ my_wide, n ^ my_narrow), 0) for w in range(wide_size) for n in range(narrow_size)
    ]
    return jnp.stack(ordered).reshape((wide_size, narrow_size) + parts.shape[1:])


def half_in_order(parts, half):
    wide_size, narrow_size = lax.axis_size("wide"), lax.axis_size("narrow")
    fars, ms = narrow_size // 2, wide_size // 2

    def place_of(wide_mask, narrow_mask):
        near, m, side, far = wide_mask & 1, wide_mask >> 1, narrow_mask & 1, narrow_mask >> 1
        outer = far * 2 + near if half == 0 else near * fars + far
        return side * (fars * 2 * ms) + outer * ms + m

    count = len(parts) // 2
    found = []
    for side in range(2):
        own = parts[side * count : (side + 1) * count]
        found += own[:fars] if half == 0 else own[fars:]
    found = [part.reshape((-1,) + part.shape[2:]) for part in found]
    return in_order(jnp.concatenate(found), wide_size, narrow_size, place_of)


def pick(value, index, axis):
    return lax.dynamic_index_in_dim(value, index, axis, keepdims=False)


def core_swap(send):
    return [swap(part, "narrow", 1) for part in send]


def cut_wide(send):
    count = min(4, send.shape[1] // 2)
    width = send.shape[1] // count
    return [lax.slice_in_dim(send, width * k, width * (k + 1), axis=1) for k in range(count)]


class Stream:
    def __init__(self, keep, arrived, order, window=None):
        rest = keep.shape[2:]
        self.quarters, self.wide = len(arrived), keep.shape[1]
        self.window = window or (0, rest[0])
        self.rest = (self.window[1] - self.window[0],) + rest[1:]
        self.order = list(order)
        self.dims = {"y": keep.shape[0], "z": keep.shape[1] // 2, "x": 2}
        self.parts = [part.reshape((1, -1) + rest) for part in [keep] + arrived]

    def plan(self):
        by_all = self.order[0] == "a"
        axis = "z" if by_all else self.order[0]
        names = [name for name in ("y", "z", "x") if name in self.dims]
        sizes = [self.dims[name] for name in names]
        cut = names.index(axis)
        stride = math.prod(sizes[cut + 1 :])
        places = [
            outer * sizes[cut] * stride + inner for outer in range(math.prod(sizes[:cut])) for inner in range(stride)
        ]
        return by_all, axis, sizes[cut], stride, places

    def outputs(self):
        by_all, unused_axis, size, unused_stride, places = self.plan()
        shape = (len(places),) + self.rest
        return [(size,) + shape] if by_all else [(1,) + shape] * size

    def sent(self, pieces):
        axis = self.order.pop(0)
        self.quarters = 0
        del self.dims["z" if axis == "a" else axis]
        self.window = (0, self.rest[0])
        if axis == "a":
            groups = [list(range(near, lax.axis_size("wide"), 2)) for near in range(2)]
            self.parts = [lax.all_to_all(pieces[0], "wide", 0, 0, axis_index_groups=groups)]
        else:
            name, scale = ("narrow", 2) if axis == "y" else ("wide", 1 if axis == "x" else 2)
            self.parts = [pieces[0]] + [swap(piece, name, scale * m) for m, piece in enumerate(pieces) if m]

    def last(self):
        return [part.reshape((-1,) + self.rest) for part in self.parts]


def fold_kernel(plans, counts, windows, quarters, me_ref, *refs):
    for (by_all, axis, size, stride, places), count, (low, high), parts in zip(plans, counts, windows, quarters):
        ins, refs = take(refs, count)
        outs, refs = take(refs, 1 if by_all else size)
        here = me_ref[1] >> 1 if axis == "y" else me_ref[0] & 1 if axis == "x" else me_ref[0] >> 1
        for step in range(size):
            at = step * stride if by_all else (here ^ step) * stride
            for k, base in enumerate(places):
                found = [(ref, source, base + at) for ref in (ins[:1] if parts else ins) for source in range(ref.shape[0])]
                if parts:
                    wide = parts[1]
                    width = wide // parts[0]
                    far, left = (here ^ step, base) if axis == "y" else (base // wide, base % wide)
                    inner = left % width if axis == "y" else left % width + at
                    found.append((ins[1 + left // width], 0, far * width + inner))
                total = sum(ref[source, place, low:high].astype(jnp.float32) for ref, source, place in found)
                out = outs[0].at[step, k] if by_all else outs[step].at[0, k]
                out[...] = total.astype(out.dtype)


def interleaved(kernel, before, extra, out_counts, counts):
    def run(*refs):
        ins, outs = refs[1:before], refs[before + extra :]
        turn = []
        for out_count, count in zip(out_counts, counts):
            part, ins = take(ins, count)
            turn += part
            part, outs = take(outs, out_count)
            turn += part
        return kernel(refs[0], *turn)

    return run


def fold_streams(streams, me, after):
    plans = [stream.plan() for stream in streams]
    counts = [len(stream.parts) for stream in streams]
    windows = [stream.window for stream in streams]
    out_shapes = [
        [jax.ShapeDtypeStruct(shape, stream.parts[0].dtype) for shape in stream.outputs()] for stream in streams
    ]
    operands = sum((stream.parts for stream in streams), [])
    quarters = [(stream.quarters, stream.wide) if stream.quarters else None for stream in streams]
    kernel = partial(fold_kernel, plans, counts, windows, quarters)
    found = pl.pallas_call(
        interleaved(kernel, 1 + len(operands), len(after), [len(shapes) for shapes in out_shapes], counts),
        in_specs=[pl.BlockSpec(memory_space=pltpu.SMEM)] + [whole_plain(a) for a in operands] + [ANYWHERE] * len(after),
        out_shape=sum(out_shapes, []),
        compiler_params=pltpu.CompilerParams(vmem_limit_bytes=LIMIT),
        cost_estimate=estimate(1e6, 6e6),
        name="fold",
    )(me, *operands, *after)
    token = found[0]
    for stream, shapes in zip(streams, out_shapes):
        part, found = take(found, len(shapes))
        stream.sent(part)
    return token


def narrow_sum(value):
    mask = 1
    while mask < lax.axis_size("narrow"):
        value = value + swap(value, "narrow", mask)
        mask *= 2
    return value


def exact(left, right, dims=(((1,), (0,)), ((), ()))):
    return lax.dot_general(left, right, dims, precision=PRECISE, preferred_element_type=jnp.float32)


def diagonal_of(shape):
    return lax.broadcasted_iota(jnp.int32, shape, 0) == lax.broadcasted_iota(jnp.int32, shape, 1)


def ortho_scale(gram_mat):
    square_sum = jnp.where(diagonal_of(gram_mat.shape), gram_mat, 0.0)
    square_sum = jnp.sum(jnp.sum(square_sum, axis=1, keepdims=True), axis=0, keepdims=True)
    return 1.0 / (jnp.sqrt(square_sum) + ORTHO_EPS)


def sweeps(grams, factors, count, last):
    for left in reversed(range(count)):
        polys = [CUBIC_COEF * gram + QUINTIC_COEF * exact(gram, gram) for gram in grams]
        polys = [jnp.where(diagonal_of(poly.shape), poly + LINEAR_COEF, poly) for poly in polys]
        factors = polys if factors is None else [exact(poly, factor) for poly, factor in zip(polys, factors)]
        if left or not last:
            grams = [exact(poly, gram) for poly, gram in zip(polys, grams)]
            grams = [exact(poly, gram) for poly, gram in zip(polys, grams)]
    return grams, factors


def ortho_start(grams):
    scales = [ortho_scale(gram) for gram in grams]
    return [gram * scale * scale for gram, scale in zip(grams, scales)], scales


def block_pairs(count):
    return [(row, column) for row in range(count) for column in range(row + 1)]


def packed_blocks(small, large, out_ref):
    size = out_ref.shape[1]
    pairs = block_pairs(large.shape[0] // size)
    for k, (row, column) in enumerate(pairs):
        out_ref[k] = large[size * row : size * (row + 1), size * column : size * (column + 1)]
    rows = small.shape[0]
    out_ref[len(pairs)] = jnp.zeros(out_ref.shape[1:], jnp.float32)
    out_ref[len(pairs), :rows, :rows] = small


def unpacked_blocks(blocks, rows, count):
    pairs = block_pairs(count)
    found = {}
    for k, (row, column) in enumerate(pairs):
        found[row, column] = blocks[k]
        if row != column:
            found[column, row] = blocks[k].T
    large = [jnp.concatenate([found[row, column] for column in range(count)], axis=1) for row in range(count)]
    return blocks[len(pairs)][:rows, :rows], jnp.concatenate(large, axis=0)


def sweep_kernel(count, rows, blocks_ref, small_ref, large_ref, small_factor_ref, large_factor_ref):
    size = blocks_ref.shape[1]
    grams = unpacked_blocks(blocks_ref[...], rows, large_ref.shape[0] // size)
    grams, scales = ortho_start(grams)
    grams, factors = sweeps(grams, None, count, False)
    for gram, factor, scale, gram_ref, factor_ref in zip(
        grams, factors, scales, (small_ref, large_ref), (small_factor_ref, large_factor_ref)
    ):
        gram_ref[...] = gram
        factor_ref[...] = factor * scale


def moment_step(gradient, moment_ref, grad_ref, new_ref, at=()):
    grad_ref[at + (slice(None), slice(None))] = gradient
    moment = MOMENT_DECAY * moment_ref[at + (slice(None), slice(None))] + gradient
    new_ref[at + (slice(None), slice(None))] = moment
    return exact(moment, moment, (((1,), (1,)), ((), ())))


def sum_of(refs):
    return sum(ref[k].astype(jnp.float32) for ref in refs for k in range(ref.shape[0]))


def take(refs, count):
    return refs[:count], refs[count:]


def attn_moment_kernel(counts, mqkv_ref, mout_ref, *refs):
    left, refs = take(refs, counts[0])
    right, refs = take(refs, counts[1])
    gqkv_ref, gout_ref, nqkv_ref, nout_ref, gram_ref = refs
    left, right = sum_of(left), sum_of(right)
    width = mout_ref.shape[1]
    gram_ref[0] = moment_step(left[:, :width], mqkv_ref, gqkv_ref, nqkv_ref, (0,))
    gram_ref[1] = moment_step(left[:, width:], mqkv_ref, gqkv_ref, nqkv_ref, (1,))
    gram_ref[2] = moment_step(right[:, :width], mqkv_ref, gqkv_ref, nqkv_ref, (2,))
    gram_ref[3] = moment_step(right[:, width:], mout_ref, gout_ref, nout_ref)


def ffn_moment_kernel(counts, unit, min_ref, mback_ref, *refs):
    found = []
    for count in counts:
        part, refs = take(refs, count)
        found.append(sum_of(part))
    gin_ref, gback_ref, nin_ref, nback_ref, blocks_ref = refs
    rows = min_ref.shape[0]
    if len(found) * 128 == mback_ref.shape[0]:
        grad_in = [part[:rows] for part in found]
        turned = [jnp.concatenate([part[rows:, :128], part[rows:, 128:]], axis=0) for part in found]
        turned = jnp.concatenate(turned, axis=1)
    else:
        grad_in, turned = [found[0]], found[1]
    pieces = [part[:, at : at + unit] for at in range(0, grad_in[0].shape[1], unit) for part in grad_in]
    small = moment_step(jnp.concatenate(pieces, axis=1), min_ref, gin_ref, nin_ref)
    packed_blocks(small, moment_step(turned.T, mback_ref, gback_ref, nback_ref), blocks_ref)


def attn_ortho_kernel(rates, gram_ref, nqkv_ref, nout_ref, wqkv_ref, wout_ref, vqkv_ref, vout_ref):
    grams, scales = ortho_start([gram_ref[j] for j in range(4)])
    factors = sweeps(grams, None, NS_ITERS, True)[1]
    for j in range(4):
        factor = factors[j] * scales[j]
        if j < 3:
            ortho = exact(factor, nqkv_ref[j])
            vqkv_ref[j] = wqkv_ref[j] * (1.0 - rates[0] * WEIGHT_DECAY) - rates[0] * ortho
        else:
            ortho = exact(factor, nout_ref[...])
            vout_ref[...] = wout_ref[...] * (1.0 - rates[1] * WEIGHT_DECAY) - rates[1] * ortho


def ffn_ortho_kernel(
    rates, count, gin_ref, gback_ref, fin_ref, fback_ref, nin_ref, nback_ref, win_ref, wback_ref, vin_ref, vback_ref
):
    grams, factors = [gin_ref[...], gback_ref[...]], [fin_ref[...], fback_ref[...]]
    factors = sweeps(grams, factors, count, True)[1]
    for rate, factor, new_ref, old_ref, out_ref in (
        (rates[0], factors[0], nin_ref, win_ref, vin_ref),
        (rates[1], factors[1], nback_ref, wback_ref, vback_ref),
    ):
        ortho = exact(factor, new_ref[...])
        out_ref[...] = old_ref[...] * (1.0 - rate * WEIGHT_DECAY) - rate * ortho


def simple_call(kernel, args, shapes, name, flops, after=()):
    def run(*refs):
        kernel(*refs[: len(args)], *refs[len(args) + len(after) :])

    return pl.pallas_call(
        run,
        in_specs=[whole_plain(a) for a in args] + [pl.BlockSpec(memory_space=pl.ANY)] * len(after),
        out_shape=[jax.ShapeDtypeStruct(shape, jnp.float32) for shape in shapes],
        compiler_params=pltpu.CompilerParams(vmem_limit_bytes=LIMIT),
        cost_estimate=estimate(flops, 4e6),
        name=name,
    )(*args, *after)


def whole_plain(unused_array):
    return pl.BlockSpec(memory_space=pltpu.VMEM)


def adam_update(param, earlier_first, earlier_second, gradient):
    first_new = FIRST_DECAY * earlier_first + (1.0 - FIRST_DECAY) * gradient
    second_new = SECOND_DECAY * earlier_second + (1.0 - SECOND_DECAY) * gradient * gradient
    first_fix = 1.0 - FIRST_DECAY**ADAM_STEP
    second_fix = 1.0 - SECOND_DECAY**ADAM_STEP
    direction = first_new / first_fix / (jnp.sqrt(second_new / second_fix) + ADAM_EPS)
    return (first_new, second_new, param - VECTOR_RATE * (direction + WEIGHT_DECAY * param))


def per_device(
    block_in,
    out_grad,
    lengths,
    feature_proj,
    attn_in,
    attn_out,
    ffn_in,
    ffn_out,
    norm_params,
    bias_in,
    bias_out,
    mom_attn_in,
    mom_attn_out,
    mom_ffn_in,
    mom_ffn_out,
    first_norms,
    first_bias_in,
    first_bias_out,
    second_norms,
    second_bias_in,
    second_bias_out,
):
    seqs, length, unused_width = block_in.shape
    wide_size, narrow_size = lax.axis_size("wide"), lax.axis_size("narrow")
    column = lax.axis_index("narrow")
    own_rows, own_cols = D // wide_size, D // narrow_size
    ffn_rows = FF // wide_size
    tiles = ffn_rows // 128 if ffn_rows % 128 == 0 else 1
    unit = ffn_rows // tiles
    width = unit * wide_size
    copied = narrow_size == 4 and own_rows % 16 == 0 and unit % 32 == 0 and (width // narrow_size) % 128 == 0
    blocks = unit == 128 and width // narrow_size == 256 and own_cols == 2 * own_rows
    bf = jnp.bfloat16

    me = jnp.stack([lax.axis_index("wide"), column]).astype(jnp.int32)

    small = jnp.concatenate([norm_params.reshape(-1), bias_in, bias_out]).astype(bf)
    small_size = small.shape[0]
    part = 4 * D // narrow_size
    four = jnp.concatenate([attn_in.astype(bf), attn_out.astype(bf)[None]])
    if part == D:
        four = pick(four, column, 0)
    else:
        four = lax.dynamic_slice_in_dim(four.transpose(1, 0, 2).reshape(own_rows, 4 * D), column * part, part, 1)
    small = jnp.pad(small, (0, -small_size % (8 * part))).reshape(-1, part)
    split = own_rows // 2
    four_gather = Gather(far_wide(jnp.concatenate([four[:split], small, four[split:]])), split)

    in_part = width // narrow_size
    back_part = unit // narrow_size
    folds = D // in_part
    low_in = ffn_in.astype(bf).reshape(own_rows, wide_size, tiles, unit).transpose(2, 0, 1, 3).reshape(tiles, own_rows, width)
    low_in = lax.dynamic_slice_in_dim(low_in, column * in_part, in_part, 2)
    low_back = lax.dynamic_slice_in_dim(ffn_out.reshape(tiles, unit, D), column * back_part, back_part, 1).astype(bf)
    low_back = low_back.reshape(tiles, back_part, folds, in_part).transpose(0, 2, 1, 3).reshape(tiles, own_rows, in_part)
    low_ffn = jnp.concatenate([low_in, low_back], axis=1)
    four_in = four_gather.near()
    ffn_gathers = [Gather(far_wide(tie(low_ffn[:1], *four_gather.pieces[1:])), own_rows)]
    four_far = four_gather.far(*ffn_gathers[0].pieces[1:])
    if tiles > 1:
        ffn_gathers.append(Gather(far_wide(tie(low_ffn[1:], *four_in)), own_rows))
    four_gather.core()
    ready = ffn_gathers[0].near(*four_far)
    for gather in ffn_gathers[1:]:
        ready += gather.pieces[1:]
    four_parts = four_gather.mine + list(tie(tuple(four_gather.theirs), *ready))
    ready = ffn_gathers[0].far(*four_gather.theirs)
    ms = wide_size // 2
    small_all = in_order(
        four_gather.extra.reshape((-1,) + small.shape), wide_size, 1, lambda w, n: (w & 1) * ms + (w >> 1)
    )
    small_all = small_all.reshape(wide_size, -1)[:, :small_size].astype(jnp.float32)
    norm_all = small_all[:, : 4 * own_rows].reshape(wide_size, 4, own_rows).transpose(1, 0, 2).reshape(4, D)
    bias_in_all = small_all[:, 4 * own_rows : 4 * own_rows + ffn_rows].reshape(wide_size, tiles, unit)
    bias_in_all = bias_in_all.transpose(1, 0, 2).reshape(tiles, 1, width)
    bias_out_all = small_all[:, 4 * own_rows + ffn_rows :].reshape(1, D)
    vectors = jnp.concatenate([norm_all, bias_out_all, jnp.zeros((3, D), jnp.float32)])

    def four_copies(piece, outs, half, w, n):
        return [(piece, outs[0].at[n, pl.ds(w * own_rows + half * split, split)])]

    def ffn_copies(piece, outs, half, w, n):
        if half == 0:
            return [(piece, outs[0].at[:, pl.ds(w * own_rows, own_rows), pl.ds(n * in_part, in_part)])]
        rows = pl.ds(w * unit + n * back_part, back_part)
        return [
            (piece.at[:, pl.ds(k * back_part, back_part)], outs[1].at[:, rows, pl.ds(k * in_part, in_part)])
            for k in range(folds)
        ]

    def ffn_weights(gather):
        parts = gather.mine + gather.theirs
        count = parts[0].shape[2]
        if copied:
            return place(me, parts, ffn_copies, [(count, D, width), (count, width, D)], folds, "place_ffn")
        w_in = half_in_order(parts, 0).transpose(2, 0, 3, 1, 4).reshape(count, D, width)
        w_back = half_in_order(parts, 1).reshape(wide_size, narrow_size, count, folds, back_part, in_part)
        return w_in, w_back.transpose(2, 0, 1, 4, 3, 5).reshape(count, width, D)

    if copied:
        (weights,) = place(me, four_parts, four_copies, [(4, D, D)], 1, "place_four")
    else:
        weights = jnp.stack([half_in_order(four_parts, half) for half in range(2)], axis=2)
        weights = weights.transpose(0, 2, 3, 1, 4).reshape(D, 4, D).transpose(1, 0, 2)

    cosine, sine = rotary_blocks(length)
    proj, projt = projection_blocks(feature_proj)
    found = attend(lengths, block_in, weights, vectors, proj, cosine, sine, None, ready)
    half_done = found[0]
    early = list(ffn_gathers[0].core())
    for gather in ffn_gathers[1:]:
        early += gather.near(*ready)
    found = attend(lengths, block_in, weights, vectors, proj, cosine, sine, found, early)
    middle, h1, h2, *kept, mixed = found
    tile_weights = [ffn_weights(ffn_gathers[0])]
    later = []
    for gather in ffn_gathers[1:]:
        later += gather.far(half_done)
        gather.core()
        tile_weights.append(ffn_weights(gather))
    past, token = None, later
    streams, bias_sums = [], []
    orders = ["yzx", "yxz", "xya"]
    for tile in range(tiles):
        ffn, grad_h2, bias_sum, *grad_tile = ffn_tile(
            max(tile - 1, 0), h2, out_grad, *tile_weights[min(tile, 1)], bias_in_all[tile : tile + 1], me, past, wide_size, narrow_size, blocks, token
        )
        past = (ffn, grad_h2)
        bias_sums.append(bias_sum)
        token = [fold_streams(streams[:1], me, [bias_sum])] if tile == 1 else []
        if blocks:
            keep, *send = grad_tile
            streams.append(Stream(keep, core_swap(send), orders[tile % 3]))
        else:
            grad_in = grad_tile[0][0].reshape(wide_size, own_rows, narrow_size, in_part).transpose(2, 0, 1, 3)
            grad_back = grad_tile[0][1].reshape(narrow_size, own_cols, wide_size, unit).transpose(0, 2, 1, 3)
            for found, order in ((grad_in, "yxz"), (grad_back, "xyz")):
                found = found.reshape((narrow_size // 2, 2) + found.shape[1:])
                arrived = core_swap(cut_wide(pick(found, 1 - (column & 1), 1)))
                streams.append(Stream(pick(found, column & 1, 1), arrived, order))
    ffn = tie(ffn, *streams[0].parts[1:])
    block_out, grad_middle, gb, sums_two = middle_back(out_grad, grad_h2, ffn, middle, vectors, narrow_size)

    def fold_open(more, after):
        found = more + [stream for stream in streams if stream.order]
        done = [part for stream in streams if not stream.order for part in stream.parts]
        return fold_streams(found, me, after + done)

    token = fold_open([], [sums_two])
    gq, gk, gv = attend_back(lengths, grad_middle, weights, projt, cosine, sine, kept, narrow_size, [token])
    token = fold_open([], [gq])
    send = attn_weights(me, h1, mixed, (gq, gk, gv, gb), wide_size, 1, [token])
    (keep,) = attn_weights(me, h1, mixed, (gq, gk, gv, gb), wide_size, 0, send[:1])
    arrived = core_swap(send)
    left = Stream(keep, arrived, "xzy", (0, own_rows))
    right = Stream(keep, arrived, "yxz", (own_rows, 2 * own_rows))
    token = fold_open([left, right], [keep])
    input_grad, sums_one = input_back(block_in, grad_middle, (gq, gk, gv), weights, vectors, [token])

    norm_sums = jnp.concatenate([sums_one[:2], sums_two[:2], sums_two[2:3]])
    inner_sums = jnp.concatenate(bias_sums).reshape(tiles, wide_size, unit).transpose(1, 0, 2)
    inner_sums = inner_sums.reshape(wide_size, narrow_size, ffn_rows // narrow_size)
    norm_part = own_rows // narrow_size
    norm_sums = norm_sums.reshape(5, wide_size, narrow_size, norm_part).transpose(1, 2, 0, 3).reshape(wide_size, narrow_size, -1)
    vector_parts = jnp.concatenate([norm_sums, inner_sums], axis=2).swapaxes(0, 1)
    vector_size = vector_parts.shape[2]
    vector_parts = jnp.pad(vector_parts, ((0, 0), (0, 0), (0, -vector_size % 128)))
    vector_parts = vector_parts.reshape(narrow_size // 2, 2, wide_size, 1, -1)
    vector_send = pick(vector_parts, 1 - (column & 1), 1)
    vector = Stream(pick(vector_parts, column & 1, 1), core_swap([vector_send]), "yxz")
    token = fold_open([left, right, vector], [sums_one])
    ffn_parts = [stream.last() for stream in streams]
    block_size = 128 if ffn_rows % 128 == 0 else ffn_rows
    block_count = len(block_pairs(ffn_rows // block_size)) + 1
    grad_in_w, grad_back_w, mom_in_new, mom_back_new, blocks_gram = simple_call(
        partial(ffn_moment_kernel, [len(parts) for parts in ffn_parts], unit),
        [mom_ffn_in, mom_ffn_out] + sum(ffn_parts, []),
        [mom_ffn_in.shape, mom_ffn_out.shape] * 2 + [(block_count, block_size, block_size)],
        "ffn_moment",
        1e9,
        [token],
    )
    blocks_gram = narrow_sum(blocks_gram)
    token = fold_streams([left, right, vector], me, [mom_in_new])
    sweep_in, sweep_back, factor_in, factor_back = simple_call(
        partial(sweep_kernel, 2, own_rows),
        [blocks_gram],
        [(own_rows, own_rows), (ffn_rows, ffn_rows)] * 2,
        "ffn_sweeps",
        1e10,
        [token],
    )
    left_parts, right_parts = left.last(), right.last()
    def own_columns(weight):
        block_width = weight.shape[-1] // narrow_size
        return lax.dynamic_slice_in_dim(
            weight, column * block_width, block_width, axis=weight.ndim - 1
        )

    rate_qkv = MUON_SCALE
    rate_out = MUON_SCALE * math.sqrt(D / (D // 64))
    rate_in = MUON_SCALE * math.sqrt(FF / D)
    rate_back = MUON_SCALE * math.sqrt(D / FF)
    shapes = [mom_attn_in.shape, mom_attn_out.shape]
    grad_qkv, grad_out_w, mom_qkv_new, mom_out_new, gram_four = simple_call(
        partial(attn_moment_kernel, (len(left_parts), len(right_parts))),
        [mom_attn_in, mom_attn_out] + left_parts + right_parts,
        shapes + shapes + [(4, own_rows, own_rows)],
        "attn_moment",
        1e9,
        [sweep_in],
    )
    fold_streams([vector], me, [gram_four])
    vector_sums = sum(jnp.sum(part, axis=0) for part in vector.last())[0, :vector_size]
    grad_norm_vals = vector_sums[: 4 * norm_part].reshape(4, norm_part)
    grad_bias_final = vector_sums[4 * norm_part : 5 * norm_part]
    grad_bias_inner = vector_sums[5 * norm_part :]
    new_in, new_back = simple_call(
        partial(ffn_ortho_kernel, (rate_in, rate_back), NS_ITERS - 2),
        [sweep_in, sweep_back, factor_in, factor_back, mom_in_new, mom_back_new, own_columns(ffn_in), own_columns(ffn_out)],
        [mom_ffn_in.shape, mom_ffn_out.shape],
        "ffn_ortho",
        1e10,
        [gram_four],
    )
    new_qkv, new_out = simple_call(
        partial(attn_ortho_kernel, (rate_qkv, rate_out)),
        [narrow_sum(gram_four), mom_qkv_new, mom_out_new, own_columns(attn_in), own_columns(attn_out)],
        shapes,
        "attn_ortho",
        5e9,
        [new_in],
    )
    norm_first, norm_second, norm_new = adam_update(
        own_columns(norm_params), first_norms, second_norms, grad_norm_vals
    )
    inner_first, inner_second, inner_new = adam_update(
        own_columns(bias_in), first_bias_in, second_bias_in, grad_bias_inner
    )
    final_first, final_second, final_new = adam_update(
        own_columns(bias_out), first_bias_out, second_bias_out, grad_bias_final
    )
    return (
        block_out,
        input_grad,
        grad_qkv,
        grad_out_w,
        grad_in_w,
        grad_back_w,
        grad_norm_vals,
        grad_bias_inner,
        grad_bias_final,
        mom_qkv_new,
        mom_out_new,
        mom_in_new,
        mom_back_new,
        new_qkv,
        new_out,
        new_in,
        new_back,
        norm_first,
        inner_first,
        final_first,
        norm_second[:2],
        norm_second[2:],
        inner_second,
        final_second,
        norm_new,
        inner_new,
        final_new,
    )


def solution(mesh):
    in_specs = (
        P(("wide", "narrow"), None, None),
        P(("wide", "narrow"), None, None),
        P(("wide", "narrow")),
        P(),
        P(None, "wide", None),
        P("wide", None),
        P("wide", None),
        P("wide", None),
        P(None, "wide"),
        P("wide"),
        P("wide"),
        P(None, "wide", "narrow"),
        P("wide", "narrow"),
        P("wide", "narrow"),
        P("wide", "narrow"),
        P(None, ("wide", "narrow")),
        P(("wide", "narrow")),
        P(("wide", "narrow")),
        P(None, ("wide", "narrow")),
        P(("wide", "narrow")),
        P(("wide", "narrow")),
    )
    out_specs = (
        P(("wide", "narrow"), None, None),
        P(("wide", "narrow"), None, None),
        P(None, "wide", "narrow"),
        P("wide", "narrow"),
        P("wide", "narrow"),
        P("wide", "narrow"),
        P(None, ("wide", "narrow")),
        P(("wide", "narrow")),
        P(("wide", "narrow")),
        P(None, "wide", "narrow"),
        P("wide", "narrow"),
        P("wide", "narrow"),
        P("wide", "narrow"),
        P(None, "wide", "narrow"),
        P("wide", "narrow"),
        P("wide", "narrow"),
        P("wide", "narrow"),
        P(None, ("wide", "narrow")),
        P(("wide", "narrow")),
        P(("wide", "narrow")),
        P(None, ("wide", "narrow")),
        P(None, ("wide", "narrow")),
        P(("wide", "narrow")),
        P(("wide", "narrow")),
        P(None, ("wide", "narrow")),
        P(("wide", "narrow")),
        P(("wide", "narrow")),
    )
    return jax.shard_map(
        per_device, mesh=mesh, in_specs=in_specs, out_specs=out_specs, check_vma=False
    )
```

```python
from functools import partial
import math

import jax
import jax.numpy as jnp
from jax import lax
from jax.experimental import pallas as pl
from jax.experimental.pallas import tpu as pltpu
from jax.sharding import PartitionSpec as P

D = 768
FF = 3072
HEADS = 12
HDIM = 64
FEAT = 32
NS_ITERS = 5
ADAM_STEP = 10


PRECISE = lax.Precision.HIGHEST
NORM_EPS = 1e-05
ORTHO_EPS = 1e-07
ADAM_EPS = 1e-08
LINEAR_COEF = 3.4445
CUBIC_COEF = -4.775
QUINTIC_COEF = 2.0315
MOMENT_DECAY = 0.5
FIRST_DECAY = 0.5
SECOND_DECAY = 0.5
MUON_SCALE = 0.6
WEIGHT_DECAY = 0.01
VECTOR_RATE = 0.4
GROUP = 4
GROUPS = HEADS // GROUP
GE = GROUP * HDIM
GF = GROUP * FEAT


def mm(left, right):
    return jnp.dot(left, right, preferred_element_type=jnp.float32)


def mm_nt(left, right):
    return lax.dot_general(left, right, (((1,), (1,)), ((), ())), preferred_element_type=jnp.float32)


def mm_tn(left, right):
    return lax.dot_general(left, right, (((0,), (0,)), ((), ())), preferred_element_type=jnp.float32)


def halves(value):
    high = value.astype(jnp.bfloat16)
    return high, (value - high.astype(jnp.float32)).astype(jnp.bfloat16)


def normalise(rows):
    centered = rows - jnp.mean(rows, axis=-1, keepdims=True)
    inverse = lax.rsqrt(jnp.mean(centered * centered, axis=-1, keepdims=True) + NORM_EPS)
    return centered * inverse, inverse


def norm_pull(normed, inverse, grad, gain):
    scaled = grad * gain
    mean_plain = jnp.mean(scaled, axis=-1, keepdims=True)
    mean_prod = jnp.mean(scaled * normed, axis=-1, keepdims=True)
    return inverse * (scaled - mean_plain - normed * mean_prod)


def partner_of(values):
    lane = lax.broadcasted_iota(jnp.int32, (values.shape[0], 128), 1)
    first = (lane & (HDIM - 1)) < HDIM // 2
    parts = []
    for at in range(0, values.shape[1], 128):
        block = values[:, at : at + 128]
        ahead = pltpu.roll(block, 128 - HDIM // 2, 1)
        behind = pltpu.roll(block, HDIM // 2, 1)
        parts.append(jnp.where(first, ahead, behind))
    return jnp.concatenate(parts, axis=1)


def head_mask(rows, columns, row_width, column_width):
    row = lax.broadcasted_iota(jnp.int32, (rows, columns), 0) // row_width
    column = lax.broadcasted_iota(jnp.int32, (rows, columns), 1) // column_width
    return row == column


def store_columns(ref, values):
    width = ref.shape[3]
    for n in range(ref.shape[0]):
        ref[n, 0] = values[:, width * n : width * (n + 1)].astype(ref.dtype)


def load_columns(ref):
    return jnp.concatenate([ref[n, 0] for n in range(ref.shape[0])], axis=1)


def attend_kernel(
    first, lengths_ref, x_ref, w_ref, vec_ref, proj_ref, cos_ref, sin_ref,
    middle_ref, h1_ref, h2_ref, wq_ref, wk_ref, pq_ref, pk_ref, v_ref, state_ref, total_ref, att_ref, rden_ref, mixed_ref,
):
    rows = x_ref.shape[1]
    x = x_ref[0].astype(jnp.float32)
    h1 = (normalise(x)[0] * vec_ref[0:1, :] + vec_ref[1:2, :]).astype(jnp.bfloat16)
    h1_ref[0] = h1
    live = lax.broadcasted_iota(jnp.int32, (rows, 1), 0) < lengths_ref[pl.program_id(0) + first]
    live = live.astype(jnp.float32)
    cosine = jnp.concatenate([cos_ref[...]] * (D // 128), axis=1)
    sine = jnp.concatenate([sin_ref[...]] * (D // 128), axis=1)
    values = mm(h1, w_ref[2]).astype(jnp.bfloat16)
    v_ref[0] = values
    feats = []
    for j, (w_out, p_out) in enumerate(((wq_ref, pq_ref), (wk_ref, pk_ref))):
        heads = mm(h1, w_ref[j])
        unit = (heads * cosine + partner_of(heads) * sine) * HDIM ** (-0.25)
        w_out[0] = unit
        high, low = halves(unit)
        sq_high, sq_low = halves(unit * unit)
        parts = []
        for g in range(GROUPS):
            cut = slice(GE * g, GE * (g + 1))
            left = jnp.concatenate([high[:, cut], low[:, cut], high[:, cut], sq_high[:, cut], sq_low[:, cut]], axis=1)
            parts.append(jnp.exp(mm(left, proj_ref[g])) * FEAT ** (-0.5))
        phi = jnp.concatenate(parts, axis=1)
        p_out[0] = phi
        feats.append(phi)
    query_low = feats[0].astype(jnp.bfloat16)
    key_vals = feats[1].astype(jnp.bfloat16).astype(jnp.float32) * live
    key_low = key_vals.astype(jnp.bfloat16)
    total_ref[0] = jnp.sum(key_vals, axis=0, keepdims=True)
    mask = head_mask(GF, GE, FEAT, HDIM)
    ones = jnp.ones((rows, GE), jnp.bfloat16)
    attended, inverse_den = [], []
    for g in range(GROUPS):
        cut = slice(GE * g, GE * (g + 1))
        fcut = slice(GF * g, GF * (g + 1))
        both = mm_tn(key_low[:, fcut], jnp.concatenate([values[:, cut], ones], axis=1))
        state = jnp.where(mask, both[:, :GE], 0.0).astype(jnp.bfloat16)
        state_ref[0, g] = state
        tot_high, tot_low = halves(jnp.where(mask, both[:, GE:], 0.0))
        query = query_low[:, fcut]
        numer = mm(query, state)
        denom = mm(jnp.concatenate([query, query], axis=1), jnp.concatenate([tot_high, tot_low], axis=0))
        inverse = 1.0 / denom
        attended.append(numer * inverse)
        inverse_den.append(inverse)
    attended = jnp.concatenate(attended, axis=1)
    att_ref[0] = attended
    rden_ref[0] = jnp.concatenate(inverse_den, axis=1)
    mixed = attended.astype(jnp.bfloat16)
    mixed_ref[0] = mixed
    middle = x + mm(mixed, w_ref[3])
    middle_ref[0] = middle
    h2_ref[0] = (normalise(middle)[0] * vec_ref[2:3, :] + vec_ref[3:4, :]).astype(jnp.bfloat16)


def middle_back_kernel(og_ref, gh2_ref, ffn_ref, middle_ref, vec_ref, out_ref, gm_ref, gb_ref, sums_ref):
    og = og_ref[0].astype(jnp.float32)
    middle = middle_ref[0]
    out_ref[0] = middle + (ffn_ref[0] + vec_ref[4:5, :])
    grad_h2 = gh2_ref[0]
    normed, inverse = normalise(middle)
    grad_middle = og + norm_pull(normed, inverse, grad_h2, vec_ref[2:3, :])
    gm_ref[0] = grad_middle
    store_columns(gb_ref, grad_middle)

    @pl.when(pl.program_id(0) == 0)
    def _():
        sums_ref[...] = jnp.zeros_like(sums_ref)

    sums_ref[0:1, :] += jnp.sum(grad_h2 * normed, axis=0, keepdims=True)
    sums_ref[1:2, :] += jnp.sum(grad_h2, axis=0, keepdims=True)
    sums_ref[2:3, :] += jnp.sum(og, axis=0, keepdims=True)


def attend_back_kernel(
    lengths_ref, gm_ref, w_ref, projt_ref, cos_ref, sin_ref,
    wq_ref, wk_ref, pq_ref, pk_ref, v_ref, state_ref, total_ref, att_ref, rden_ref,
    gq_ref, gk_ref, gv_ref,
):
    rows = gm_ref.shape[1]
    branch = gm_ref[0].astype(jnp.bfloat16)
    grad_numer = mm_nt(branch, w_ref[0]) * rden_ref[0]
    gn_high, gn_low = halves(grad_numer)
    pr_high, pr_low = halves(grad_numer * att_ref[0])
    live = (lax.broadcasted_iota(jnp.int32, (rows, 1), 0) < lengths_ref[pl.program_id(0)]).astype(jnp.float32)
    query_low = pq_ref[0].astype(jnp.bfloat16)
    key_low = (pk_ref[0].astype(jnp.bfloat16).astype(jnp.float32) * live).astype(jnp.bfloat16)
    mask = head_mask(GF, GE, FEAT, HDIM)
    spread = head_mask(GE, GF, HDIM, FEAT).astype(jnp.float32).astype(jnp.bfloat16)
    spread2 = jnp.concatenate([spread, spread], axis=0)
    gather = mask.astype(jnp.float32).astype(jnp.bfloat16)
    gather2 = jnp.concatenate([gather, gather], axis=0)
    grad_u = ([], [])
    grad_v = []
    for g in range(GROUPS):
        cut = slice(GE * g, GE * (g + 1))
        fcut = slice(GF * g, GF * (g + 1))
        query, key, values = query_low[:, fcut], key_low[:, fcut], v_ref[0, :, cut]
        state = state_ref[0, g]
        grad_denom = -mm(jnp.concatenate([pr_high[:, cut], pr_low[:, cut]], axis=1), spread2)
        two = jnp.concatenate([gn_high[:, cut], gn_low[:, cut]], axis=1)
        grad_qfeat = mm_nt(two, jnp.concatenate([state, state], axis=1)) + grad_denom * total_ref[0, :, fcut]
        pair = mm_tn(query, two)
        grad_state = jnp.where(mask, pair[:, :GE] + pair[:, GE:], 0.0)
        grad_total = jnp.sum(grad_denom * query.astype(jnp.float32), axis=0, keepdims=True)
        gs_high, gs_low = halves(grad_state)
        grad_kfeat = mm_nt(
            jnp.concatenate([values, values], axis=1), jnp.concatenate([gs_high, gs_low], axis=1)
        )
        grad_kfeat = (grad_kfeat + grad_total) * live
        grad_v.append(mm(jnp.concatenate([key, key], axis=1), jnp.concatenate([gs_high, gs_low], axis=0)))
        for j, (grad_feat, p_in, w_in) in enumerate(((grad_qfeat, pq_ref, wq_ref), (grad_kfeat, pk_ref, wk_ref))):
            t_high, t_low = halves(grad_feat * p_in[0, :, fcut])
            pulled = mm(jnp.concatenate([t_high, t_low, t_high], axis=1), projt_ref[g])
            weight = mm(jnp.concatenate([t_high, t_low], axis=1), gather2)
            grad_u[j].append((pulled - weight * w_in[0, :, cut]) * HDIM ** (-0.25))
    cosine = jnp.concatenate([cos_ref[...]] * (D // 128), axis=1)
    sine = jnp.concatenate([sin_ref[...]] * (D // 128), axis=1)
    for grads, ref in zip(grad_u, (gq_ref, gk_ref)):
        turned = jnp.concatenate(grads, axis=1)
        store_columns(ref, turned * cosine - partner_of(turned) * sine)
    store_columns(gv_ref, jnp.concatenate(grad_v, axis=1))


def input_back_kernel(x_ref, gm_ref, gq_ref, gk_ref, gv_ref, w_ref, vec_ref, out_ref, sums_ref):
    grad_h1 = sum(mm_nt(load_columns(ref), w_ref[j]) for j, ref in enumerate((gq_ref, gk_ref, gv_ref)))
    normed, inverse = normalise(x_ref[0].astype(jnp.float32))
    out_ref[0] = gm_ref[0] + norm_pull(normed, inverse, grad_h1, vec_ref[0:1, :])

    @pl.when(pl.program_id(0) == 0)
    def _():
        sums_ref[...] = jnp.zeros_like(sums_ref)

    sums_ref[0:1, :] += jnp.sum(grad_h1 * normed, axis=0, keepdims=True)
    sums_ref[1:2, :] += jnp.sum(grad_h1, axis=0, keepdims=True)


def attn_weight_kernel(me_ref, h1_ref, mixed_ref, gq_ref, gk_ref, gv_ref, gb_ref, *out_refs):
    width, rows = out_refs[0].shape[1], out_refs[0].shape[2] // 2
    h1 = h1_ref[...]
    left = mm_tn(h1, jnp.concatenate([gq_ref[...], gk_ref[...]], axis=1)).astype(jnp.bfloat16)
    right = jnp.concatenate([mm_tn(h1, gv_ref[...]), mm_tn(mixed_ref[...], gb_ref[...])], axis=1).astype(jnp.bfloat16)
    for w in range(width * len(out_refs)):
        out_refs[w // width][0, w % width, :rows] = left[rows * w : rows * (w + 1)]
        out_refs[w // width][0, w % width, rows:] = right[rows * w : rows * (w + 1)]


def ffn_kernel(has_past, blocks, h2_ref, og_ref, win_ref, wback_ref, bias_ref, me_ref, *rest):
    if has_past:
        out_past_ref, gh2_past_ref, *rest = rest
    if blocks:
        out_ref, gh2_ref, bsum_ref, keep_ref, *send_refs, act_ref, gi_ref, gw_ref = rest
    else:
        out_ref, gh2_ref, bsum_ref, gw_ref, act_ref, gi_ref = rest
    seqs, rows = out_ref.shape[0], out_ref.shape[1]
    step = pl.program_id(0)
    win, wback = win_ref[...], wback_ref[...]
    bias = bias_ref[...]

    def part(s, carry):
        span = pl.ds(pl.multiple_of(s * rows, rows), rows)
        inner = mm(h2_ref[s], win) + bias
        grad_act = mm_nt(og_ref[s], wback)
        cdf = 0.5 * (1.0 + lax.erf(inner * (2.0**-0.5)))
        pdf = jnp.exp(-0.5 * inner * inner) * (2.0 * math.pi) ** -0.5
        act = (inner * cdf).astype(jnp.bfloat16)
        grad_inner = (grad_act * (cdf + inner * pdf)).astype(jnp.bfloat16)
        act_ref[span, :] = act
        gi_ref[span, :] = grad_inner
        out_part = mm(act, wback)
        gh2_part = mm_nt(grad_inner, win)

        @pl.when(step == 0)
        def _():
            if has_past:
                out_ref[s] = out_past_ref[s] + out_part
                gh2_ref[s] = gh2_past_ref[s] + gh2_part
            else:
                out_ref[s] = out_part
                gh2_ref[s] = gh2_part

        @pl.when(step > 0)
        def _():
            out_ref[s] += out_part
            gh2_ref[s] += gh2_part

        return carry + jnp.sum(grad_inner.astype(jnp.float32), axis=0, keepdims=True)

    bsum_ref[...] = lax.fori_loop(0, seqs, part, jnp.zeros(bias.shape, jnp.float32), unroll=True)
    h2 = h2_ref[...].reshape(seqs * rows, D)
    og = og_ref[...].reshape(seqs * rows, D)
    grad_in = mm_tn(h2, gi_ref[...]).astype(jnp.bfloat16)
    grad_back = mm_tn(og, act_ref[...]).astype(jnp.bfloat16)
    if not blocks:
        gw_ref[0] = grad_in
        gw_ref[1] = grad_back
        return
    narrow, wide = gw_ref.shape[0], gw_ref.shape[1]
    in_rows, in_cols = D // wide, gw_ref.shape[3]
    width = grad_in.shape[1]
    for k in range(width // in_cols):
        for w in range(wide):
            gw_ref[step * (width // in_cols) + k, w, :in_rows, :] = grad_in[
                in_rows * w : in_rows * (w + 1), in_cols * k : in_cols * (k + 1)
            ]
    back_rows = D // narrow
    half = back_rows // 2
    for k in range(width // 128):
        for n in range(narrow):
            for h in range(2):
                gw_ref[n, step * (width // 128) + k, in_rows:, 128 * h : 128 * (h + 1)] = grad_back[
                    back_rows * n + half * h : back_rows * n + half * (h + 1), 128 * k : 128 * (k + 1)
                ]

    @pl.when(step == pl.num_programs(0) - 1)
    def _():
        side = me_ref[1] & 1
        for far in range(narrow // 2):
            for w in range(wide):
                keep_ref[far, w] = gw_ref[2 * far + side, w]
                width = wide // len(send_refs)
                send_refs[w // width][far, w % width] = gw_ref[2 * far + (1 - side), w]


def spec(shape, index):
    return pl.BlockSpec(shape, index)


LIMIT = 60 * 1024 * 1024
ANYWHERE = pl.BlockSpec(memory_space=pl.ANY)


def skipping(kernel, before, extra):
    def run(*refs):
        return kernel(*refs[:before], *refs[before + extra :])

    return run


def estimate(flops, moved, transcendentals=0):
    return pl.CostEstimate(flops=int(flops), bytes_accessed=int(moved), transcendentals=int(transcendentals))


def whole(array):
    rank = array.ndim
    return pl.BlockSpec(array.shape, lambda *unused: (0,) * rank)


def by_seq(shape):
    rank = len(shape)
    return pl.BlockSpec((1,) + tuple(shape[1:]), lambda s, *unused: (s,) + (0,) * (rank - 1))


def by_seq_second(shape):
    rank = len(shape)
    return pl.BlockSpec((shape[0], 1) + tuple(shape[2:]), lambda s, *unused: (0, s) + (0,) * (rank - 2))


def attend(lengths, x, weights, vectors, proj, cosine, sine, before, after):
    seqs, rows, unused_width = x.shape
    bf, f4 = jnp.bfloat16, jnp.float32
    shapes = [
        ((seqs, rows, D), f4), ((seqs, rows, D), bf), ((seqs, rows, D), bf), ((seqs, rows, D), f4), ((seqs, rows, D), f4),
        ((seqs, rows, HEADS * FEAT), f4), ((seqs, rows, HEADS * FEAT), f4), ((seqs, rows, D), bf),
        ((seqs, GROUPS, GF, GE), bf), ((seqs, 1, HEADS * FEAT), f4), ((seqs, rows, D), f4), ((seqs, rows, D), f4),
        ((seqs, rows, D), bf),
    ]
    half = seqs // 2
    first = 0 if before is None else half
    before = list(before or [])

    def part(shape):
        rank = len(shape)
        return pl.BlockSpec((1,) + tuple(shape[1:]), lambda s, *unused: (s + first,) + (0,) * (rank - 1))

    return pl.pallas_call(
        skipping(partial(attend_kernel, first), 7, len(after) + len(before)),
        grid_spec=pltpu.PrefetchScalarGridSpec(
            num_scalar_prefetch=1,
            grid=(half if first == 0 else seqs - half,),
            in_specs=[part(x.shape)] + [whole(a) for a in (weights, vectors, proj, cosine, sine)]
            + [ANYWHERE] * (len(after) + len(before)),
            out_specs=[part(shape) for shape, unused in shapes],
        ),
        out_shape=[jax.ShapeDtypeStruct(shape, dtype) for shape, dtype in shapes],
        input_output_aliases={7 + len(after) + k: k for k in range(len(before))},
        compiler_params=pltpu.CompilerParams(vmem_limit_bytes=LIMIT),
        cost_estimate=estimate(seqs * rows * D * D * 6, 20e6),
        name="attend",
    )(lengths, x, weights, vectors, proj, cosine, sine, *after, *before)


def middle_back(og, grad_h2, ffn, middle, vectors, narrow_size):
    seqs, rows, unused_width = og.shape
    blocked = (narrow_size, seqs, rows, D // narrow_size)
    full = jax.ShapeDtypeStruct(og.shape, jnp.float32)
    return pl.pallas_call(
        middle_back_kernel,
        grid=(seqs,),
        in_specs=[by_seq(og.shape)] * 4 + [whole(vectors)],
        out_specs=[by_seq(og.shape)] * 2 + [by_seq_second(blocked), pl.BlockSpec((8, D), lambda s: (0, 0))],
        out_shape=[full, full, jax.ShapeDtypeStruct(blocked, jnp.bfloat16), jax.ShapeDtypeStruct((8, D), jnp.float32)],
        compiler_params=pltpu.CompilerParams(vmem_limit_bytes=LIMIT),
        cost_estimate=estimate(1e7, 16e6),
        name="middle_back",
    )(og, grad_h2, ffn, middle, vectors)


def attend_back(lengths, grad_middle, weights, projt, cosine, sine, kept, narrow_size, after):
    seqs, rows, unused_width = grad_middle.shape
    blocked = (narrow_size, seqs, rows, D // narrow_size)
    count = 6 + len(kept)
    return pl.pallas_call(
        skipping(attend_back_kernel, count, len(after)),
        grid_spec=pltpu.PrefetchScalarGridSpec(
            num_scalar_prefetch=1,
            grid=(seqs,),
            in_specs=[by_seq(grad_middle.shape), pl.BlockSpec((1, D, D), lambda s, *unused: (3, 0, 0))]
            + [whole(a) for a in (projt, cosine, sine)]
            + [by_seq(a.shape) for a in kept]
            + [ANYWHERE] * len(after),
            out_specs=[by_seq_second(blocked)] * 3,
        ),
        out_shape=[jax.ShapeDtypeStruct(blocked, jnp.bfloat16)] * 3,
        compiler_params=pltpu.CompilerParams(vmem_limit_bytes=LIMIT),
        cost_estimate=estimate(seqs * rows * D * D * 8, 40e6),
        name="attend_back",
    )(lengths, grad_middle, weights, projt, cosine, sine, *kept, *after)


def input_back(x, grad_middle, grads, weights, vectors, after):
    seqs, rows, unused_width = x.shape
    return pl.pallas_call(
        skipping(input_back_kernel, 4 + len(grads), len(after)),
        grid=(seqs,),
        in_specs=[by_seq(x.shape), by_seq(x.shape)] + [by_seq_second(a.shape) for a in grads] + [whole(weights), whole(vectors)] + [ANYWHERE] * len(after),
        out_specs=[by_seq(x.shape), pl.BlockSpec((8, D), lambda s: (0, 0))],
        out_shape=[jax.ShapeDtypeStruct(x.shape, jnp.float32), jax.ShapeDtypeStruct((8, D), jnp.float32)],
        compiler_params=pltpu.CompilerParams(vmem_limit_bytes=LIMIT),
        cost_estimate=estimate(seqs * rows * D * D * 6, 15e6),
        name="input_back",
    )(x, grad_middle, *grads, weights, vectors, *after)


def attn_weights(me, h1, mixed, grads, wide_size, side, after):
    narrow_size, seqs, rows, width = grads[0].shape
    tokens = seqs * rows
    flat = [a.reshape(narrow_size, tokens, width) for a in grads]
    h1, mixed = h1.reshape(tokens, D), mixed.reshape(tokens, D)
    count = min(4, wide_size // 2) if side else 1
    shape = (narrow_size // 2, wide_size // count, 2 * D // wide_size, 2 * width)

    def block_at(i, me_ref):
        return (2 * i + ((me_ref[1] & 1) ^ side), 0, 0)

    return pl.pallas_call(
        skipping(attn_weight_kernel, 7, len(after)),
        grid_spec=pltpu.PrefetchScalarGridSpec(
            num_scalar_prefetch=1,
            grid=(narrow_size // 2,),
            in_specs=[whole(h1), whole(mixed)] + [pl.BlockSpec((None, tokens, width), block_at)] * 4 + [ANYWHERE] * len(after),
            out_specs=[pl.BlockSpec((1,) + shape[1:], lambda i, *unused: (i, 0, 0, 0))] * count,
        ),
        out_shape=[jax.ShapeDtypeStruct(shape, jnp.bfloat16)] * count,
        compiler_params=pltpu.CompilerParams(vmem_limit_bytes=LIMIT),
        cost_estimate=estimate(tokens * D * D * 4, 8e6),
        name="attn_weights",
    )(me, h1, mixed, *flat, *after)


def ffn_tile(tile, h2, og, w_in, w_back, bias, me, past, wide_size, narrow_size, blocks, after):
    seqs, rows, unused_width = h2.shape
    width = w_in.shape[2]
    step = 1024 if width % 1024 == 0 else width
    tokens = jax.ShapeDtypeStruct(h2.shape, jnp.float32)
    out_specs = [whole(h2), whole(h2), pl.BlockSpec((1, step), lambda i: (0, i))]
    out_shape = [tokens, tokens, jax.ShapeDtypeStruct((1, width), jnp.float32)]
    scratch = [pltpu.VMEM((seqs * rows, step), jnp.bfloat16)] * 2
    if blocks:
        block = (2 * D // wide_size, width // narrow_size)
        half = jax.ShapeDtypeStruct((narrow_size // 2, wide_size) + block, jnp.bfloat16)
        part = jax.ShapeDtypeStruct((narrow_size // 2, wide_size // 4) + block, jnp.bfloat16)
        out_specs += [whole(half)] + [whole(part)] * 4
        out_shape += [half] + [part] * 4
        scratch.append(pltpu.VMEM((narrow_size, wide_size) + block, jnp.bfloat16))
    else:
        out_specs.append(pl.BlockSpec((2, D, step), lambda i: (0, 0, i)))
        out_shape.append(jax.ShapeDtypeStruct((2, D, width), jnp.bfloat16))
    return pl.pallas_call(
        skipping(partial(ffn_kernel, past is not None, blocks), 6 + len(past or ()), len(after)),
        grid=(width // step,),
        in_specs=[
            whole(h2),
            whole(og),
            pl.BlockSpec((None, D, step), lambda i: (tile, 0, i)),
            pl.BlockSpec((None, step, D), lambda i: (tile, i, 0)),
            pl.BlockSpec((None, 1, step), lambda i: (0, 0, i)),
            pl.BlockSpec(memory_space=pltpu.SMEM),
        ]
        + [whole(a) for a in past or ()]
        + [ANYWHERE] * len(after),
        out_specs=out_specs,
        out_shape=out_shape,
        scratch_shapes=scratch,
        compiler_params=pltpu.CompilerParams(vmem_limit_bytes=LIMIT),
        cost_estimate=estimate(seqs * rows * D * width * 12, 20e6, seqs * rows * width * 2),
        name="ffn_tile",
    )(h2, og, w_in, w_back, bias, me, *(past or ()), *after)


def rotary_blocks(length):
    half = HDIM // 2
    frequency = jnp.exp(jnp.arange(half, dtype=jnp.float32) * (-2.0 * math.log(10000.0) / HDIM))
    angles = jnp.arange(length, dtype=jnp.float32)[:, None] * frequency[None, :]
    cosine, sine = jnp.cos(angles), jnp.sin(angles)
    return jnp.tile(cosine, (1, 4)), jnp.tile(jnp.concatenate([-sine, sine], axis=1), (1, 2))


def projection_blocks(feature_proj):
    rows = jnp.arange(GF)[:, None] // FEAT
    columns = jnp.arange(GE)[None, :] // HDIM
    mask = (rows == columns).astype(jnp.float32)
    tall = jnp.tile(feature_proj.reshape(GROUPS, GF, HDIM), (1, 1, GROUP)) * mask
    high, low = halves(tall)
    square = jnp.broadcast_to(-0.5 * mask, tall.shape).astype(jnp.bfloat16)
    turned = [a.swapaxes(1, 2) for a in (high, high, low, square, square)]
    return jnp.concatenate(turned, axis=1), jnp.concatenate([high, high, low], axis=1)


def xor_pairs(size, mask):
    return [(index, index ^ mask) for index in range(size)]


def tie(value, *earlier):
    return lax.optimization_barrier((value, earlier))[0]


def swap(value, axis_name, mask):
    return lax.ppermute(value, axis_name, xor_pairs(lax.axis_size(axis_name), mask))


def far_masks(axis_name):
    return [2 * m for m in range(1, lax.axis_size(axis_name) // 2)]


class Gather:
    def __init__(self, pieces, cut):
        self.cut = cut
        self.pieces = pieces

    def near(self, *earlier):
        self.pieces = [tie(piece, *earlier) for piece in self.pieces] if earlier else self.pieces
        self.first = jnp.stack([piece[..., : -self.cut, :] for piece in self.pieces])
        self.second = jnp.stack([piece[..., -self.cut :, :] for piece in self.pieces])
        self.first_in = swap(self.first, "wide", 1)
        self.second_in = [swap(self.second, "narrow", mask) for mask in far_masks("narrow")]
        return [self.first_in] + self.second_in

    def far(self, *earlier):
        if earlier:
            self.first_in = tie(self.first_in, *earlier)
        self.first = jnp.stack([self.first, self.first_in])
        self.extra = self.first[..., self.cut :, :]
        self.first = self.first[..., : self.cut, :]
        self.second = jnp.stack([self.second] + (list(tie(tuple(self.second_in), *earlier)) if earlier else self.second_in))
        self.first_in = [swap(self.first, "narrow", mask) for mask in far_masks("narrow")]
        self.second_in = swap(self.second, "wide", 1)
        return self.first_in + [self.second_in]

    def core(self, *earlier):
        if earlier:
            late = tie((tuple(self.first_in), self.second_in), *earlier)
            self.first_in, self.second_in = list(late[0]), late[1]
        self.mine = [self.first] + self.first_in + [self.second, self.second_in]
        self.theirs = [swap(part, "narrow", 1) for part in self.mine]
        return self.theirs


def far_wide(piece):
    return [piece] + [swap(piece, "wide", mask) for mask in far_masks("wide")]


def gathered_at(part, index, side, fars, ms):
    m, index = index % ms, index // ms
    half, near, far = (0, index, part) if part < fars else (1, part - fars, index)
    return half, 2 * m + near, 2 * far + side


def place_kernel(copies, fars, ms, me_ref, *rest):
    count = 2 * (fars + 2)
    refs, outs, sems = rest[:count], rest[count:-1], rest[-1]
    started = []
    for k, ref in enumerate(refs):
        side, part = divmod(k, count // 2)
        for index in range(ref.shape[0] * ms):
            half, wide_mask, narrow_mask = gathered_at(part, index, side, fars, ms)
            wide, narrow = me_ref[0] ^ wide_mask, me_ref[1] ^ narrow_mask
            for source, target in copies(ref.at[index // ms, index % ms], outs, half, wide, narrow):
                copy = pltpu.make_async_copy(source, target, sems.at[len(started)])
                copy.start()
                started.append(copy)
    for copy in started:
        copy.wait()


def place(me, parts, copies, shapes, each, name):
    fars, ms = lax.axis_size("narrow") // 2, lax.axis_size("wide") // 2
    return pl.pallas_call(
        partial(place_kernel, copies, fars, ms),
        out_shape=[jax.ShapeDtypeStruct(shape, parts[0].dtype) for shape in shapes],
        in_specs=[pl.BlockSpec(memory_space=pltpu.SMEM)] + [ANYWHERE] * len(parts),
        out_specs=[pl.BlockSpec(memory_space=pltpu.VMEM)] * len(shapes),
        compiler_params=pltpu.CompilerParams(vmem_limit_bytes=LIMIT),
        scratch_shapes=[pltpu.SemaphoreType.DMA((4 * fars * ms * (1 + each),))],
        cost_estimate=estimate(0, 4 * sum(math.prod(shape) for shape in shapes)),
        name=name,
    )(me, *parts)


def in_order(parts, wide_size, narrow_size, place_of):
    my_wide, my_narrow = lax.axis_index("wide"), lax.axis_index("narrow")
    ordered = [
        pick(parts, place_of(w ^ my_wide, n ^ my_narrow), 0) for w in range(wide_size) for n in range(narrow_size)
    ]
    return jnp.stack(ordered).reshape((wide_size, narrow_size) + parts.shape[1:])


def half_in_order(parts, half):
    wide_size, narrow_size = lax.axis_size("wide"), lax.axis_size("narrow")
    fars, ms = narrow_size // 2, wide_size // 2

    def place_of(wide_mask, narrow_mask):
        near, m, side, far = wide_mask & 1, wide_mask >> 1, narrow_mask & 1, narrow_mask >> 1
        outer = far * 2 + near if half == 0 else near * fars + far
        return side * (fars * 2 * ms) + outer * ms + m

    count = len(parts) // 2
    found = []
    for side in range(2):
        own = parts[side * count : (side + 1) * count]
        found += own[:fars] if half == 0 else own[fars:]
    found = [part.reshape((-1,) + part.shape[2:]) for part in found]
    return in_order(jnp.concatenate(found), wide_size, narrow_size, place_of)


def pick(value, index, axis):
    return lax.dynamic_index_in_dim(value, index, axis, keepdims=False)


def core_swap(send):
    return [swap(part, "narrow", 1) for part in send]


def cut_wide(send):
    count = min(4, send.shape[1] // 2)
    width = send.shape[1] // count
    return [lax.slice_in_dim(send, width * k, width * (k + 1), axis=1) for k in range(count)]


class Stream:
    def __init__(self, keep, arrived, order, window=None):
        rest = keep.shape[2:]
        self.quarters, self.wide = len(arrived), keep.shape[1]
        self.window = window or (0, rest[0])
        self.rest = (self.window[1] - self.window[0],) + rest[1:]
        self.order = list(order)
        self.dims = {"y": keep.shape[0], "z": keep.shape[1] // 2, "x": 2}
        self.parts = [part.reshape((1, -1) + rest) for part in [keep] + arrived]

    def plan(self):
        by_all = self.order[0] == "a"
        axis = "z" if by_all else self.order[0]
        names = [name for name in ("y", "z", "x") if name in self.dims]
        sizes = [self.dims[name] for name in names]
        cut = names.index(axis)
        stride = math.prod(sizes[cut + 1 :])
        places = [
            outer * sizes[cut] * stride + inner for outer in range(math.prod(sizes[:cut])) for inner in range(stride)
        ]
        return by_all, axis, sizes[cut], stride, places

    def outputs(self):
        by_all, unused_axis, size, unused_stride, places = self.plan()
        shape = (len(places),) + self.rest
        return [(size,) + shape] if by_all else [(1,) + shape] * size

    def sent(self, pieces):
        axis = self.order.pop(0)
        self.quarters = 0
        del self.dims["z" if axis == "a" else axis]
        self.window = (0, self.rest[0])
        if axis == "a":
            groups = [list(range(near, lax.axis_size("wide"), 2)) for near in range(2)]
            self.parts = [lax.all_to_all(pieces[0], "wide", 0, 0, axis_index_groups=groups)]
        else:
            name, scale = ("narrow", 2) if axis == "y" else ("wide", 1 if axis == "x" else 2)
            self.parts = [pieces[0]] + [swap(piece, name, scale * m) for m, piece in enumerate(pieces) if m]

    def last(self):
        return [part.reshape((-1,) + self.rest) for part in self.parts]


def fold_kernel(plans, counts, windows, quarters, me_ref, *refs):
    for (by_all, axis, size, stride, places), count, (low, high), parts in zip(plans, counts, windows, quarters):
        ins, refs = take(refs, count)
        outs, refs = take(refs, 1 if by_all else size)
        here = me_ref[1] >> 1 if axis == "y" else me_ref[0] & 1 if axis == "x" else me_ref[0] >> 1
        for step in range(size):
            at = step * stride if by_all else (here ^ step) * stride
            for k, base in enumerate(places):
                found = [(ref, source, base + at) for ref in (ins[:1] if parts else ins) for source in range(ref.shape[0])]
                if parts:
                    wide = parts[1]
                    width = wide // parts[0]
                    far, left = (here ^ step, base) if axis == "y" else (base // wide, base % wide)
                    inner = left % width if axis == "y" else left % width + at
                    found.append((ins[1 + left // width], 0, far * width + inner))
                total = sum(ref[source, place, low:high].astype(jnp.float32) for ref, source, place in found)
                out = outs[0].at[step, k] if by_all else outs[step].at[0, k]
                out[...] = total.astype(out.dtype)


def interleaved(kernel, before, extra, out_counts, counts):
    def run(*refs):
        ins, outs = refs[1:before], refs[before + extra :]
        turn = []
        for out_count, count in zip(out_counts, counts):
            part, ins = take(ins, count)
            turn += part
            part, outs = take(outs, out_count)
            turn += part
        return kernel(refs[0], *turn)

    return run


def fold_streams(streams, me, after):
    plans = [stream.plan() for stream in streams]
    counts = [len(stream.parts) for stream in streams]
    windows = [stream.window for stream in streams]
    out_shapes = [
        [jax.ShapeDtypeStruct(shape, stream.parts[0].dtype) for shape in stream.outputs()] for stream in streams
    ]
    operands = sum((stream.parts for stream in streams), [])
    quarters = [(stream.quarters, stream.wide) if stream.quarters else None for stream in streams]
    kernel = partial(fold_kernel, plans, counts, windows, quarters)
    found = pl.pallas_call(
        interleaved(kernel, 1 + len(operands), len(after), [len(shapes) for shapes in out_shapes], counts),
        in_specs=[pl.BlockSpec(memory_space=pltpu.SMEM)] + [whole_plain(a) for a in operands] + [ANYWHERE] * len(after),
        out_shape=sum(out_shapes, []),
        compiler_params=pltpu.CompilerParams(vmem_limit_bytes=LIMIT),
        cost_estimate=estimate(1e6, 6e6),
        name="fold",
    )(me, *operands, *after)
    token = found[0]
    for stream, shapes in zip(streams, out_shapes):
        part, found = take(found, len(shapes))
        stream.sent(part)
    return token


def narrow_sum(value):
    mask = 1
    while mask < lax.axis_size("narrow"):
        value = value + swap(value, "narrow", mask)
        mask *= 2
    return value


def exact(left, right, dims=(((1,), (0,)), ((), ()))):
    return lax.dot_general(left, right, dims, precision=PRECISE, preferred_element_type=jnp.float32)


def close(left, right):
    left_high, left_low = halves(left)
    right_high, right_low = halves(right)
    return mm(
        jnp.concatenate([left_high, left_low, left_high], axis=1), jnp.concatenate([right_high, right_high, right_low], axis=0)
    )


def diagonal_of(shape):
    return lax.broadcasted_iota(jnp.int32, shape, 0) == lax.broadcasted_iota(jnp.int32, shape, 1)


def ortho_scale(gram_mat):
    square_sum = jnp.where(diagonal_of(gram_mat.shape), gram_mat, 0.0)
    square_sum = jnp.sum(jnp.sum(square_sum, axis=1, keepdims=True), axis=0, keepdims=True)
    return 1.0 / (jnp.sqrt(square_sum) + ORTHO_EPS)


def sweeps(grams, factors, count, last):
    for left in reversed(range(count)):
        polys = [CUBIC_COEF * gram + QUINTIC_COEF * close(gram, gram) for gram in grams]
        polys = [jnp.where(diagonal_of(poly.shape), poly + LINEAR_COEF, poly) for poly in polys]
        if not left and last:
            return grams, [close(poly, factor) for poly, factor in zip(polys, factors)]
        if factors is None:
            factors, halfway = polys, [close(poly, gram) for poly, gram in zip(polys, grams)]
        else:
            both = [
                close(poly, jnp.concatenate([factor, gram], axis=1)) for poly, factor, gram in zip(polys, factors, grams)
            ]
            factors, halfway = zip(*[(pair[:, : pair.shape[0]], pair[:, pair.shape[0] :]) for pair in both])
        grams = [close(poly, half) for poly, half in zip(polys, halfway)]
    return grams, factors


def apply_factor(factor, block):
    rows = block.shape[0]
    if rows % 128 == 0:
        return close(factor, block)
    return exact(factor[:rows, :rows], block)


def ortho_start(grams):
    scales = [ortho_scale(gram) for gram in grams]
    return [gram * scale * scale for gram, scale in zip(grams, scales)], scales


def block_pairs(count):
    return [(row, column) for row in range(count) for column in range(row + 1)]


def padded(size):
    return -(-size // 128) * 128


def store_padded(gram, out_ref):
    out_ref[...] = jnp.zeros(out_ref.shape, jnp.float32)
    out_ref[: gram.shape[0], : gram.shape[1]] = gram


def packed_blocks(small, large, out_ref):
    pairs = block_pairs(padded(large.shape[0]) // 128)
    for k, (row, column) in enumerate(pairs):
        store_padded(large[128 * row : 128 * (row + 1), 128 * column : 128 * (column + 1)], out_ref.at[k])
    store_padded(small, out_ref.at[len(pairs)])


def unpacked_blocks(blocks, count):
    pairs = block_pairs(count)
    found = {}
    for k, (row, column) in enumerate(pairs):
        found[row, column] = blocks[k]
        if row != column:
            found[column, row] = blocks[k].T
    large = [jnp.concatenate([found[row, column] for column in range(count)], axis=1) for row in range(count)]
    return blocks[len(pairs)], jnp.concatenate(large, axis=0)


def sweep_kernel(count, blocks_ref, small_ref, large_ref, small_factor_ref, large_factor_ref):
    grams = unpacked_blocks(blocks_ref[...], large_ref.shape[0] // 128)
    grams, scales = ortho_start(grams)
    grams, factors = sweeps(grams, None, count, False)
    for gram, factor, scale, gram_ref, factor_ref in zip(
        grams, factors, scales, (small_ref, large_ref), (small_factor_ref, large_factor_ref)
    ):
        gram_ref[...] = gram
        factor_ref[...] = factor * scale


def moment_step(gradient, moment_ref, grad_ref, new_ref, at=()):
    grad_ref[at + (slice(None), slice(None))] = gradient
    moment = MOMENT_DECAY * moment_ref[at + (slice(None), slice(None))] + gradient
    new_ref[at + (slice(None), slice(None))] = moment
    return exact(moment, moment, (((1,), (1,)), ((), ())))


def sum_of(refs):
    return sum(ref[k].astype(jnp.float32) for ref in refs for k in range(ref.shape[0]))


def take(refs, count):
    return refs[:count], refs[count:]


def attn_moment_kernel(counts, mqkv_ref, mout_ref, *refs):
    left, refs = take(refs, counts[0])
    right, refs = take(refs, counts[1])
    gqkv_ref, gout_ref, nqkv_ref, nout_ref, gram_ref = refs
    left, right = sum_of(left), sum_of(right)
    width = mout_ref.shape[1]
    store_padded(moment_step(left[:, :width], mqkv_ref, gqkv_ref, nqkv_ref, (0,)), gram_ref.at[0])
    store_padded(moment_step(left[:, width:], mqkv_ref, gqkv_ref, nqkv_ref, (1,)), gram_ref.at[1])
    store_padded(moment_step(right[:, :width], mqkv_ref, gqkv_ref, nqkv_ref, (2,)), gram_ref.at[2])
    store_padded(moment_step(right[:, width:], mout_ref, gout_ref, nout_ref), gram_ref.at[3])


def ffn_moment_kernel(counts, unit, min_ref, mback_ref, *refs):
    found = []
    for count in counts:
        part, refs = take(refs, count)
        found.append(sum_of(part))
    gin_ref, gback_ref, nin_ref, nback_ref, blocks_ref = refs
    rows = min_ref.shape[0]
    if len(found) * 128 == mback_ref.shape[0]:
        grad_in = [part[:rows] for part in found]
        turned = [jnp.concatenate([part[rows:, :128], part[rows:, 128:]], axis=0) for part in found]
        turned = jnp.concatenate(turned, axis=1)
    else:
        grad_in, turned = [found[0]], found[1]
    pieces = [part[:, at : at + unit] for at in range(0, grad_in[0].shape[1], unit) for part in grad_in]
    small = moment_step(jnp.concatenate(pieces, axis=1), min_ref, gin_ref, nin_ref)
    packed_blocks(small, moment_step(turned.T, mback_ref, gback_ref, nback_ref), blocks_ref)


def with_own_columns(me_ref, old, width, use):
    for n in range(old.shape[-1] // width):
        pl.when(me_ref[1] == n)(partial(use, old[..., width * n : width * (n + 1)]))


def attn_ortho_kernel(rates, me_ref, gram_ref, nqkv_ref, nout_ref, wqkv_ref, wout_ref, vqkv_ref, vout_ref):
    grams, scales = ortho_start([gram_ref[j] for j in range(4)])
    factors = sweeps(grams, None, NS_ITERS, True)[1]
    for j in range(4):
        new, old, rate = (nqkv_ref[j], wqkv_ref[j], rates[0]) if j < 3 else (nout_ref[...], wout_ref[...], rates[1])
        ortho = apply_factor(factors[j] * scales[j], new)

        def store(own, j=j, rate=rate, ortho=ortho):
            value = own * (1.0 - rate * WEIGHT_DECAY) - rate * ortho
            if j < 3:
                vqkv_ref[j] = value
            else:
                vout_ref[...] = value

        with_own_columns(me_ref, old, ortho.shape[1], store)


def ffn_ortho_kernel(
    rates, count, me_ref, gin_ref, gback_ref, fin_ref, fback_ref, nin_ref, nback_ref, win_ref, wback_ref, vin_ref, vback_ref
):
    grams, factors = [gin_ref[...], gback_ref[...]], [fin_ref[...], fback_ref[...]]
    factors = sweeps(grams, factors, count, True)[1]
    for rate, factor, new_ref, old_ref, out_ref in (
        (rates[0], factors[0], nin_ref, win_ref, vin_ref),
        (rates[1], factors[1], nback_ref, wback_ref, vback_ref),
    ):
        ortho = apply_factor(factor, new_ref[...])

        def store(own, out_ref=out_ref, rate=rate, ortho=ortho):
            out_ref[...] = own * (1.0 - rate * WEIGHT_DECAY) - rate * ortho

        with_own_columns(me_ref, old_ref[...], ortho.shape[1], store)


def simple_call(kernel, args, shapes, name, flops, after=()):
    def run(*refs):
        kernel(*refs[: len(args)], *refs[len(args) + len(after) :])

    return pl.pallas_call(
        run,
        in_specs=[whole_plain(a) for a in args] + [pl.BlockSpec(memory_space=pl.ANY)] * len(after),
        out_shape=[jax.ShapeDtypeStruct(shape, jnp.float32) for shape in shapes],
        compiler_params=pltpu.CompilerParams(vmem_limit_bytes=LIMIT),
        cost_estimate=estimate(flops, 4e6),
        name=name,
    )(*args, *after)


def whole_plain(array):
    return pl.BlockSpec(memory_space=pltpu.SMEM if array.dtype == jnp.int32 else pltpu.VMEM)


def adam_update(param, earlier_first, earlier_second, gradient):
    first_new = FIRST_DECAY * earlier_first + (1.0 - FIRST_DECAY) * gradient
    second_new = SECOND_DECAY * earlier_second + (1.0 - SECOND_DECAY) * gradient * gradient
    first_fix = 1.0 - FIRST_DECAY**ADAM_STEP
    second_fix = 1.0 - SECOND_DECAY**ADAM_STEP
    direction = first_new / first_fix / (jnp.sqrt(second_new / second_fix) + ADAM_EPS)
    return (first_new, second_new, param - VECTOR_RATE * (direction + WEIGHT_DECAY * param))


def per_device(
    block_in,
    out_grad,
    lengths,
    feature_proj,
    attn_in,
    attn_out,
    ffn_in,
    ffn_out,
    norm_params,
    bias_in,
    bias_out,
    mom_attn_in,
    mom_attn_out,
    mom_ffn_in,
    mom_ffn_out,
    first_norms,
    first_bias_in,
    first_bias_out,
    second_norms,
    second_bias_in,
    second_bias_out,
):
    seqs, length, unused_width = block_in.shape
    wide_size, narrow_size = lax.axis_size("wide"), lax.axis_size("narrow")
    column = lax.axis_index("narrow")
    own_rows, own_cols = D // wide_size, D // narrow_size
    ffn_rows = FF // wide_size
    tiles = ffn_rows // 128 if ffn_rows % 128 == 0 else 1
    unit = ffn_rows // tiles
    width = unit * wide_size
    copied = narrow_size == 4 and own_rows % 16 == 0 and unit % 32 == 0 and (width // narrow_size) % 128 == 0
    blocks = unit == 128 and width // narrow_size == 256 and own_cols == 2 * own_rows
    bf = jnp.bfloat16

    me = jnp.stack([lax.axis_index("wide"), column]).astype(jnp.int32)

    small = jnp.concatenate([norm_params.reshape(-1), bias_in, bias_out]).astype(bf)
    small_size = small.shape[0]
    part = 4 * D // narrow_size
    four = jnp.concatenate([attn_in.astype(bf), attn_out.astype(bf)[None]])
    if part == D:
        four = pick(four, column, 0)
    else:
        four = lax.dynamic_slice_in_dim(four.transpose(1, 0, 2).reshape(own_rows, 4 * D), column * part, part, 1)
    small = jnp.pad(small, (0, -small_size % (8 * part))).reshape(-1, part)
    split = own_rows // 2
    four_gather = Gather(far_wide(jnp.concatenate([four[:split], small, four[split:]])), split)

    in_part = width // narrow_size
    back_part = unit // narrow_size
    folds = D // in_part
    low_in = ffn_in.astype(bf).reshape(own_rows, wide_size, tiles, unit).transpose(2, 0, 1, 3).reshape(tiles, own_rows, width)
    low_in = lax.dynamic_slice_in_dim(low_in, column * in_part, in_part, 2)
    low_back = lax.dynamic_slice_in_dim(ffn_out.reshape(tiles, unit, D), column * back_part, back_part, 1).astype(bf)
    low_back = low_back.reshape(tiles, back_part, folds, in_part).transpose(0, 2, 1, 3).reshape(tiles, own_rows, in_part)
    low_ffn = jnp.concatenate([low_in, low_back], axis=1)
    four_in = four_gather.near()
    ffn_gathers = [Gather(far_wide(tie(low_ffn[:1], *four_gather.pieces[1:])), own_rows)]
    four_far = four_gather.far(*ffn_gathers[0].pieces[1:])
    if tiles > 1:
        ffn_gathers.append(Gather(far_wide(tie(low_ffn[1:], *four_in)), own_rows))
    for gather in ffn_gathers[1:]:
        four_gather.second_in = tie(four_gather.second_in, *gather.pieces[1:])
    four_gather.core()
    ready = ffn_gathers[0].near(*four_far)
    four_parts = four_gather.mine + four_gather.theirs
    ms = wide_size // 2
    small_all = in_order(
        four_gather.extra.reshape((-1,) + small.shape), wide_size, 1, lambda w, n: (w & 1) * ms + (w >> 1)
    )
    small_all = small_all.reshape(wide_size, -1)[:, :small_size].astype(jnp.float32)
    norm_all = small_all[:, : 4 * own_rows].reshape(wide_size, 4, own_rows).transpose(1, 0, 2).reshape(4, D)
    bias_in_all = small_all[:, 4 * own_rows : 4 * own_rows + ffn_rows].reshape(wide_size, tiles, unit)
    bias_in_all = bias_in_all.transpose(1, 0, 2).reshape(tiles, 1, width)
    bias_out_all = small_all[:, 4 * own_rows + ffn_rows :].reshape(1, D)
    vectors = jnp.concatenate([norm_all, bias_out_all, jnp.zeros((3, D), jnp.float32)])

    def four_copies(piece, outs, half, w, n):
        return [(piece, outs[0].at[n, pl.ds(w * own_rows + half * split, split)])]

    def ffn_copies(piece, outs, half, w, n):
        if half == 0:
            return [(piece, outs[0].at[:, pl.ds(w * own_rows, own_rows), pl.ds(n * in_part, in_part)])]
        rows = pl.ds(w * unit + n * back_part, back_part)
        return [
            (piece.at[:, pl.ds(k * back_part, back_part)], outs[1].at[:, rows, pl.ds(k * in_part, in_part)])
            for k in range(folds)
        ]

    def ffn_weights(gather):
        parts = gather.mine + gather.theirs
        count = parts[0].shape[2]
        if copied:
            return place(me, parts, ffn_copies, [(count, D, width), (count, width, D)], folds, "place_ffn")
        w_in = half_in_order(parts, 0).transpose(2, 0, 3, 1, 4).reshape(count, D, width)
        w_back = half_in_order(parts, 1).reshape(wide_size, narrow_size, count, folds, back_part, in_part)
        return w_in, w_back.transpose(2, 0, 1, 4, 3, 5).reshape(count, width, D)

    if copied:
        (weights,) = place(me, four_parts, four_copies, [(4, D, D)], 1, "place_four")
    else:
        weights = jnp.stack([half_in_order(four_parts, half) for half in range(2)], axis=2)
        weights = weights.transpose(0, 2, 3, 1, 4).reshape(D, 4, D).transpose(1, 0, 2)

    cosine, sine = rotary_blocks(length)
    proj, projt = projection_blocks(feature_proj)
    found = attend(lengths, block_in, weights, vectors, proj, cosine, sine, None, ready)
    half_done = found[0]
    early = ffn_gathers[0].far()
    found = attend(lengths, block_in, weights, vectors, proj, cosine, sine, found, early)
    middle, h1, h2, *kept, mixed = found
    ffn_gathers[0].core()
    tile_weights = [ffn_weights(ffn_gathers[0])]
    later = []
    for gather in ffn_gathers[1:]:
        later += gather.near(half_done)
        gather.far(middle)
    past, token = None, later
    streams, bias_sums = [], []
    orders = ["yzx", "yax", "xya"]
    for tile in range(tiles):
        if tile == 1:
            ffn_gathers[1].core(bias_sums[0])
            tile_weights.append(ffn_weights(ffn_gathers[1]))
        ffn, grad_h2, bias_sum, *grad_tile = ffn_tile(
            max(tile - 1, 0), h2, out_grad, *tile_weights[min(tile, 1)], bias_in_all[tile : tile + 1], me, past, wide_size, narrow_size, blocks, token
        )
        past = (ffn, grad_h2)
        bias_sums.append(bias_sum)
        token = [fold_streams(streams[:1], me, [bias_sum])] if tile == 1 else []
        if blocks:
            keep, *send = grad_tile
            streams.append(Stream(keep, core_swap(send), orders[tile % 3]))
        else:
            grad_in = grad_tile[0][0].reshape(wide_size, own_rows, narrow_size, in_part).transpose(2, 0, 1, 3)
            grad_back = grad_tile[0][1].reshape(narrow_size, own_cols, wide_size, unit).transpose(0, 2, 1, 3)
            for found, order in ((grad_in, "yxz"), (grad_back, "xyz")):
                found = found.reshape((narrow_size // 2, 2) + found.shape[1:])
                arrived = core_swap(cut_wide(pick(found, 1 - (column & 1), 1)))
                streams.append(Stream(pick(found, column & 1, 1), arrived, order))
    ffn = tie(ffn, *streams[0].parts[1:])
    block_out, grad_middle, gb, sums_two = middle_back(out_grad, grad_h2, ffn, middle, vectors, narrow_size)

    def fold_open(more, after):
        found = more + [stream for stream in streams if stream.order]
        done = [part for stream in streams if not stream.order for part in stream.parts]
        return fold_streams(found, me, after + done)

    token = fold_open([], [sums_two])
    gq, gk, gv = attend_back(lengths, grad_middle, weights, projt, cosine, sine, kept, narrow_size, [token])
    token = fold_open([], [gq])
    send = attn_weights(me, h1, mixed, (gq, gk, gv, gb), wide_size, 1, [token])
    (keep,) = attn_weights(me, h1, mixed, (gq, gk, gv, gb), wide_size, 0, send[:1])
    arrived = core_swap(send)
    left = Stream(keep, arrived, "xzy", (0, own_rows))
    right = Stream(keep, arrived, "yxz", (own_rows, 2 * own_rows))
    token = fold_open([left, right], [keep])
    input_grad, sums_one = input_back(block_in, grad_middle, (gq, gk, gv), weights, vectors, [token])

    norm_sums = jnp.concatenate([sums_one[:2], sums_two[:2], sums_two[2:3]])
    inner_sums = jnp.concatenate(bias_sums).reshape(tiles, wide_size, unit).transpose(1, 0, 2)
    inner_sums = inner_sums.reshape(wide_size, narrow_size, ffn_rows // narrow_size)
    norm_part = own_rows // narrow_size
    norm_sums = norm_sums.reshape(5, wide_size, narrow_size, norm_part).transpose(1, 2, 0, 3).reshape(wide_size, narrow_size, -1)
    vector_parts = jnp.concatenate([norm_sums, inner_sums], axis=2).swapaxes(0, 1)
    vector_size = vector_parts.shape[2]
    vector_parts = jnp.pad(vector_parts, ((0, 0), (0, 0), (0, -vector_size % 128)))
    vector_parts = vector_parts.reshape(narrow_size // 2, 2, wide_size, 1, -1)
    vector_send = pick(vector_parts, 1 - (column & 1), 1)
    vector = Stream(pick(vector_parts, column & 1, 1), core_swap([vector_send]), "yxz")
    token = fold_open([left, right, vector], [sums_one])
    ffn_parts = [stream.last() for stream in streams]
    small_size, large_size = padded(own_rows), padded(ffn_rows)
    block_count = len(block_pairs(large_size // 128)) + small_size // 128
    grad_in_w, grad_back_w, mom_in_new, mom_back_new, blocks_gram = simple_call(
        partial(ffn_moment_kernel, [len(parts) for parts in ffn_parts], unit),
        [mom_ffn_in, mom_ffn_out] + sum(ffn_parts, []),
        [mom_ffn_in.shape, mom_ffn_out.shape] * 2 + [(block_count, 128, 128)],
        "ffn_moment",
        1e9,
        [token],
    )
    token = fold_streams([left, right, vector], me, [mom_in_new])
    blocks_gram = tie(blocks_gram, token)
    blocks_near = blocks_gram + swap(blocks_gram, "narrow", 1)
    blocks_gram = blocks_near
    for mask in far_masks("narrow"):
        blocks_gram = blocks_gram + swap(blocks_near, "narrow", mask)
    token = fold_streams([vector], me, [blocks_near])
    left_parts, right_parts = left.last(), right.last()
    def own_columns(weight):
        block_width = weight.shape[-1] // narrow_size
        return lax.dynamic_slice_in_dim(
            weight, column * block_width, block_width, axis=weight.ndim - 1
        )

    rate_qkv = MUON_SCALE
    rate_out = MUON_SCALE * math.sqrt(D / (D // 64))
    rate_in = MUON_SCALE * math.sqrt(FF / D)
    rate_back = MUON_SCALE * math.sqrt(D / FF)
    shapes = [mom_attn_in.shape, mom_attn_out.shape]
    grad_qkv, grad_out_w, mom_qkv_new, mom_out_new, gram_four = simple_call(
        partial(attn_moment_kernel, (len(left_parts), len(right_parts))),
        [mom_attn_in, mom_attn_out] + left_parts + right_parts,
        shapes + shapes + [(4, padded(own_rows), padded(own_rows))],
        "attn_moment",
        1e9,
        [token],
    )
    gram_near = gram_four + swap(gram_four, "narrow", 1)
    sweep_in, sweep_back, factor_in, factor_back = simple_call(
        partial(sweep_kernel, 2),
        [blocks_gram],
        [(small_size, small_size), (large_size, large_size)] * 2,
        "ffn_sweeps",
        1e10,
        [gram_four],
    )
    vector_sums = sum(jnp.sum(part, axis=0) for part in vector.last())[0, :vector_size]
    grad_norm_vals = vector_sums[: 4 * norm_part].reshape(4, norm_part)
    grad_bias_final = vector_sums[4 * norm_part : 5 * norm_part]
    grad_bias_inner = vector_sums[5 * norm_part :]
    gram_all = gram_near
    for mask in far_masks("narrow"):
        gram_all = gram_all + swap(gram_near, "narrow", mask)
    new_in, new_back = simple_call(
        partial(ffn_ortho_kernel, (rate_in, rate_back), NS_ITERS - 2),
        [me, sweep_in, sweep_back, factor_in, factor_back, mom_in_new, mom_back_new, ffn_in, ffn_out],
        [mom_ffn_in.shape, mom_ffn_out.shape],
        "ffn_ortho",
        1e10,
        [gram_near],
    )
    new_qkv, new_out = simple_call(
        partial(attn_ortho_kernel, (rate_qkv, rate_out)),
        [me, gram_all, mom_qkv_new, mom_out_new, attn_in, attn_out],
        shapes,
        "attn_ortho",
        5e9,
        [new_in],
    )
    norm_first, norm_second, norm_new = adam_update(
        own_columns(norm_params), first_norms, second_norms, grad_norm_vals
    )
    inner_first, inner_second, inner_new = adam_update(
        own_columns(bias_in), first_bias_in, second_bias_in, grad_bias_inner
    )
    final_first, final_second, final_new = adam_update(
        own_columns(bias_out), first_bias_out, second_bias_out, grad_bias_final
    )
    return (
        block_out,
        input_grad,
        grad_qkv,
        grad_out_w,
        grad_in_w,
        grad_back_w,
        grad_norm_vals,
        grad_bias_inner,
        grad_bias_final,
        mom_qkv_new,
        mom_out_new,
        mom_in_new,
        mom_back_new,
        new_qkv,
        new_out,
        new_in,
        new_back,
        norm_first,
        inner_first,
        final_first,
        norm_second[:2],
        norm_second[2:],
        inner_second,
        final_second,
        norm_new,
        inner_new,
        final_new,
    )


def solution(mesh):
    in_specs = (
        P(("wide", "narrow"), None, None),
        P(("wide", "narrow"), None, None),
        P(("wide", "narrow")),
        P(),
        P(None, "wide", None),
        P("wide", None),
        P("wide", None),
        P("wide", None),
        P(None, "wide"),
        P("wide"),
        P("wide"),
        P(None, "wide", "narrow"),
        P("wide", "narrow"),
        P("wide", "narrow"),
        P("wide", "narrow"),
        P(None, ("wide", "narrow")),
        P(("wide", "narrow")),
        P(("wide", "narrow")),
        P(None, ("wide", "narrow")),
        P(("wide", "narrow")),
        P(("wide", "narrow")),
    )
    out_specs = (
        P(("wide", "narrow"), None, None),
        P(("wide", "narrow"), None, None),
        P(None, "wide", "narrow"),
        P("wide", "narrow"),
        P("wide", "narrow"),
        P("wide", "narrow"),
        P(None, ("wide", "narrow")),
        P(("wide", "narrow")),
        P(("wide", "narrow")),
        P(None, "wide", "narrow"),
        P("wide", "narrow"),
        P("wide", "narrow"),
        P("wide", "narrow"),
        P(None, "wide", "narrow"),
        P("wide", "narrow"),
        P("wide", "narrow"),
        P("wide", "narrow"),
        P(None, ("wide", "narrow")),
        P(("wide", "narrow")),
        P(("wide", "narrow")),
        P(None, ("wide", "narrow")),
        P(None, ("wide", "narrow")),
        P(("wide", "narrow")),
        P(("wide", "narrow")),
        P(None, ("wide", "narrow")),
        P(("wide", "narrow")),
        P(("wide", "narrow")),
    )
    return jax.shard_map(
        per_device, mesh=mesh, in_specs=in_specs, out_specs=out_specs, check_vma=False
    )
```

```python
from functools import partial
import math

import jax
import jax.numpy as jnp
from jax import lax
from jax.experimental import pallas as pl
from jax.experimental.pallas import tpu as pltpu
from jax.sharding import PartitionSpec as P

D = 768
FF = 3072
HEADS = 12
HDIM = 64
FEAT = 32
NS_ITERS = 5
ADAM_STEP = 10


PRECISE = lax.Precision.HIGHEST
NORM_EPS = 1e-05
ORTHO_EPS = 1e-07
ADAM_EPS = 1e-08
LINEAR_COEF = 3.4445
CUBIC_COEF = -4.775
QUINTIC_COEF = 2.0315
MOMENT_DECAY = 0.5
FIRST_DECAY = 0.5
SECOND_DECAY = 0.5
MUON_SCALE = 0.6
WEIGHT_DECAY = 0.01
VECTOR_RATE = 0.4
GROUP = 4
GROUPS = HEADS // GROUP
GE = GROUP * HDIM
GF = GROUP * FEAT


def mm(left, right):
    return jnp.dot(left, right, preferred_element_type=jnp.float32)


def mm_nt(left, right):
    return lax.dot_general(left, right, (((1,), (1,)), ((), ())), preferred_element_type=jnp.float32)


def mm_tn(left, right):
    return lax.dot_general(left, right, (((0,), (0,)), ((), ())), preferred_element_type=jnp.float32)


def halves(value):
    high = value.astype(jnp.bfloat16)
    return high, (value - high.astype(jnp.float32)).astype(jnp.bfloat16)


def normalise(rows):
    centered = rows - jnp.mean(rows, axis=-1, keepdims=True)
    inverse = lax.rsqrt(jnp.mean(centered * centered, axis=-1, keepdims=True) + NORM_EPS)
    return centered * inverse, inverse


def norm_pull(normed, inverse, grad, gain):
    scaled = grad * gain
    mean_plain = jnp.mean(scaled, axis=-1, keepdims=True)
    mean_prod = jnp.mean(scaled * normed, axis=-1, keepdims=True)
    return inverse * (scaled - mean_plain - normed * mean_prod)


def partner_of(values):
    lane = lax.broadcasted_iota(jnp.int32, (values.shape[0], 128), 1)
    first = (lane & (HDIM - 1)) < HDIM // 2
    parts = []
    for at in range(0, values.shape[1], 128):
        block = values[:, at : at + 128]
        ahead = pltpu.roll(block, 128 - HDIM // 2, 1)
        behind = pltpu.roll(block, HDIM // 2, 1)
        parts.append(jnp.where(first, ahead, behind))
    return jnp.concatenate(parts, axis=1)


def head_mask(rows, columns, row_width, column_width):
    row = lax.broadcasted_iota(jnp.int32, (rows, columns), 0) // row_width
    column = lax.broadcasted_iota(jnp.int32, (rows, columns), 1) // column_width
    return row == column


def store_columns(ref, values):
    width = ref.shape[3]
    for n in range(ref.shape[0]):
        ref[n, 0] = values[:, width * n : width * (n + 1)].astype(ref.dtype)


def load_columns(ref):
    return jnp.concatenate([ref[n, 0] for n in range(ref.shape[0])], axis=1)


def attend_kernel(
    lengths_ref, x_ref, w_ref, vec_ref, proj_ref, cos_ref, sin_ref,
    middle_ref, h1_ref, h2_ref, wq_ref, wk_ref, pq_ref, pk_ref, v_ref, state_ref, total_ref, att_ref, rden_ref, mixed_ref,
):
    rows = x_ref.shape[1]
    x = x_ref[0].astype(jnp.float32)
    h1 = (normalise(x)[0] * vec_ref[0:1, :] + vec_ref[1:2, :]).astype(jnp.bfloat16)
    h1_ref[0] = h1
    live = lax.broadcasted_iota(jnp.int32, (rows, 1), 0) < lengths_ref[pl.program_id(0)]
    live = live.astype(jnp.float32)
    cosine = jnp.concatenate([cos_ref[...]] * (D // 128), axis=1)
    sine = jnp.concatenate([sin_ref[...]] * (D // 128), axis=1)
    values = mm(h1, w_ref[2]).astype(jnp.bfloat16)
    v_ref[0] = values
    feats = []
    for j, (w_out, p_out) in enumerate(((wq_ref, pq_ref), (wk_ref, pk_ref))):
        heads = mm(h1, w_ref[j])
        unit = (heads * cosine + partner_of(heads) * sine) * HDIM ** (-0.25)
        w_out[0] = unit
        high, low = halves(unit)
        sq_high, sq_low = halves(unit * unit)
        parts = []
        for g in range(GROUPS):
            cut = slice(GE * g, GE * (g + 1))
            left = jnp.concatenate([high[:, cut], low[:, cut], high[:, cut], sq_high[:, cut], sq_low[:, cut]], axis=1)
            parts.append(jnp.exp(mm(left, proj_ref[g])) * FEAT ** (-0.5))
        phi = jnp.concatenate(parts, axis=1)
        p_out[0] = phi
        feats.append(phi)
    query_low = feats[0].astype(jnp.bfloat16)
    key_vals = feats[1].astype(jnp.bfloat16).astype(jnp.float32) * live
    key_low = key_vals.astype(jnp.bfloat16)
    total_ref[0] = jnp.sum(key_vals, axis=0, keepdims=True)
    mask = head_mask(GF, GE, FEAT, HDIM)
    ones = jnp.ones((rows, GE), jnp.bfloat16)
    attended, inverse_den = [], []
    for g in range(GROUPS):
        cut = slice(GE * g, GE * (g + 1))
        fcut = slice(GF * g, GF * (g + 1))
        both = mm_tn(key_low[:, fcut], jnp.concatenate([values[:, cut], ones], axis=1))
        state = jnp.where(mask, both[:, :GE], 0.0).astype(jnp.bfloat16)
        state_ref[0, g] = state
        tot_high, tot_low = halves(jnp.where(mask, both[:, GE:], 0.0))
        query = query_low[:, fcut]
        numer = mm(query, state)
        denom = mm(jnp.concatenate([query, query], axis=1), jnp.concatenate([tot_high, tot_low], axis=0))
        inverse = 1.0 / denom
        attended.append(numer * inverse)
        inverse_den.append(inverse)
    attended = jnp.concatenate(attended, axis=1)
    att_ref[0] = attended
    rden_ref[0] = jnp.concatenate(inverse_den, axis=1)
    mixed = attended.astype(jnp.bfloat16)
    mixed_ref[0] = mixed
    middle = x + mm(mixed, w_ref[3])
    middle_ref[0] = middle
    h2_ref[0] = (normalise(middle)[0] * vec_ref[2:3, :] + vec_ref[3:4, :]).astype(jnp.bfloat16)


def middle_back_kernel(og_ref, gh2_ref, ffn_ref, middle_ref, vec_ref, out_ref, gm_ref, gb_ref, sums_ref):
    og = og_ref[0].astype(jnp.float32)
    middle = middle_ref[0]
    out_ref[0] = middle + (ffn_ref[0] + vec_ref[4:5, :])
    grad_h2 = gh2_ref[0]
    normed, inverse = normalise(middle)
    grad_middle = og + norm_pull(normed, inverse, grad_h2, vec_ref[2:3, :])
    gm_ref[0] = grad_middle
    store_columns(gb_ref, grad_middle)

    @pl.when(pl.program_id(0) == 0)
    def _():
        sums_ref[...] = jnp.zeros_like(sums_ref)

    sums_ref[0:1, :] += jnp.sum(grad_h2 * normed, axis=0, keepdims=True)
    sums_ref[1:2, :] += jnp.sum(grad_h2, axis=0, keepdims=True)
    sums_ref[2:3, :] += jnp.sum(og, axis=0, keepdims=True)


def attend_back_kernel(
    lengths_ref, gm_ref, w_ref, projt_ref, cos_ref, sin_ref,
    wq_ref, wk_ref, pq_ref, pk_ref, v_ref, state_ref, total_ref, att_ref, rden_ref,
    gq_ref, gk_ref, gv_ref,
):
    rows = gm_ref.shape[1]
    branch = gm_ref[0].astype(jnp.bfloat16)
    grad_numer = mm_nt(branch, w_ref[0]) * rden_ref[0]
    gn_high, gn_low = halves(grad_numer)
    pr_high, pr_low = halves(grad_numer * att_ref[0])
    live = (lax.broadcasted_iota(jnp.int32, (rows, 1), 0) < lengths_ref[pl.program_id(0)]).astype(jnp.float32)
    query_low = pq_ref[0].astype(jnp.bfloat16)
    key_low = (pk_ref[0].astype(jnp.bfloat16).astype(jnp.float32) * live).astype(jnp.bfloat16)
    mask = head_mask(GF, GE, FEAT, HDIM)
    spread = head_mask(GE, GF, HDIM, FEAT).astype(jnp.float32).astype(jnp.bfloat16)
    spread2 = jnp.concatenate([spread, spread], axis=0)
    gather = mask.astype(jnp.float32).astype(jnp.bfloat16)
    gather2 = jnp.concatenate([gather, gather], axis=0)
    grad_u = ([], [])
    grad_v = []
    for g in range(GROUPS):
        cut = slice(GE * g, GE * (g + 1))
        fcut = slice(GF * g, GF * (g + 1))
        query, key, values = query_low[:, fcut], key_low[:, fcut], v_ref[0, :, cut]
        state = state_ref[0, g]
        grad_denom = -mm(jnp.concatenate([pr_high[:, cut], pr_low[:, cut]], axis=1), spread2)
        two = jnp.concatenate([gn_high[:, cut], gn_low[:, cut]], axis=1)
        grad_qfeat = mm_nt(two, jnp.concatenate([state, state], axis=1)) + grad_denom * total_ref[0, :, fcut]
        pair = mm_tn(query, two)
        grad_state = jnp.where(mask, pair[:, :GE] + pair[:, GE:], 0.0)
        grad_total = jnp.sum(grad_denom * query.astype(jnp.float32), axis=0, keepdims=True)
        gs_high, gs_low = halves(grad_state)
        grad_kfeat = mm_nt(
            jnp.concatenate([values, values], axis=1), jnp.concatenate([gs_high, gs_low], axis=1)
        )
        grad_kfeat = (grad_kfeat + grad_total) * live
        grad_v.append(mm(jnp.concatenate([key, key], axis=1), jnp.concatenate([gs_high, gs_low], axis=0)))
        for j, (grad_feat, p_in, w_in) in enumerate(((grad_qfeat, pq_ref, wq_ref), (grad_kfeat, pk_ref, wk_ref))):
            t_high, t_low = halves(grad_feat * p_in[0, :, fcut])
            pulled = mm(jnp.concatenate([t_high, t_low, t_high], axis=1), projt_ref[g])
            weight = mm(jnp.concatenate([t_high, t_low], axis=1), gather2)
            grad_u[j].append((pulled - weight * w_in[0, :, cut]) * HDIM ** (-0.25))
    cosine = jnp.concatenate([cos_ref[...]] * (D // 128), axis=1)
    sine = jnp.concatenate([sin_ref[...]] * (D // 128), axis=1)
    for grads, ref in zip(grad_u, (gq_ref, gk_ref)):
        turned = jnp.concatenate(grads, axis=1)
        store_columns(ref, turned * cosine - partner_of(turned) * sine)
    store_columns(gv_ref, jnp.concatenate(grad_v, axis=1))


def input_back_kernel(x_ref, gm_ref, gq_ref, gk_ref, gv_ref, w_ref, vec_ref, out_ref, sums_ref):
    grad_h1 = sum(mm_nt(load_columns(ref), w_ref[j]) for j, ref in enumerate((gq_ref, gk_ref, gv_ref)))
    normed, inverse = normalise(x_ref[0].astype(jnp.float32))
    out_ref[0] = gm_ref[0] + norm_pull(normed, inverse, grad_h1, vec_ref[0:1, :])

    @pl.when(pl.program_id(0) == 0)
    def _():
        sums_ref[...] = jnp.zeros_like(sums_ref)

    sums_ref[0:1, :] += jnp.sum(grad_h1 * normed, axis=0, keepdims=True)
    sums_ref[1:2, :] += jnp.sum(grad_h1, axis=0, keepdims=True)


def attn_weight_kernel(me_ref, h1_ref, mixed_ref, gq_ref, gk_ref, gv_ref, gb_ref, *out_refs):
    width, rows = out_refs[0].shape[1], out_refs[0].shape[2] // 2
    h1 = h1_ref[...]
    left = mm_tn(h1, jnp.concatenate([gq_ref[...], gk_ref[...]], axis=1)).astype(jnp.bfloat16)
    right = jnp.concatenate([mm_tn(h1, gv_ref[...]), mm_tn(mixed_ref[...], gb_ref[...])], axis=1).astype(jnp.bfloat16)
    for w in range(width * len(out_refs)):
        out_refs[w // width][0, w % width, :rows] = left[rows * w : rows * (w + 1)]
        out_refs[w // width][0, w % width, rows:] = right[rows * w : rows * (w + 1)]


def ffn_kernel(has_past, blocks, h2_ref, og_ref, win_ref, wback_ref, bias_ref, me_ref, *rest):
    if has_past:
        out_past_ref, gh2_past_ref, *rest = rest
    if blocks:
        out_ref, gh2_ref, bsum_ref, keep_ref, *send_refs, act_ref, gi_ref, gw_ref = rest
    else:
        out_ref, gh2_ref, bsum_ref, gw_ref, act_ref, gi_ref = rest
    seqs, rows = out_ref.shape[0], out_ref.shape[1]
    step = pl.program_id(0)
    win, wback = win_ref[...], wback_ref[...]
    bias = bias_ref[...]

    def part(s, carry):
        span = pl.ds(pl.multiple_of(s * rows, rows), rows)
        inner = mm(h2_ref[s], win) + bias
        grad_act = mm_nt(og_ref[s], wback)
        cdf = 0.5 * (1.0 + lax.erf(inner * (2.0**-0.5)))
        pdf = jnp.exp(-0.5 * inner * inner) * (2.0 * math.pi) ** -0.5
        act = (inner * cdf).astype(jnp.bfloat16)
        grad_inner = (grad_act * (cdf + inner * pdf)).astype(jnp.bfloat16)
        act_ref[span, :] = act
        gi_ref[span, :] = grad_inner
        out_part = mm(act, wback)
        gh2_part = mm_nt(grad_inner, win)

        @pl.when(step == 0)
        def _():
            if has_past:
                out_ref[s] = out_past_ref[s] + out_part
                gh2_ref[s] = gh2_past_ref[s] + gh2_part
            else:
                out_ref[s] = out_part
                gh2_ref[s] = gh2_part

        @pl.when(step > 0)
        def _():
            out_ref[s] += out_part
            gh2_ref[s] += gh2_part

        return carry + jnp.sum(grad_inner.astype(jnp.float32), axis=0, keepdims=True)

    bsum_ref[...] = lax.fori_loop(0, seqs, part, jnp.zeros(bias.shape, jnp.float32), unroll=True)
    h2 = h2_ref[...].reshape(seqs * rows, D)
    og = og_ref[...].reshape(seqs * rows, D)
    grad_in = mm_tn(h2, gi_ref[...]).astype(jnp.bfloat16)
    grad_back = mm_tn(og, act_ref[...]).astype(jnp.bfloat16)
    if not blocks:
        gw_ref[0] = grad_in
        gw_ref[1] = grad_back
        return
    narrow, wide = gw_ref.shape[0], gw_ref.shape[1]
    in_rows, in_cols = D // wide, gw_ref.shape[3]
    width = grad_in.shape[1]
    for k in range(width // in_cols):
        for w in range(wide):
            gw_ref[step * (width // in_cols) + k, w, :in_rows, :] = grad_in[
                in_rows * w : in_rows * (w + 1), in_cols * k : in_cols * (k + 1)
            ]
    back_rows = D // narrow
    half = back_rows // 2
    for k in range(width // 128):
        for n in range(narrow):
            for h in range(2):
                gw_ref[n, step * (width // 128) + k, in_rows:, 128 * h : 128 * (h + 1)] = grad_back[
                    back_rows * n + half * h : back_rows * n + half * (h + 1), 128 * k : 128 * (k + 1)
                ]

    @pl.when(step == pl.num_programs(0) - 1)
    def _():
        side = me_ref[1] & 1
        for far in range(narrow // 2):
            for w in range(wide):
                keep_ref[far, w] = gw_ref[2 * far + side, w]
                width = wide // len(send_refs)
                send_refs[w // width][far, w % width] = gw_ref[2 * far + (1 - side), w]


def spec(shape, index):
    return pl.BlockSpec(shape, index)


LIMIT = 60 * 1024 * 1024
ANYWHERE = pl.BlockSpec(memory_space=pl.ANY)


def skipping(kernel, before, extra):
    def run(*refs):
        return kernel(*refs[:before], *refs[before + extra :])

    return run


def estimate(flops, moved, transcendentals=0):
    return pl.CostEstimate(flops=int(flops), bytes_accessed=int(moved), transcendentals=int(transcendentals))


def whole(array):
    rank = array.ndim
    return pl.BlockSpec(array.shape, lambda *unused: (0,) * rank)


def by_seq(shape):
    rank = len(shape)
    return pl.BlockSpec((1,) + tuple(shape[1:]), lambda s, *unused: (s,) + (0,) * (rank - 1))


def by_seq_second(shape):
    rank = len(shape)
    return pl.BlockSpec((shape[0], 1) + tuple(shape[2:]), lambda s, *unused: (0, s) + (0,) * (rank - 2))


def attend(lengths, x, weights, vectors, proj, cosine, sine, after):
    seqs, rows, unused_width = x.shape
    bf, f4 = jnp.bfloat16, jnp.float32
    shapes = [
        ((seqs, rows, D), f4), ((seqs, rows, D), bf), ((seqs, rows, D), bf), ((seqs, rows, D), f4), ((seqs, rows, D), f4),
        ((seqs, rows, HEADS * FEAT), f4), ((seqs, rows, HEADS * FEAT), f4), ((seqs, rows, D), bf),
        ((seqs, GROUPS, GF, GE), bf), ((seqs, 1, HEADS * FEAT), f4), ((seqs, rows, D), f4), ((seqs, rows, D), f4),
        ((seqs, rows, D), bf),
    ]
    return pl.pallas_call(
        skipping(attend_kernel, 7, len(after)),
        grid_spec=pltpu.PrefetchScalarGridSpec(
            num_scalar_prefetch=1,
            grid=(seqs,),
            in_specs=[by_seq(x.shape)] + [whole(a) for a in (weights, vectors, proj, cosine, sine)]
            + [ANYWHERE] * len(after),
            out_specs=[by_seq(shape) for shape, unused in shapes],
        ),
        out_shape=[jax.ShapeDtypeStruct(shape, dtype) for shape, dtype in shapes],
        compiler_params=pltpu.CompilerParams(vmem_limit_bytes=LIMIT),
        cost_estimate=estimate(seqs * rows * D * D * 6, 20e6),
        name="attend",
    )(lengths, x, weights, vectors, proj, cosine, sine, *after)


def middle_back(og, grad_h2, ffn, middle, vectors, narrow_size):
    seqs, rows, unused_width = og.shape
    blocked = (narrow_size, seqs, rows, D // narrow_size)
    full = jax.ShapeDtypeStruct(og.shape, jnp.float32)
    return pl.pallas_call(
        middle_back_kernel,
        grid=(seqs,),
        in_specs=[by_seq(og.shape)] * 4 + [whole(vectors)],
        out_specs=[by_seq(og.shape)] * 2 + [by_seq_second(blocked), pl.BlockSpec((8, D), lambda s: (0, 0))],
        out_shape=[full, full, jax.ShapeDtypeStruct(blocked, jnp.bfloat16), jax.ShapeDtypeStruct((8, D), jnp.float32)],
        compiler_params=pltpu.CompilerParams(vmem_limit_bytes=LIMIT),
        cost_estimate=estimate(1e7, 16e6),
        name="middle_back",
    )(og, grad_h2, ffn, middle, vectors)


def attend_back(lengths, grad_middle, weights, projt, cosine, sine, kept, narrow_size, after):
    seqs, rows, unused_width = grad_middle.shape
    blocked = (narrow_size, seqs, rows, D // narrow_size)
    count = 6 + len(kept)
    return pl.pallas_call(
        skipping(attend_back_kernel, count, len(after)),
        grid_spec=pltpu.PrefetchScalarGridSpec(
            num_scalar_prefetch=1,
            grid=(seqs,),
            in_specs=[by_seq(grad_middle.shape), pl.BlockSpec((1, D, D), lambda s, *unused: (3, 0, 0))]
            + [whole(a) for a in (projt, cosine, sine)]
            + [by_seq(a.shape) for a in kept]
            + [ANYWHERE] * len(after),
            out_specs=[by_seq_second(blocked)] * 3,
        ),
        out_shape=[jax.ShapeDtypeStruct(blocked, jnp.bfloat16)] * 3,
        compiler_params=pltpu.CompilerParams(vmem_limit_bytes=LIMIT),
        cost_estimate=estimate(seqs * rows * D * D * 8, 40e6),
        name="attend_back",
    )(lengths, grad_middle, weights, projt, cosine, sine, *kept, *after)


def input_back(x, grad_middle, grads, weights, vectors, after):
    seqs, rows, unused_width = x.shape
    return pl.pallas_call(
        skipping(input_back_kernel, 4 + len(grads), len(after)),
        grid=(seqs,),
        in_specs=[by_seq(x.shape), by_seq(x.shape)] + [by_seq_second(a.shape) for a in grads] + [whole(weights), whole(vectors)] + [ANYWHERE] * len(after),
        out_specs=[by_seq(x.shape), pl.BlockSpec((8, D), lambda s: (0, 0))],
        out_shape=[jax.ShapeDtypeStruct(x.shape, jnp.float32), jax.ShapeDtypeStruct((8, D), jnp.float32)],
        compiler_params=pltpu.CompilerParams(vmem_limit_bytes=LIMIT),
        cost_estimate=estimate(seqs * rows * D * D * 6, 15e6),
        name="input_back",
    )(x, grad_middle, *grads, weights, vectors, *after)


def attn_weights(me, h1, mixed, grads, wide_size, side, after):
    narrow_size, seqs, rows, width = grads[0].shape
    tokens = seqs * rows
    flat = [a.reshape(narrow_size, tokens, width) for a in grads]
    h1, mixed = h1.reshape(tokens, D), mixed.reshape(tokens, D)
    count = 2 if side else 1
    shape = (narrow_size // 2, wide_size // count, 2 * D // wide_size, 2 * width)

    def block_at(i, me_ref):
        return (2 * i + ((me_ref[1] & 1) ^ side), 0, 0)

    return pl.pallas_call(
        skipping(attn_weight_kernel, 7, len(after)),
        grid_spec=pltpu.PrefetchScalarGridSpec(
            num_scalar_prefetch=1,
            grid=(narrow_size // 2,),
            in_specs=[whole(h1), whole(mixed)] + [pl.BlockSpec((None, tokens, width), block_at)] * 4 + [ANYWHERE] * len(after),
            out_specs=[pl.BlockSpec((1,) + shape[1:], lambda i, *unused: (i, 0, 0, 0))] * count,
        ),
        out_shape=[jax.ShapeDtypeStruct(shape, jnp.bfloat16)] * count,
        compiler_params=pltpu.CompilerParams(vmem_limit_bytes=LIMIT),
        cost_estimate=estimate(tokens * D * D * 4, 8e6),
        name="attn_weights",
    )(me, h1, mixed, *flat, *after)


def ffn_tile(tile, h2, og, w_in, w_back, bias, me, past, wide_size, narrow_size, blocks, after):
    seqs, rows, unused_width = h2.shape
    width = w_in.shape[2]
    step = 1024 if width % 1024 == 0 else width
    tokens = jax.ShapeDtypeStruct(h2.shape, jnp.float32)
    out_specs = [whole(h2), whole(h2), pl.BlockSpec((1, step), lambda i: (0, i))]
    out_shape = [tokens, tokens, jax.ShapeDtypeStruct((1, width), jnp.float32)]
    scratch = [pltpu.VMEM((seqs * rows, step), jnp.bfloat16)] * 2
    if blocks:
        block = (2 * D // wide_size, width // narrow_size)
        half = jax.ShapeDtypeStruct((narrow_size // 2, wide_size) + block, jnp.bfloat16)
        part = jax.ShapeDtypeStruct((narrow_size // 2, wide_size // 4) + block, jnp.bfloat16)
        out_specs += [whole(half)] + [whole(part)] * 4
        out_shape += [half] + [part] * 4
        scratch.append(pltpu.VMEM((narrow_size, wide_size) + block, jnp.bfloat16))
    else:
        out_specs.append(pl.BlockSpec((2, D, step), lambda i: (0, 0, i)))
        out_shape.append(jax.ShapeDtypeStruct((2, D, width), jnp.bfloat16))
    return pl.pallas_call(
        skipping(partial(ffn_kernel, past is not None, blocks), 6 + len(past or ()), len(after)),
        grid=(width // step,),
        in_specs=[
            whole(h2),
            whole(og),
            pl.BlockSpec((None, D, step), lambda i: (tile, 0, i)),
            pl.BlockSpec((None, step, D), lambda i: (tile, i, 0)),
            pl.BlockSpec((None, 1, step), lambda i: (0, 0, i)),
            pl.BlockSpec(memory_space=pltpu.SMEM),
        ]
        + [whole(a) for a in past or ()]
        + [ANYWHERE] * len(after),
        out_specs=out_specs,
        out_shape=out_shape,
        scratch_shapes=scratch,
        compiler_params=pltpu.CompilerParams(vmem_limit_bytes=LIMIT),
        cost_estimate=estimate(seqs * rows * D * width * 12, 20e6, seqs * rows * width * 2),
        name="ffn_tile",
    )(h2, og, w_in, w_back, bias, me, *(past or ()), *after)


def rotary_blocks(length):
    half = HDIM // 2
    frequency = jnp.exp(jnp.arange(half, dtype=jnp.float32) * (-2.0 * math.log(10000.0) / HDIM))
    angles = jnp.arange(length, dtype=jnp.float32)[:, None] * frequency[None, :]
    cosine, sine = jnp.cos(angles), jnp.sin(angles)
    return jnp.tile(cosine, (1, 4)), jnp.tile(jnp.concatenate([-sine, sine], axis=1), (1, 2))


def projection_blocks(feature_proj):
    rows = jnp.arange(GF)[:, None] // FEAT
    columns = jnp.arange(GE)[None, :] // HDIM
    mask = (rows == columns).astype(jnp.float32)
    tall = jnp.tile(feature_proj.reshape(GROUPS, GF, HDIM), (1, 1, GROUP)) * mask
    high, low = halves(tall)
    square = jnp.broadcast_to(-0.5 * mask, tall.shape).astype(jnp.bfloat16)
    turned = [a.swapaxes(1, 2) for a in (high, high, low, square, square)]
    return jnp.concatenate(turned, axis=1), jnp.concatenate([high, high, low], axis=1)


def xor_pairs(size, mask):
    return [(index, index ^ mask) for index in range(size)]


def tie(value, *earlier):
    return lax.optimization_barrier((value, earlier))[0]


def swap(value, axis_name, mask):
    return lax.ppermute(value, axis_name, xor_pairs(lax.axis_size(axis_name), mask))


def far_masks(axis_name):
    return [2 * m for m in range(1, lax.axis_size(axis_name) // 2)]


class Gather:
    def __init__(self, pieces, cut, turn=None):
        self.cut = cut
        self.turn = turn or (lambda piece: piece)
        self.pieces = pieces

    def near(self, *earlier):
        self.pieces = [tie(piece, *earlier) for piece in self.pieces] if earlier else self.pieces
        self.first = jnp.stack([piece[..., : -self.cut, :] for piece in self.pieces])
        self.second = jnp.stack([self.turn(piece[..., -self.cut :, :]) for piece in self.pieces])
        self.first_in = swap(self.first, "wide", 1)
        self.second_in = [swap(self.second, "narrow", mask) for mask in far_masks("narrow")]
        return [self.first_in] + self.second_in

    def far(self, *earlier):
        if earlier:
            self.first_in = tie(self.first_in, *earlier)
        self.first = jnp.stack([self.first, self.first_in])
        self.extra = self.first[..., self.cut :, :]
        self.first = self.first[..., : self.cut, :]
        self.second = jnp.stack([self.second] + (list(tie(tuple(self.second_in), *earlier)) if earlier else self.second_in))
        self.first_in = [swap(self.first, "narrow", mask) for mask in far_masks("narrow")]
        self.second_in = swap(self.second, "wide", 1)
        return self.first_in + [self.second_in]

    def core(self, *earlier):
        if earlier:
            late = tie((tuple(self.first_in), self.second_in), *earlier)
            self.first_in, self.second_in = list(late[0]), late[1]
        self.mine = [self.first] + self.first_in + [self.second, self.second_in]
        self.theirs = [swap(part, "narrow", 1) for part in self.mine]
        return self.theirs


def far_wide(piece):
    return [piece] + [swap(piece, "wide", mask) for mask in far_masks("wide")]


def gathered_at(part, index, side, fars, ms):
    m, index = index % ms, index // ms
    half, near, far = (0, index, part) if part < fars else (1, part - fars, index)
    return half, 2 * m + near, 2 * far + side


def placing(copies, fars, ms, me_ref, refs, outs, sems):
    found = []
    for k, ref in enumerate(refs):
        side, part = divmod(k, fars + 2)
        for index in range(ref.shape[0] * ms):
            half, wide_mask, narrow_mask = gathered_at(part, index, side, fars, ms)
            wide, narrow = me_ref[0] ^ wide_mask, me_ref[1] ^ narrow_mask
            for source, target in copies(ref.at[index // ms, index % ms], outs, half, wide, narrow):
                found.append(pltpu.make_async_copy(source, target, sems.at[len(found)]))
    return found


def place_kernel(copies, fars, ms, me_ref, *rest):
    count = 2 * (fars + 2)
    found = placing(copies, fars, ms, me_ref, rest[:count], rest[count:-1], rest[-1])
    for copy in found:
        copy.start()
    for copy in found:
        copy.wait()


def place(me, parts, copies, shapes, name):
    fars, ms = lax.axis_size("narrow") // 2, lax.axis_size("wide") // 2
    return pl.pallas_call(
        partial(place_kernel, copies, fars, ms),
        out_shape=[jax.ShapeDtypeStruct(shape, parts[0].dtype) for shape in shapes],
        in_specs=[pl.BlockSpec(memory_space=pltpu.SMEM)] + [ANYWHERE] * len(parts),
        out_specs=[pl.BlockSpec(memory_space=pltpu.VMEM)] * len(shapes),
        compiler_params=pltpu.CompilerParams(vmem_limit_bytes=LIMIT),
        scratch_shapes=[pltpu.SemaphoreType.DMA((8 * fars * ms,))],
        cost_estimate=estimate(0, 4 * sum(math.prod(shape) for shape in shapes)),
        name=name,
    )(me, *parts)


def in_order(parts, wide_size, narrow_size, place_of):
    my_wide, my_narrow = lax.axis_index("wide"), lax.axis_index("narrow")
    ordered = [
        pick(parts, place_of(w ^ my_wide, n ^ my_narrow), 0) for w in range(wide_size) for n in range(narrow_size)
    ]
    return jnp.stack(ordered).reshape((wide_size, narrow_size) + parts.shape[1:])


def half_in_order(parts, half):
    wide_size, narrow_size = lax.axis_size("wide"), lax.axis_size("narrow")
    fars, ms = narrow_size // 2, wide_size // 2

    def place_of(wide_mask, narrow_mask):
        near, m, side, far = wide_mask & 1, wide_mask >> 1, narrow_mask & 1, narrow_mask >> 1
        outer = far * 2 + near if half == 0 else near * fars + far
        return side * (fars * 2 * ms) + outer * ms + m

    count = len(parts) // 2
    found = []
    for side in range(2):
        own = parts[side * count : (side + 1) * count]
        found += own[:fars] if half == 0 else own[fars:]
    found = [part.reshape((-1,) + part.shape[2:]) for part in found]
    return in_order(jnp.concatenate(found), wide_size, narrow_size, place_of)


def pick(value, index, axis):
    return lax.dynamic_index_in_dim(value, index, axis, keepdims=False)


def core_swap(send):
    return [swap(part, "narrow", 1) for part in send]


def cut_wide(send):
    count = min(4, send.shape[1] // 2)
    width = send.shape[1] // count
    return [lax.slice_in_dim(send, width * k, width * (k + 1), axis=1) for k in range(count)]


def far_all_to_all(pieces):
    groups = [list(range(near, lax.axis_size("wide"), 2)) for near in range(2)]
    widths = [piece.shape[1] for piece in pieces]
    joint = lax.all_to_all(jnp.concatenate(pieces, axis=1), "wide", 0, 0, axis_index_groups=groups)
    found, at = [], 0
    for width in widths:
        found.append(lax.slice_in_dim(joint, at, at + width, axis=1))
        at += width
    return found


class Stream:
    def __init__(self, keep, arrived, order, window=None):
        rest = keep.shape[2:]
        self.quarters, self.wide = len(arrived), keep.shape[1]
        self.window = window or (0, rest[0])
        self.rest = (self.window[1] - self.window[0],) + rest[1:]
        self.order = list(order)
        self.dims = {"y": keep.shape[0], "z": keep.shape[1] // 2, "x": 2}
        self.parts = [part.reshape((1, -1) + rest) for part in [keep] + arrived]

    def plan(self):
        by_all = self.order[0] == "a"
        axis = "z" if by_all else self.order[0]
        names = [name for name in ("y", "z", "x") if name in self.dims]
        sizes = [self.dims[name] for name in names]
        cut = names.index(axis)
        stride = math.prod(sizes[cut + 1 :])
        places = [
            outer * sizes[cut] * stride + inner for outer in range(math.prod(sizes[:cut])) for inner in range(stride)
        ]
        return by_all, axis, sizes[cut], stride, places

    def outputs(self):
        by_all, unused_axis, size, unused_stride, places = self.plan()
        shape = (len(places),) + self.rest
        return [(size,) + shape] if by_all else [(1,) + shape] * size

    def sent(self, pieces):
        axis = self.order.pop(0)
        self.quarters = 0
        del self.dims["z" if axis == "a" else axis]
        self.window = (0, self.rest[0])
        if axis == "a":
            self.parts = list(pieces)
        else:
            name, scale = ("narrow", 2) if axis == "y" else ("wide", 1 if axis == "x" else 2)
            self.parts = [pieces[0]] + [swap(piece, name, scale * m) for m, piece in enumerate(pieces) if m]

    def last(self):
        return [part.reshape((-1,) + self.rest) for part in self.parts]


def fold_kernel(plans, counts, windows, quarters, me_ref, *refs):
    for (by_all, axis, size, stride, places), count, (low, high), parts in zip(plans, counts, windows, quarters):
        ins, refs = take(refs, count)
        outs, refs = take(refs, 1 if by_all else size)
        here = me_ref[1] >> 1 if axis == "y" else me_ref[0] & 1 if axis == "x" else me_ref[0] >> 1
        for step in range(size):
            at = step * stride if by_all else (here ^ step) * stride
            for k, base in enumerate(places):
                found = [(ref, source, base + at) for ref in (ins[:1] if parts else ins) for source in range(ref.shape[0])]
                if parts:
                    wide = parts[1]
                    width = wide // parts[0]
                    far, left = (here ^ step, base) if axis == "y" else (base // wide, base % wide)
                    inner = left % width if axis == "y" else left % width + at
                    found.append((ins[1 + left // width], 0, far * width + inner))
                total = sum(ref[source, place, low:high].astype(jnp.float32) for ref, source, place in found)
                out = outs[0].at[step, k] if by_all else outs[step].at[0, k]
                out[...] = total.astype(out.dtype)


def interleaved(kernel, before, extra, out_counts, counts):
    def run(*refs):
        ins, outs = refs[1:before], refs[before + extra :]
        turn = []
        for out_count, count in zip(out_counts, counts):
            part, ins = take(ins, count)
            turn += part
            part, outs = take(outs, out_count)
            turn += part
        return kernel(refs[0], *turn)

    return run


def fold_streams(streams, me, after):
    plans = [stream.plan() for stream in streams]
    counts = [len(stream.parts) for stream in streams]
    windows = [stream.window for stream in streams]
    out_shapes = [
        [jax.ShapeDtypeStruct(shape, stream.parts[0].dtype) for shape in stream.outputs()] for stream in streams
    ]
    operands = sum((stream.parts for stream in streams), [])
    quarters = [(stream.quarters, stream.wide) if stream.quarters else None for stream in streams]
    kernel = partial(fold_kernel, plans, counts, windows, quarters)
    found = pl.pallas_call(
        interleaved(kernel, 1 + len(operands), len(after), [len(shapes) for shapes in out_shapes], counts),
        in_specs=[pl.BlockSpec(memory_space=pltpu.SMEM)] + [whole_plain(a) for a in operands] + [ANYWHERE] * len(after),
        out_shape=sum(out_shapes, []),
        compiler_params=pltpu.CompilerParams(vmem_limit_bytes=LIMIT),
        cost_estimate=estimate(1e6, 6e6),
        name="fold",
    )(me, *operands, *after)
    token = found[0]
    by_all = []
    for stream, shapes, plan in zip(streams, out_shapes, plans):
        part, found = take(found, len(shapes))
        stream.sent(part)
        if plan[0]:
            by_all.append(stream)
    if by_all:
        for stream, part in zip(by_all, far_all_to_all([stream.parts[0] for stream in by_all])):
            stream.parts = [part]
    return token


def narrow_sum(value):
    mask = 1
    while mask < lax.axis_size("narrow"):
        value = value + swap(value, "narrow", mask)
        mask *= 2
    return value


def exact(left, right, dims=(((1,), (0,)), ((), ()))):
    return lax.dot_general(left, right, dims, precision=PRECISE, preferred_element_type=jnp.float32)


def close(left, right):
    left_high, left_low = halves(left)
    right_high, right_low = halves(right)
    return mm(
        jnp.concatenate([left_high, left_low, left_high], axis=1), jnp.concatenate([right_high, right_high, right_low], axis=0)
    )


def diagonal_of(shape):
    return lax.broadcasted_iota(jnp.int32, shape, 0) == lax.broadcasted_iota(jnp.int32, shape, 1)


def ortho_scale(gram_mat):
    square_sum = jnp.where(diagonal_of(gram_mat.shape), gram_mat, 0.0)
    square_sum = jnp.sum(jnp.sum(square_sum, axis=1, keepdims=True), axis=0, keepdims=True)
    return 1.0 / (jnp.sqrt(square_sum) + ORTHO_EPS)


def sweeps(grams, factors, count, last):
    for left in reversed(range(count)):
        polys = [CUBIC_COEF * gram + QUINTIC_COEF * close(gram, gram) for gram in grams]
        polys = [jnp.where(diagonal_of(poly.shape), poly + LINEAR_COEF, poly) for poly in polys]
        if not left and last:
            return grams, [close(poly, factor) for poly, factor in zip(polys, factors)]
        if factors is None:
            factors, halfway = polys, [close(poly, gram) for poly, gram in zip(polys, grams)]
        else:
            both = [
                close(poly, jnp.concatenate([factor, gram], axis=1)) for poly, factor, gram in zip(polys, factors, grams)
            ]
            factors, halfway = zip(*[(pair[:, : pair.shape[0]], pair[:, pair.shape[0] :]) for pair in both])
        grams = [close(poly, half) for poly, half in zip(polys, halfway)]
    return grams, factors


def apply_factor(factor, block):
    rows = block.shape[0]
    return exact(factor[:rows, :rows], block)


def apply_factor_turned(factor, block):
    rows = block.shape[1]
    return close(block, factor) if rows % 128 == 0 else exact(block, factor[:rows, :rows])


def ortho_start(grams):
    scales = [ortho_scale(gram) for gram in grams]
    return [gram * scale * scale for gram, scale in zip(grams, scales)], scales


def block_pairs(count):
    return [(row, column) for row in range(count) for column in range(row + 1)]


def padded(size):
    return -(-size // 128) * 128


def store_padded(gram, out_ref):
    out_ref[...] = jnp.zeros(out_ref.shape, jnp.float32)
    out_ref[: gram.shape[0], : gram.shape[1]] = gram


def packed_blocks(small, large, out_ref):
    pairs = block_pairs(padded(large.shape[0]) // 128)
    for k, (row, column) in enumerate(pairs):
        store_padded(large[128 * row : 128 * (row + 1), 128 * column : 128 * (column + 1)], out_ref.at[k])
    store_padded(small, out_ref.at[len(pairs)])


def unpacked_blocks(blocks, count):
    pairs = block_pairs(count)
    found = {}
    for k, (row, column) in enumerate(pairs):
        found[row, column] = blocks[k]
        if row != column:
            found[column, row] = blocks[k].T
    large = [jnp.concatenate([found[row, column] for column in range(count)], axis=1) for row in range(count)]
    return blocks[len(pairs)], jnp.concatenate(large, axis=0)


def sweep_kernel(count, *refs):
    blocks, (small_ref, large_ref, small_factor_ref, large_factor_ref) = refs[:-4], refs[-4:]
    grams = unpacked_blocks(sum(ref[...] for ref in blocks), large_ref.shape[0] // 128)
    grams, scales = ortho_start(grams)
    grams, factors = sweeps(grams, None, count, False)
    for gram, factor, scale, gram_ref, factor_ref in zip(
        grams, factors, scales, (small_ref, large_ref), (small_factor_ref, large_factor_ref)
    ):
        gram_ref[...] = gram
        factor_ref[...] = factor * scale


def moment_step(gradient, moment_ref, grad_ref, new_ref, at=(), along=1):
    grad_ref[at + (slice(None), slice(None))] = gradient
    moment = MOMENT_DECAY * moment_ref[at + (slice(None), slice(None))] + gradient
    new_ref[at + (slice(None), slice(None))] = moment
    return exact(moment, moment, (((along,), (along,)), ((), ())))


def sum_of(refs):
    return sum(ref[k].astype(jnp.float32) for ref in refs for k in range(ref.shape[0]))


def take(refs, count):
    return refs[:count], refs[count:]


def attn_moment_kernel(counts, mqkv_ref, mout_ref, *refs):
    left, refs = take(refs, counts[0])
    right, refs = take(refs, counts[1])
    gqkv_ref, gout_ref, nqkv_ref, nout_ref, gram_ref = refs
    left, right = sum_of(left), sum_of(right)
    width = mout_ref.shape[1]
    store_padded(moment_step(left[:, :width], mqkv_ref, gqkv_ref, nqkv_ref, (0,)), gram_ref.at[0])
    store_padded(moment_step(left[:, width:], mqkv_ref, gqkv_ref, nqkv_ref, (1,)), gram_ref.at[1])
    store_padded(moment_step(right[:, :width], mqkv_ref, gqkv_ref, nqkv_ref, (2,)), gram_ref.at[2])
    store_padded(moment_step(right[:, width:], mout_ref, gout_ref, nout_ref), gram_ref.at[3])


def ffn_moment_kernel(counts, unit, min_ref, mback_ref, *refs):
    found = []
    for count in counts:
        part, refs = take(refs, count)
        found.append(sum_of(part))
    gin_ref, gback_ref, nin_ref, nback_ref, blocks_ref = refs
    rows = min_ref.shape[0]
    if len(found) * 128 == mback_ref.shape[1]:
        grad_in = [part[:rows] for part in found]
        turned = [jnp.concatenate([part[rows:, :128], part[rows:, 128:]], axis=0) for part in found]
        turned = jnp.concatenate(turned, axis=1)
    else:
        grad_in, turned = [found[0]], found[1]
    pieces = [part[:, at : at + unit] for at in range(0, grad_in[0].shape[1], unit) for part in grad_in]
    small = moment_step(jnp.concatenate(pieces, axis=1), min_ref, gin_ref, nin_ref)
    packed_blocks(small, moment_step(turned, mback_ref, gback_ref, nback_ref, (), 0), blocks_ref)


def with_own_columns(me_ref, old, width, use):
    for n in range(old.shape[-1] // width):
        pl.when(me_ref[1] == n)(partial(use, old[..., width * n : width * (n + 1)]))


def attn_ortho_kernel(rates, me_ref, *refs):
    parts, (nqkv_ref, nout_ref, wqkv_ref, wout_ref, vqkv_ref, vout_ref) = refs[:-6], refs[-6:]
    grams, scales = ortho_start([sum(ref[j] for ref in parts) for j in range(4)])
    factors = sweeps(grams, None, NS_ITERS, True)[1]
    for j in range(4):
        new, old, rate = (nqkv_ref[j], wqkv_ref[j], rates[0]) if j < 3 else (nout_ref[...], wout_ref[...], rates[1])
        ortho = apply_factor(factors[j] * scales[j], new)

        def store(own, j=j, rate=rate, ortho=ortho):
            value = own * (1.0 - rate * WEIGHT_DECAY) - rate * ortho
            if j < 3:
                vqkv_ref[j] = value
            else:
                vout_ref[...] = value

        with_own_columns(me_ref, old, ortho.shape[1], store)


def ffn_ortho_kernel(
    rates, count, me_ref, gin_ref, gback_ref, fin_ref, fback_ref, nin_ref, nback_ref, win_ref, wback_ref, vin_ref, vback_ref
):
    grams, factors = [gin_ref[...], gback_ref[...]], [fin_ref[...], fback_ref[...]]
    factors = sweeps(grams, factors, count, True)[1]
    ortho_in = apply_factor(factors[0], nin_ref[...])
    ortho_back = apply_factor_turned(factors[1], nback_ref[...])

    def store_in(own):
        vin_ref[...] = own * (1.0 - rates[0] * WEIGHT_DECAY) - rates[0] * ortho_in

    def store_back(own):
        vback_ref[...] = own.T * (1.0 - rates[1] * WEIGHT_DECAY) - rates[1] * ortho_back

    with_own_columns(me_ref, win_ref[...], ortho_in.shape[1], store_in)
    with_own_columns(me_ref, wback_ref[...], ortho_back.shape[0], store_back)


def simple_call(kernel, args, shapes, name, flops, after=()):
    def run(*refs):
        kernel(*refs[: len(args)], *refs[len(args) + len(after) :])

    return pl.pallas_call(
        run,
        in_specs=[whole_plain(a) for a in args] + [pl.BlockSpec(memory_space=pl.ANY)] * len(after),
        out_shape=[jax.ShapeDtypeStruct(shape, jnp.float32) for shape in shapes],
        compiler_params=pltpu.CompilerParams(vmem_limit_bytes=LIMIT),
        cost_estimate=estimate(flops, 4e6),
        name=name,
    )(*args, *after)


def whole_plain(array):
    return pl.BlockSpec(memory_space=pltpu.SMEM if array.dtype == jnp.int32 else pltpu.VMEM)


def adam_update(param, earlier_first, earlier_second, gradient):
    first_new = FIRST_DECAY * earlier_first + (1.0 - FIRST_DECAY) * gradient
    second_new = SECOND_DECAY * earlier_second + (1.0 - SECOND_DECAY) * gradient * gradient
    first_fix = 1.0 - FIRST_DECAY**ADAM_STEP
    second_fix = 1.0 - SECOND_DECAY**ADAM_STEP
    direction = first_new / first_fix / (jnp.sqrt(second_new / second_fix) + ADAM_EPS)
    return (first_new, second_new, param - VECTOR_RATE * (direction + WEIGHT_DECAY * param))


def per_device(
    block_in,
    out_grad,
    lengths,
    feature_proj,
    attn_in,
    attn_out,
    ffn_in,
    ffn_out,
    norm_params,
    bias_in,
    bias_out,
    mom_attn_in,
    mom_attn_out,
    mom_ffn_in,
    mom_ffn_out,
    first_norms,
    first_bias_in,
    first_bias_out,
    second_norms,
    second_bias_in,
    second_bias_out,
):
    seqs, length, unused_width = block_in.shape
    wide_size, narrow_size = lax.axis_size("wide"), lax.axis_size("narrow")
    column = lax.axis_index("narrow")
    own_rows, own_cols = D // wide_size, D // narrow_size
    ffn_rows = FF // wide_size
    tiles = ffn_rows // 128 if ffn_rows % 128 == 0 else 1
    unit = ffn_rows // tiles
    width = unit * wide_size
    copied = narrow_size == 4 and own_rows % 16 == 0 and unit % 32 == 0 and (width // narrow_size) % 128 == 0
    blocks = unit == 128 and width // narrow_size == 256 and own_cols == 2 * own_rows
    bf = jnp.bfloat16

    me = jnp.stack([lax.axis_index("wide"), column]).astype(jnp.int32)

    small = jnp.concatenate([norm_params.reshape(-1), bias_in, bias_out]).astype(bf)
    small_size = small.shape[0]
    part = 4 * D // narrow_size
    four = jnp.concatenate([attn_in.astype(bf), attn_out.astype(bf)[None]])
    if part == D:
        four = pick(four, column, 0)
    else:
        four = lax.dynamic_slice_in_dim(four.transpose(1, 0, 2).reshape(own_rows, 4 * D), column * part, part, 1)
    small = jnp.pad(small, (0, -small_size % (8 * part))).reshape(-1, part)
    split = own_rows // 2
    four_gather = Gather(far_wide(jnp.concatenate([four[:split], small, four[split:]])), split)

    in_part = width // narrow_size
    back_part = unit // narrow_size
    folds = D // in_part
    low_in = ffn_in.astype(bf).reshape(own_rows, wide_size, tiles, unit).transpose(2, 0, 1, 3).reshape(tiles, own_rows, width)
    low_in = lax.dynamic_slice_in_dim(low_in, column * in_part, in_part, 2)
    low_back = lax.dynamic_slice_in_dim(ffn_out.reshape(tiles, unit, D), column * back_part, back_part, 1).astype(bf)
    low_back = low_back.reshape(tiles, back_part, folds, in_part).transpose(0, 2, 1, 3).reshape(tiles, own_rows, in_part)
    low_ffn = jnp.concatenate([low_in, low_back], axis=1)

    def as_rows(piece):
        return piece.reshape(-1, folds, back_part, in_part).swapaxes(1, 2).reshape(-1, back_part, D)

    four_gather.near()
    ffn_far = far_wide(tie(low_ffn, *four_gather.pieces[1:]))
    middle_piece = len(ffn_far) // 2
    four_far = four_gather.far(ffn_far[middle_piece])
    four_gather.second_in = tie(four_gather.second_in, *ffn_far[1:])
    four_gather.core()
    ffn_gather = Gather(ffn_far, own_rows, as_rows)
    early = ffn_gather.near(*four_far)
    four_parts = four_gather.mine + list(tie(tuple(four_gather.theirs), *early))
    ms = wide_size // 2
    small_all = in_order(
        four_gather.extra.reshape((-1,) + small.shape), wide_size, 1, lambda w, n: (w & 1) * ms + (w >> 1)
    )
    small_all = small_all.reshape(wide_size, -1)[:, :small_size].astype(jnp.float32)
    norm_all = small_all[:, : 4 * own_rows].reshape(wide_size, 4, own_rows).transpose(1, 0, 2).reshape(4, D)
    bias_in_all = small_all[:, 4 * own_rows : 4 * own_rows + ffn_rows].reshape(wide_size, tiles, unit)
    bias_in_all = bias_in_all.transpose(1, 0, 2).reshape(tiles, 1, width)
    bias_out_all = small_all[:, 4 * own_rows + ffn_rows :].reshape(1, D)
    vectors = jnp.concatenate([norm_all, bias_out_all, jnp.zeros((3, D), jnp.float32)])

    def four_copies(piece, outs, half, w, n):
        return [(piece, outs[0].at[n, pl.ds(w * own_rows + half * split, split)])]

    def ffn_copies(piece, outs, half, w, n):
        if half == 0:
            return [(piece, outs[0].at[:, pl.ds(w * own_rows, own_rows), pl.ds(n * in_part, in_part)])]
        return [(piece, outs[1].at[:, pl.ds(w * unit + n * back_part, back_part)])]

    if copied:
        (weights,) = place(me, four_parts, four_copies, [(4, D, D)], "place_four")
    else:
        weights = jnp.stack([half_in_order(four_parts, half) for half in range(2)], axis=2)
        weights = weights.transpose(0, 2, 3, 1, 4).reshape(D, 4, D).transpose(1, 0, 2)

    cosine, sine = rotary_blocks(length)
    proj, projt = projection_blocks(feature_proj)
    middle, h1, h2, *kept, mixed = attend(lengths, block_in, weights, vectors, proj, cosine, sine, [])
    ffn_gather.far()
    ffn_gather.core(middle)
    ffn_parts = ffn_gather.mine + ffn_gather.theirs
    if copied:
        w_in, w_back = place(me, ffn_parts, ffn_copies, [(tiles, D, width), (tiles, width, D)], "place_ffn")
    else:
        w_in = half_in_order(ffn_parts, 0).transpose(2, 0, 3, 1, 4).reshape(tiles, D, width)
        w_back = half_in_order(ffn_parts, 1).transpose(2, 0, 1, 3, 4).reshape(tiles, width, D)
    past, token = None, []
    streams, bias_sums = [], []
    orders = ["yzx", "yxa", "xya"]
    for tile in range(tiles):
        ffn, grad_h2, bias_sum, *grad_tile = ffn_tile(
            tile, h2, out_grad, w_in, w_back, bias_in_all[tile : tile + 1], me, past, wide_size, narrow_size, blocks, token
        )
        past = (ffn, grad_h2)
        bias_sums.append(bias_sum)
        token = [fold_streams(streams[:1], me, [bias_sum])] if tile == 1 else []
        if blocks:
            keep, *send = grad_tile
            streams.append(Stream(keep, core_swap(send), orders[tile % 3]))
        else:
            grad_in = grad_tile[0][0].reshape(wide_size, own_rows, narrow_size, in_part).transpose(2, 0, 1, 3)
            grad_back = grad_tile[0][1].reshape(narrow_size, own_cols, wide_size, unit).transpose(0, 2, 1, 3)
            for found, order in ((grad_in, "yxz"), (grad_back, "xyz")):
                found = found.reshape((narrow_size // 2, 2) + found.shape[1:])
                arrived = core_swap(cut_wide(pick(found, 1 - (column & 1), 1)))
                streams.append(Stream(pick(found, column & 1, 1), arrived, order))
    ffn = tie(ffn, *streams[0].parts[1:])
    block_out, grad_middle, gb, sums_two = middle_back(out_grad, grad_h2, ffn, middle, vectors, narrow_size)

    def fold_open(more, after):
        found = more + [stream for stream in streams if stream.order]
        done = [part for stream in streams if not stream.order for part in stream.parts]
        return fold_streams(found, me, after + done)

    token = fold_open([], [sums_two])
    gq, gk, gv = attend_back(lengths, grad_middle, weights, projt, cosine, sine, kept, narrow_size, [token])
    token = fold_open([], [gq])
    send = attn_weights(me, h1, mixed, (gq, gk, gv, gb), wide_size, 1, [token])
    (keep,) = attn_weights(me, h1, mixed, (gq, gk, gv, gb), wide_size, 0, send[:1])
    arrived = core_swap(send)
    left = Stream(keep, arrived, "xzy", (0, own_rows))
    right = Stream(keep, arrived, "yxz", (own_rows, 2 * own_rows))
    token = fold_open([left, right], [keep])
    input_grad, sums_one = input_back(block_in, grad_middle, (gq, gk, gv), weights, vectors, [token])

    norm_sums = jnp.concatenate([sums_one[:2], sums_two[:2], sums_two[2:3]])
    inner_sums = jnp.concatenate(bias_sums).reshape(tiles, wide_size, unit).transpose(1, 0, 2)
    inner_sums = inner_sums.reshape(wide_size, narrow_size, ffn_rows // narrow_size)
    norm_part = own_rows // narrow_size
    norm_sums = norm_sums.reshape(5, wide_size, narrow_size, norm_part).transpose(1, 2, 0, 3).reshape(wide_size, narrow_size, -1)
    vector_parts = jnp.concatenate([norm_sums, inner_sums], axis=2).swapaxes(0, 1)
    vector_size = vector_parts.shape[2]
    vector_parts = jnp.pad(vector_parts, ((0, 0), (0, 0), (0, -vector_size % 128)))
    vector_parts = vector_parts.reshape(narrow_size // 2, 2, wide_size, 1, -1)
    vector_send = tie(pick(vector_parts, 1 - (column & 1), 1), *left.parts[1:], *right.parts[1:])
    vector = Stream(pick(vector_parts, column & 1, 1), core_swap([vector_send]), "yxz")
    token = fold_streams([left, right, vector], me, [sums_one])
    sum_parts = [stream.last() for stream in streams]
    small_size, large_size = padded(own_rows), padded(ffn_rows)
    block_count = len(block_pairs(large_size // 128)) + small_size // 128
    grad_in_w, grad_back_w, mom_in_new, mom_back_new, blocks_gram = simple_call(
        partial(ffn_moment_kernel, [len(parts) for parts in sum_parts], unit),
        [mom_ffn_in, mom_ffn_out.T] + sum(sum_parts, []),
        [mom_ffn_in.shape, mom_ffn_out.T.shape] * 2 + [(block_count, 128, 128)],
        "ffn_moment",
        1e9,
        [token],
    )
    token = fold_streams([left, right, vector], me, [mom_in_new])
    blocks_gram = tie(blocks_gram, token)
    blocks_near = blocks_gram + swap(blocks_gram, "narrow", 1)
    blocks_all = [blocks_near] + [swap(blocks_near, "narrow", mask) for mask in far_masks("narrow")]
    token = fold_streams([vector], me, [blocks_near])
    left_parts, right_parts = left.last(), right.last()
    def own_columns(weight):
        block_width = weight.shape[-1] // narrow_size
        return lax.dynamic_slice_in_dim(
            weight, column * block_width, block_width, axis=weight.ndim - 1
        )

    rate_qkv = MUON_SCALE
    rate_out = MUON_SCALE * math.sqrt(D / (D // 64))
    rate_in = MUON_SCALE * math.sqrt(FF / D)
    rate_back = MUON_SCALE * math.sqrt(D / FF)
    shapes = [mom_attn_in.shape, mom_attn_out.shape]
    grad_qkv, grad_out_w, mom_qkv_new, mom_out_new, gram_four = simple_call(
        partial(attn_moment_kernel, (len(left_parts), len(right_parts))),
        [mom_attn_in, mom_attn_out] + left_parts + right_parts,
        shapes + shapes + [(4, padded(own_rows), padded(own_rows))],
        "attn_moment",
        1e9,
        [token],
    )
    gram_near = gram_four + swap(gram_four, "narrow", 1)
    sweep_in, sweep_back, factor_in, factor_back = simple_call(
        partial(sweep_kernel, 2),
        blocks_all,
        [(small_size, small_size), (large_size, large_size)] * 2,
        "ffn_sweeps",
        1e10,
        [gram_four],
    )
    vector_sums = sum(jnp.sum(part, axis=0) for part in vector.last())[0, :vector_size]
    grad_norm_vals = vector_sums[: 4 * norm_part].reshape(4, norm_part)
    grad_bias_final = vector_sums[4 * norm_part : 5 * norm_part]
    grad_bias_inner = vector_sums[5 * norm_part :]
    gram_all = [gram_near] + [swap(gram_near, "narrow", mask) for mask in far_masks("narrow")]
    new_in, new_back = simple_call(
        partial(ffn_ortho_kernel, (rate_in, rate_back), NS_ITERS - 2),
        [me, sweep_in, sweep_back, factor_in, factor_back, mom_in_new, mom_back_new, ffn_in, ffn_out],
        [mom_ffn_in.shape, mom_ffn_out.T.shape],
        "ffn_ortho",
        1e10,
        [gram_near],
    )
    new_qkv, new_out = simple_call(
        partial(attn_ortho_kernel, (rate_qkv, rate_out)),
        [me, *gram_all, mom_qkv_new, mom_out_new, attn_in, attn_out],
        shapes,
        "attn_ortho",
        5e9,
        [new_in],
    )
    norm_first, norm_second, norm_new = adam_update(
        own_columns(norm_params), first_norms, second_norms, grad_norm_vals
    )
    inner_first, inner_second, inner_new = adam_update(
        own_columns(bias_in), first_bias_in, second_bias_in, grad_bias_inner
    )
    final_first, final_second, final_new = adam_update(
        own_columns(bias_out), first_bias_out, second_bias_out, grad_bias_final
    )
    return (
        block_out,
        input_grad,
        grad_qkv,
        grad_out_w,
        grad_in_w,
        grad_back_w.T,
        grad_norm_vals,
        grad_bias_inner,
        grad_bias_final,
        mom_qkv_new,
        mom_out_new,
        mom_in_new,
        mom_back_new.T,
        new_qkv,
        new_out,
        new_in,
        new_back.T,
        norm_first,
        inner_first,
        final_first,
        norm_second[:2],
        norm_second[2:],
        inner_second,
        final_second,
        norm_new,
        inner_new,
        final_new,
    )


def solution(mesh):
    in_specs = (
        P(("wide", "narrow"), None, None),
        P(("wide", "narrow"), None, None),
        P(("wide", "narrow")),
        P(),
        P(None, "wide", None),
        P("wide", None),
        P("wide", None),
        P("wide", None),
        P(None, "wide"),
        P("wide"),
        P("wide"),
        P(None, "wide", "narrow"),
        P("wide", "narrow"),
        P("wide", "narrow"),
        P("wide", "narrow"),
        P(None, ("wide", "narrow")),
        P(("wide", "narrow")),
        P(("wide", "narrow")),
        P(None, ("wide", "narrow")),
        P(("wide", "narrow")),
        P(("wide", "narrow")),
    )
    out_specs = (
        P(("wide", "narrow"), None, None),
        P(("wide", "narrow"), None, None),
        P(None, "wide", "narrow"),
        P("wide", "narrow"),
        P("wide", "narrow"),
        P("wide", "narrow"),
        P(None, ("wide", "narrow")),
        P(("wide", "narrow")),
        P(("wide", "narrow")),
        P(None, "wide", "narrow"),
        P("wide", "narrow"),
        P("wide", "narrow"),
        P("wide", "narrow"),
        P(None, "wide", "narrow"),
        P("wide", "narrow"),
        P("wide", "narrow"),
        P("wide", "narrow"),
        P(None, ("wide", "narrow")),
        P(("wide", "narrow")),
        P(("wide", "narrow")),
        P(None, ("wide", "narrow")),
        P(None, ("wide", "narrow")),
        P(("wide", "narrow")),
        P(("wide", "narrow")),
        P(None, ("wide", "narrow")),
        P(("wide", "narrow")),
        P(("wide", "narrow")),
    )
    return jax.shard_map(
        per_device, mesh=mesh, in_specs=in_specs, out_specs=out_specs, check_vma=False
    )
```

```python
from functools import partial
import math

import jax
import jax.numpy as jnp
from jax import lax
from jax.experimental import pallas as pl
from jax.experimental.pallas import tpu as pltpu
from jax.sharding import PartitionSpec as P

D = 768
FF = 3072
HEADS = 12
HDIM = 64
FEAT = 32
NS_ITERS = 5
ADAM_STEP = 10


PRECISE = lax.Precision.HIGHEST
NORM_EPS = 1e-05
ORTHO_EPS = 1e-07
ADAM_EPS = 1e-08
LINEAR_COEF = 3.4445
CUBIC_COEF = -4.775
QUINTIC_COEF = 2.0315
MOMENT_DECAY = 0.5
FIRST_DECAY = 0.5
SECOND_DECAY = 0.5
MUON_SCALE = 0.6
WEIGHT_DECAY = 0.01
VECTOR_RATE = 0.4
GROUP = 4
GROUPS = HEADS // GROUP
GE = GROUP * HDIM
GF = GROUP * FEAT


def mm(left, right):
    return jnp.dot(left, right, preferred_element_type=jnp.float32)


def mm_nt(left, right):
    return lax.dot_general(left, right, (((1,), (1,)), ((), ())), preferred_element_type=jnp.float32)


def mm_tn(left, right):
    return lax.dot_general(left, right, (((0,), (0,)), ((), ())), preferred_element_type=jnp.float32)


def halves(value):
    high = value.astype(jnp.bfloat16)
    return high, (value - high.astype(jnp.float32)).astype(jnp.bfloat16)


def normalise(rows):
    centered = rows - jnp.mean(rows, axis=-1, keepdims=True)
    inverse = lax.rsqrt(jnp.mean(centered * centered, axis=-1, keepdims=True) + NORM_EPS)
    return centered * inverse, inverse


def norm_pull(normed, inverse, grad, gain):
    scaled = grad * gain
    mean_plain = jnp.mean(scaled, axis=-1, keepdims=True)
    mean_prod = jnp.mean(scaled * normed, axis=-1, keepdims=True)
    return inverse * (scaled - mean_plain - normed * mean_prod)


def partner_of(values):
    lane = lax.broadcasted_iota(jnp.int32, (values.shape[0], 128), 1)
    first = (lane & (HDIM - 1)) < HDIM // 2
    parts = []
    for at in range(0, values.shape[1], 128):
        block = values[:, at : at + 128]
        ahead = pltpu.roll(block, 128 - HDIM // 2, 1)
        behind = pltpu.roll(block, HDIM // 2, 1)
        parts.append(jnp.where(first, ahead, behind))
    return jnp.concatenate(parts, axis=1)


def head_mask(rows, columns, row_width, column_width):
    row = lax.broadcasted_iota(jnp.int32, (rows, columns), 0) // row_width
    column = lax.broadcasted_iota(jnp.int32, (rows, columns), 1) // column_width
    return row == column


def store_columns(ref, values):
    width = ref.shape[3]
    for n in range(ref.shape[0]):
        ref[n, 0] = values[:, width * n : width * (n + 1)].astype(ref.dtype)


def load_columns(ref):
    return jnp.concatenate([ref[n, 0] for n in range(ref.shape[0])], axis=1)


def attend_kernel(
    lengths_ref, x_ref, w_ref, vec_ref, proj_ref, cos_ref, sin_ref,
    middle_ref, h1_ref, h2_ref, wq_ref, wk_ref, pq_ref, pk_ref, v_ref, state_ref, total_ref, att_ref, rden_ref, mixed_ref,
):
    rows = x_ref.shape[1]
    x = x_ref[0].astype(jnp.float32)
    h1 = (normalise(x)[0] * vec_ref[0:1, :] + vec_ref[1:2, :]).astype(jnp.bfloat16)
    h1_ref[0] = h1
    live = lax.broadcasted_iota(jnp.int32, (rows, 1), 0) < lengths_ref[pl.program_id(0)]
    live = live.astype(jnp.float32)
    cosine = jnp.concatenate([cos_ref[...]] * (D // 128), axis=1)
    sine = jnp.concatenate([sin_ref[...]] * (D // 128), axis=1)
    values = mm(h1, w_ref[2]).astype(jnp.bfloat16)
    v_ref[0] = values
    feats = []
    for j, (w_out, p_out) in enumerate(((wq_ref, pq_ref), (wk_ref, pk_ref))):
        heads = mm(h1, w_ref[j])
        unit = (heads * cosine + partner_of(heads) * sine) * HDIM ** (-0.25)
        w_out[0] = unit
        high, low = halves(unit)
        sq_high, sq_low = halves(unit * unit)
        parts = []
        for g in range(GROUPS):
            cut = slice(GE * g, GE * (g + 1))
            left = jnp.concatenate([high[:, cut], low[:, cut], high[:, cut], sq_high[:, cut], sq_low[:, cut]], axis=1)
            parts.append(jnp.exp(mm(left, proj_ref[g])) * FEAT ** (-0.5))
        phi = jnp.concatenate(parts, axis=1)
        p_out[0] = phi
        feats.append(phi)
    query_low = feats[0].astype(jnp.bfloat16)
    key_vals = feats[1].astype(jnp.bfloat16).astype(jnp.float32) * live
    key_low = key_vals.astype(jnp.bfloat16)
    total_ref[0] = jnp.sum(key_vals, axis=0, keepdims=True)
    mask = head_mask(GF, GE, FEAT, HDIM)
    ones = jnp.ones((rows, GE), jnp.bfloat16)
    attended, inverse_den = [], []
    for g in range(GROUPS):
        cut = slice(GE * g, GE * (g + 1))
        fcut = slice(GF * g, GF * (g + 1))
        both = mm_tn(key_low[:, fcut], jnp.concatenate([values[:, cut], ones], axis=1))
        state = jnp.where(mask, both[:, :GE], 0.0).astype(jnp.bfloat16)
        state_ref[0, g] = state
        tot_high, tot_low = halves(jnp.where(mask, both[:, GE:], 0.0))
        query = query_low[:, fcut]
        numer = mm(query, state)
        denom = mm(jnp.concatenate([query, query], axis=1), jnp.concatenate([tot_high, tot_low], axis=0))
        inverse = 1.0 / denom
        attended.append(numer * inverse)
        inverse_den.append(inverse)
    attended = jnp.concatenate(attended, axis=1)
    att_ref[0] = attended
    rden_ref[0] = jnp.concatenate(inverse_den, axis=1)
    mixed = attended.astype(jnp.bfloat16)
    mixed_ref[0] = mixed
    middle = x + mm(mixed, w_ref[3])
    middle_ref[0] = middle
    h2_ref[0] = (normalise(middle)[0] * vec_ref[2:3, :] + vec_ref[3:4, :]).astype(jnp.bfloat16)


def output_kernel(ffn_ref, middle_ref, vec_ref, out_ref):
    out_ref[0] = middle_ref[0] + (ffn_ref[0] + vec_ref[4:5, :])


def middle_back_kernel(og_ref, gh2_ref, middle_ref, vec_ref, gm_ref, gb_ref, sums_ref):
    og = og_ref[0].astype(jnp.float32)
    middle = middle_ref[0]
    grad_h2 = gh2_ref[0]
    normed, inverse = normalise(middle)
    grad_middle = og + norm_pull(normed, inverse, grad_h2, vec_ref[2:3, :])
    gm_ref[0] = grad_middle
    store_columns(gb_ref, grad_middle)

    @pl.when(pl.program_id(0) == 0)
    def _():
        sums_ref[...] = jnp.zeros_like(sums_ref)

    sums_ref[0:1, :] += jnp.sum(grad_h2 * normed, axis=0, keepdims=True)
    sums_ref[1:2, :] += jnp.sum(grad_h2, axis=0, keepdims=True)
    sums_ref[2:3, :] += jnp.sum(og, axis=0, keepdims=True)


def attend_back_kernel(
    lengths_ref, gm_ref, w_ref, projt_ref, cos_ref, sin_ref,
    wq_ref, wk_ref, pq_ref, pk_ref, v_ref, state_ref, total_ref, att_ref, rden_ref,
    gq_ref, gk_ref, gv_ref,
):
    rows = gm_ref.shape[1]
    branch = gm_ref[0].astype(jnp.bfloat16)
    grad_numer = mm_nt(branch, w_ref[0]) * rden_ref[0]
    gn_high, gn_low = halves(grad_numer)
    pr_high, pr_low = halves(grad_numer * att_ref[0])
    live = (lax.broadcasted_iota(jnp.int32, (rows, 1), 0) < lengths_ref[pl.program_id(0)]).astype(jnp.float32)
    query_low = pq_ref[0].astype(jnp.bfloat16)
    key_low = (pk_ref[0].astype(jnp.bfloat16).astype(jnp.float32) * live).astype(jnp.bfloat16)
    mask = head_mask(GF, GE, FEAT, HDIM)
    spread = head_mask(GE, GF, HDIM, FEAT).astype(jnp.float32).astype(jnp.bfloat16)
    spread2 = jnp.concatenate([spread, spread], axis=0)
    gather = mask.astype(jnp.float32).astype(jnp.bfloat16)
    gather2 = jnp.concatenate([gather, gather], axis=0)
    grad_u = ([], [])
    grad_v = []
    for g in range(GROUPS):
        cut = slice(GE * g, GE * (g + 1))
        fcut = slice(GF * g, GF * (g + 1))
        query, key, values = query_low[:, fcut], key_low[:, fcut], v_ref[0, :, cut]
        state = state_ref[0, g]
        grad_denom = -mm(jnp.concatenate([pr_high[:, cut], pr_low[:, cut]], axis=1), spread2)
        two = jnp.concatenate([gn_high[:, cut], gn_low[:, cut]], axis=1)
        grad_qfeat = mm_nt(two, jnp.concatenate([state, state], axis=1)) + grad_denom * total_ref[0, :, fcut]
        pair = mm_tn(query, two)
        grad_state = jnp.where(mask, pair[:, :GE] + pair[:, GE:], 0.0)
        grad_total = jnp.sum(grad_denom * query.astype(jnp.float32), axis=0, keepdims=True)
        gs_high, gs_low = halves(grad_state)
        grad_kfeat = mm_nt(
            jnp.concatenate([values, values], axis=1), jnp.concatenate([gs_high, gs_low], axis=1)
        )
        grad_kfeat = (grad_kfeat + grad_total) * live
        grad_v.append(mm(jnp.concatenate([key, key], axis=1), jnp.concatenate([gs_high, gs_low], axis=0)))
        for j, (grad_feat, p_in, w_in) in enumerate(((grad_qfeat, pq_ref, wq_ref), (grad_kfeat, pk_ref, wk_ref))):
            t_high, t_low = halves(grad_feat * p_in[0, :, fcut])
            pulled = mm(jnp.concatenate([t_high, t_low, t_high], axis=1), projt_ref[g])
            weight = mm(jnp.concatenate([t_high, t_low], axis=1), gather2)
            grad_u[j].append((pulled - weight * w_in[0, :, cut]) * HDIM ** (-0.25))
    cosine = jnp.concatenate([cos_ref[...]] * (D // 128), axis=1)
    sine = jnp.concatenate([sin_ref[...]] * (D // 128), axis=1)
    for grads, ref in zip(grad_u, (gq_ref, gk_ref)):
        turned = jnp.concatenate(grads, axis=1)
        store_columns(ref, turned * cosine - partner_of(turned) * sine)
    store_columns(gv_ref, jnp.concatenate(grad_v, axis=1))


def input_back_kernel(x_ref, gm_ref, gq_ref, gk_ref, gv_ref, w_ref, vec_ref, out_ref, sums_ref):
    grad_h1 = sum(mm_nt(load_columns(ref), w_ref[j]) for j, ref in enumerate((gq_ref, gk_ref, gv_ref)))
    normed, inverse = normalise(x_ref[0].astype(jnp.float32))
    out_ref[0] = gm_ref[0] + norm_pull(normed, inverse, grad_h1, vec_ref[0:1, :])

    @pl.when(pl.program_id(0) == 0)
    def _():
        sums_ref[...] = jnp.zeros_like(sums_ref)

    sums_ref[0:1, :] += jnp.sum(grad_h1 * normed, axis=0, keepdims=True)
    sums_ref[1:2, :] += jnp.sum(grad_h1, axis=0, keepdims=True)


def attn_weight_kernel(me_ref, h1_ref, mixed_ref, gq_ref, gk_ref, gv_ref, gb_ref, *out_refs):
    width, rows = out_refs[0].shape[1], out_refs[0].shape[2] // 2
    h1 = h1_ref[...]
    left = mm_tn(h1, jnp.concatenate([gq_ref[...], gk_ref[...]], axis=1)).astype(jnp.bfloat16)
    right = jnp.concatenate([mm_tn(h1, gv_ref[...]), mm_tn(mixed_ref[...], gb_ref[...])], axis=1).astype(jnp.bfloat16)
    for w in range(width * len(out_refs)):
        out_refs[w // width][0, w % width, :rows] = left[rows * w : rows * (w + 1)]
        out_refs[w // width][0, w % width, rows:] = right[rows * w : rows * (w + 1)]


def ffn_kernel(has_past, blocks, h2_ref, og_ref, win_ref, wback_ref, bias_ref, me_ref, *rest):
    if has_past:
        out_past_ref, gh2_past_ref, *rest = rest
    if blocks:
        out_ref, gh2_ref, bsum_ref, keep_ref, *send_refs, act_ref, gi_ref, gw_ref = rest
    else:
        out_ref, gh2_ref, bsum_ref, gw_ref, act_ref, gi_ref = rest
    seqs, rows = out_ref.shape[0], out_ref.shape[1]
    step = pl.program_id(0)
    win, wback = win_ref[...], wback_ref[...]
    bias = bias_ref[...]

    def part(s, carry):
        span = pl.ds(pl.multiple_of(s * rows, rows), rows)
        inner = mm(h2_ref[s], win) + bias
        grad_act = mm_nt(og_ref[s], wback)
        cdf = 0.5 * (1.0 + lax.erf(inner * (2.0**-0.5)))
        pdf = jnp.exp(-0.5 * inner * inner) * (2.0 * math.pi) ** -0.5
        act = (inner * cdf).astype(jnp.bfloat16)
        grad_inner = (grad_act * (cdf + inner * pdf)).astype(jnp.bfloat16)
        act_ref[span, :] = act
        gi_ref[span, :] = grad_inner
        out_part = mm(act, wback)
        gh2_part = mm_nt(grad_inner, win)

        @pl.when(step == 0)
        def _():
            if has_past:
                out_ref[s] = out_past_ref[s] + out_part
                gh2_ref[s] = gh2_past_ref[s] + gh2_part
            else:
                out_ref[s] = out_part
                gh2_ref[s] = gh2_part

        @pl.when(step > 0)
        def _():
            out_ref[s] += out_part
            gh2_ref[s] += gh2_part

        return carry + jnp.sum(grad_inner.astype(jnp.float32), axis=0, keepdims=True)

    bsum_ref[...] = lax.fori_loop(0, seqs, part, jnp.zeros(bias.shape, jnp.float32), unroll=True)
    h2 = h2_ref[...].reshape(seqs * rows, D)
    og = og_ref[...].reshape(seqs * rows, D)
    grad_in = mm_tn(h2, gi_ref[...]).astype(jnp.bfloat16)
    grad_back = mm_tn(og, act_ref[...]).astype(jnp.bfloat16)
    if not blocks:
        gw_ref[0] = grad_in
        gw_ref[1] = grad_back
        return
    narrow, wide = gw_ref.shape[0], gw_ref.shape[1]
    in_rows, in_cols = D // wide, gw_ref.shape[3]
    width = grad_in.shape[1]
    for k in range(width // in_cols):
        for w in range(wide):
            gw_ref[step * (width // in_cols) + k, w, :in_rows, :] = grad_in[
                in_rows * w : in_rows * (w + 1), in_cols * k : in_cols * (k + 1)
            ]
    back_rows = D // narrow
    half = back_rows // 2
    for k in range(width // 128):
        for n in range(narrow):
            for h in range(2):
                gw_ref[n, step * (width // 128) + k, in_rows:, 128 * h : 128 * (h + 1)] = grad_back[
                    back_rows * n + half * h : back_rows * n + half * (h + 1), 128 * k : 128 * (k + 1)
                ]

    @pl.when(step == pl.num_programs(0) - 1)
    def _():
        side = me_ref[1] & 1
        for far in range(narrow // 2):
            for w in range(wide):
                keep_ref[far, w] = gw_ref[2 * far + side, w]
                width = wide // len(send_refs)
                send_refs[w // width][far, w % width] = gw_ref[2 * far + (1 - side), w]


def spec(shape, index):
    return pl.BlockSpec(shape, index)


LIMIT = 60 * 1024 * 1024
ANYWHERE = pl.BlockSpec(memory_space=pl.ANY)


def skipping(kernel, before, extra):
    def run(*refs):
        return kernel(*refs[:before], *refs[before + extra :])

    return run


def estimate(flops, moved, transcendentals=0):
    return pl.CostEstimate(flops=int(flops), bytes_accessed=int(moved), transcendentals=int(transcendentals))


def whole(array):
    rank = array.ndim
    return pl.BlockSpec(array.shape, lambda *unused: (0,) * rank)


def by_seq(shape):
    rank = len(shape)
    return pl.BlockSpec((1,) + tuple(shape[1:]), lambda s, *unused: (s,) + (0,) * (rank - 1))


def by_seq_second(shape):
    rank = len(shape)
    return pl.BlockSpec((shape[0], 1) + tuple(shape[2:]), lambda s, *unused: (0, s) + (0,) * (rank - 2))


def attend(lengths, x, weights, vectors, proj, cosine, sine, after):
    seqs, rows, unused_width = x.shape
    bf, f4 = jnp.bfloat16, jnp.float32
    shapes = [
        ((seqs, rows, D), f4), ((seqs, rows, D), bf), ((seqs, rows, D), bf), ((seqs, rows, D), f4), ((seqs, rows, D), f4),
        ((seqs, rows, HEADS * FEAT), f4), ((seqs, rows, HEADS * FEAT), f4), ((seqs, rows, D), bf),
        ((seqs, GROUPS, GF, GE), bf), ((seqs, 1, HEADS * FEAT), f4), ((seqs, rows, D), f4), ((seqs, rows, D), f4),
        ((seqs, rows, D), bf),
    ]
    return pl.pallas_call(
        skipping(attend_kernel, 7, len(after)),
        grid_spec=pltpu.PrefetchScalarGridSpec(
            num_scalar_prefetch=1,
            grid=(seqs,),
            in_specs=[by_seq(x.shape)] + [whole(a) for a in (weights, vectors, proj, cosine, sine)]
            + [ANYWHERE] * len(after),
            out_specs=[by_seq(shape) for shape, unused in shapes],
        ),
        out_shape=[jax.ShapeDtypeStruct(shape, dtype) for shape, dtype in shapes],
        compiler_params=pltpu.CompilerParams(vmem_limit_bytes=LIMIT),
        cost_estimate=estimate(seqs * rows * D * D * 6, 20e6),
        name="attend",
    )(lengths, x, weights, vectors, proj, cosine, sine, *after)


def layer_output(ffn, middle, vectors, after):
    return pl.pallas_call(
        skipping(output_kernel, 3, len(after)),
        grid=(ffn.shape[0],),
        in_specs=[by_seq(ffn.shape)] * 2 + [whole(vectors)] + [ANYWHERE] * len(after),
        out_specs=by_seq(ffn.shape),
        out_shape=jax.ShapeDtypeStruct(ffn.shape, jnp.float32),
        compiler_params=pltpu.CompilerParams(vmem_limit_bytes=LIMIT),
        cost_estimate=estimate(1e6, 8e6),
        name="layer_output",
    )(ffn, middle, vectors, *after)


def middle_back(og, grad_h2, middle, vectors, narrow_size):
    seqs, rows, unused_width = og.shape
    blocked = (narrow_size, seqs, rows, D // narrow_size)
    full = jax.ShapeDtypeStruct(og.shape, jnp.float32)
    return pl.pallas_call(
        middle_back_kernel,
        grid=(seqs,),
        in_specs=[by_seq(og.shape)] * 3 + [whole(vectors)],
        out_specs=[by_seq(og.shape)] + [by_seq_second(blocked), pl.BlockSpec((8, D), lambda s: (0, 0))],
        out_shape=[full, jax.ShapeDtypeStruct(blocked, jnp.bfloat16), jax.ShapeDtypeStruct((8, D), jnp.float32)],
        compiler_params=pltpu.CompilerParams(vmem_limit_bytes=LIMIT),
        cost_estimate=estimate(1e7, 16e6),
        name="middle_back",
    )(og, grad_h2, middle, vectors)


def attend_back(lengths, grad_middle, weights, projt, cosine, sine, kept, narrow_size, after):
    seqs, rows, unused_width = grad_middle.shape
    blocked = (narrow_size, seqs, rows, D // narrow_size)
    count = 6 + len(kept)
    return pl.pallas_call(
        skipping(attend_back_kernel, count, len(after)),
        grid_spec=pltpu.PrefetchScalarGridSpec(
            num_scalar_prefetch=1,
            grid=(seqs,),
            in_specs=[by_seq(grad_middle.shape), pl.BlockSpec((1, D, D), lambda s, *unused: (3, 0, 0))]
            + [whole(a) for a in (projt, cosine, sine)]
            + [by_seq(a.shape) for a in kept]
            + [ANYWHERE] * len(after),
            out_specs=[by_seq_second(blocked)] * 3,
        ),
        out_shape=[jax.ShapeDtypeStruct(blocked, jnp.bfloat16)] * 3,
        compiler_params=pltpu.CompilerParams(vmem_limit_bytes=LIMIT),
        cost_estimate=estimate(seqs * rows * D * D * 8, 40e6),
        name="attend_back",
    )(lengths, grad_middle, weights, projt, cosine, sine, *kept, *after)


def input_back(x, grad_middle, grads, weights, vectors, after):
    seqs, rows, unused_width = x.shape
    return pl.pallas_call(
        skipping(input_back_kernel, 4 + len(grads), len(after)),
        grid=(seqs,),
        in_specs=[by_seq(x.shape), by_seq(x.shape)] + [by_seq_second(a.shape) for a in grads] + [whole(weights), whole(vectors)] + [ANYWHERE] * len(after),
        out_specs=[by_seq(x.shape), pl.BlockSpec((8, D), lambda s: (0, 0))],
        out_shape=[jax.ShapeDtypeStruct(x.shape, jnp.float32), jax.ShapeDtypeStruct((8, D), jnp.float32)],
        compiler_params=pltpu.CompilerParams(vmem_limit_bytes=LIMIT),
        cost_estimate=estimate(seqs * rows * D * D * 6, 15e6),
        name="input_back",
    )(x, grad_middle, *grads, weights, vectors, *after)


def attn_weights(me, h1, mixed, grads, wide_size, side, after):
    narrow_size, seqs, rows, width = grads[0].shape
    tokens = seqs * rows
    flat = [a.reshape(narrow_size, tokens, width) for a in grads]
    h1, mixed = h1.reshape(tokens, D), mixed.reshape(tokens, D)
    count = 2 if side else 1
    shape = (narrow_size // 2, wide_size // count, 2 * D // wide_size, 2 * width)

    def block_at(i, me_ref):
        return (2 * i + ((me_ref[1] & 1) ^ side), 0, 0)

    return pl.pallas_call(
        skipping(attn_weight_kernel, 7, len(after)),
        grid_spec=pltpu.PrefetchScalarGridSpec(
            num_scalar_prefetch=1,
            grid=(narrow_size // 2,),
            in_specs=[whole(h1), whole(mixed)] + [pl.BlockSpec((None, tokens, width), block_at)] * 4 + [ANYWHERE] * len(after),
            out_specs=[pl.BlockSpec((1,) + shape[1:], lambda i, *unused: (i, 0, 0, 0))] * count,
        ),
        out_shape=[jax.ShapeDtypeStruct(shape, jnp.bfloat16)] * count,
        compiler_params=pltpu.CompilerParams(vmem_limit_bytes=LIMIT),
        cost_estimate=estimate(tokens * D * D * 4, 8e6),
        name="attn_weights",
    )(me, h1, mixed, *flat, *after)


def ffn_tile(tile, h2, og, w_in, w_back, bias, me, past, wide_size, narrow_size, blocks, after):
    seqs, rows, unused_width = h2.shape
    width = w_in.shape[2]
    step = 1024 if width % 1024 == 0 else width
    tokens = jax.ShapeDtypeStruct(h2.shape, jnp.float32)
    out_specs = [whole(h2), whole(h2), pl.BlockSpec((1, step), lambda i: (0, i))]
    out_shape = [tokens, tokens, jax.ShapeDtypeStruct((1, width), jnp.float32)]
    scratch = [pltpu.VMEM((seqs * rows, step), jnp.bfloat16)] * 2
    if blocks:
        block = (2 * D // wide_size, width // narrow_size)
        half = jax.ShapeDtypeStruct((narrow_size // 2, wide_size) + block, jnp.bfloat16)
        part = jax.ShapeDtypeStruct((narrow_size // 2, wide_size // 4) + block, jnp.bfloat16)
        out_specs += [whole(half)] + [whole(part)] * 4
        out_shape += [half] + [part] * 4
        scratch.append(pltpu.VMEM((narrow_size, wide_size) + block, jnp.bfloat16))
    else:
        out_specs.append(pl.BlockSpec((2, D, step), lambda i: (0, 0, i)))
        out_shape.append(jax.ShapeDtypeStruct((2, D, width), jnp.bfloat16))
    return pl.pallas_call(
        skipping(partial(ffn_kernel, past is not None, blocks), 6 + len(past or ()), len(after)),
        grid=(width // step,),
        in_specs=[
            whole(h2),
            whole(og),
            pl.BlockSpec((None, D, step), lambda i: (tile, 0, i)),
            pl.BlockSpec((None, step, D), lambda i: (tile, i, 0)),
            pl.BlockSpec((None, 1, step), lambda i: (0, 0, i)),
            pl.BlockSpec(memory_space=pltpu.SMEM),
        ]
        + [whole(a) for a in past or ()]
        + [ANYWHERE] * len(after),
        out_specs=out_specs,
        out_shape=out_shape,
        scratch_shapes=scratch,
        compiler_params=pltpu.CompilerParams(vmem_limit_bytes=LIMIT),
        cost_estimate=estimate(seqs * rows * D * width * 12, 20e6, seqs * rows * width * 2),
        name="ffn_tile",
    )(h2, og, w_in, w_back, bias, me, *(past or ()), *after)


def rotary_blocks(length):
    half = HDIM // 2
    frequency = jnp.exp(jnp.arange(half, dtype=jnp.float32) * (-2.0 * math.log(10000.0) / HDIM))
    angles = jnp.arange(length, dtype=jnp.float32)[:, None] * frequency[None, :]
    cosine, sine = jnp.cos(angles), jnp.sin(angles)
    return jnp.tile(cosine, (1, 4)), jnp.tile(jnp.concatenate([-sine, sine], axis=1), (1, 2))


def projection_blocks(feature_proj):
    rows = jnp.arange(GF)[:, None] // FEAT
    columns = jnp.arange(GE)[None, :] // HDIM
    mask = (rows == columns).astype(jnp.float32)
    tall = jnp.tile(feature_proj.reshape(GROUPS, GF, HDIM), (1, 1, GROUP)) * mask
    high, low = halves(tall)
    square = jnp.broadcast_to(-0.5 * mask, tall.shape).astype(jnp.bfloat16)
    turned = [a.swapaxes(1, 2) for a in (high, high, low, square, square)]
    return jnp.concatenate(turned, axis=1), jnp.concatenate([high, high, low], axis=1)


def xor_pairs(size, mask):
    return [(index, index ^ mask) for index in range(size)]


def tie(value, *earlier):
    return lax.optimization_barrier((value, earlier))[0]


def swap(value, axis_name, mask):
    return lax.ppermute(value, axis_name, xor_pairs(lax.axis_size(axis_name), mask))


def far_masks(axis_name):
    return [2 * m for m in range(1, lax.axis_size(axis_name) // 2)]


class Gather:
    def __init__(self, pieces, cut, turn=None):
        self.cut = cut
        self.turn = turn or (lambda piece: piece)
        self.pieces = pieces

    def near(self, *earlier):
        self.pieces = [tie(piece, *earlier) for piece in self.pieces] if earlier else self.pieces
        self.first = jnp.stack([piece[..., : -self.cut, :] for piece in self.pieces])
        self.second = jnp.stack([self.turn(piece[..., -self.cut :, :]) for piece in self.pieces])
        self.first_in = swap(self.first, "wide", 1)
        self.second_in = [swap(self.second, "narrow", mask) for mask in far_masks("narrow")]
        return [self.first_in] + self.second_in

    def far(self, *earlier):
        if earlier:
            self.first_in = tie(self.first_in, *earlier)
        self.first = jnp.stack([self.first, self.first_in])
        self.extra = self.first[..., self.cut :, :]
        self.first = self.first[..., : self.cut, :]
        self.second = jnp.stack([self.second] + (list(tie(tuple(self.second_in), *earlier)) if earlier else self.second_in))
        self.first_in = [swap(self.first, "narrow", mask) for mask in far_masks("narrow")]
        self.second_in = swap(self.second, "wide", 1)
        return self.first_in + [self.second_in]

    def core(self, *earlier):
        if earlier:
            late = tie((tuple(self.first_in), self.second_in), *earlier)
            self.first_in, self.second_in = list(late[0]), late[1]
        self.mine = [self.first] + self.first_in + [self.second, self.second_in]
        self.theirs = [swap(part, "narrow", 1) for part in self.mine]
        return self.theirs


def far_wide(piece):
    return [piece] + [swap(piece, "wide", mask) for mask in far_masks("wide")]


def gathered_at(part, index, side, fars, ms):
    m, index = index % ms, index // ms
    half, near, far = (0, index, part) if part < fars else (1, part - fars, index)
    return half, 2 * m + near, 2 * far + side


def placing(copies, fars, ms, me_ref, refs, outs, sems):
    found = []
    for k, ref in enumerate(refs):
        side, part = divmod(k, fars + 2)
        for index in range(ref.shape[0] * ms):
            half, wide_mask, narrow_mask = gathered_at(part, index, side, fars, ms)
            wide, narrow = me_ref[0] ^ wide_mask, me_ref[1] ^ narrow_mask
            for source, target in copies(ref.at[index // ms, index % ms], outs, half, wide, narrow):
                found.append(pltpu.make_async_copy(source, target, sems.at[len(found)]))
    return found


def place_kernel(copies, fars, ms, me_ref, *rest):
    count = 2 * (fars + 2)
    found = placing(copies, fars, ms, me_ref, rest[:count], rest[count:-1], rest[-1])
    for copy in found:
        copy.start()
    for copy in found:
        copy.wait()


def place(me, parts, copies, shapes, name):
    fars, ms = lax.axis_size("narrow") // 2, lax.axis_size("wide") // 2
    return pl.pallas_call(
        partial(place_kernel, copies, fars, ms),
        out_shape=[jax.ShapeDtypeStruct(shape, parts[0].dtype) for shape in shapes],
        in_specs=[pl.BlockSpec(memory_space=pltpu.SMEM)] + [ANYWHERE] * len(parts),
        out_specs=[pl.BlockSpec(memory_space=pltpu.VMEM)] * len(shapes),
        compiler_params=pltpu.CompilerParams(vmem_limit_bytes=LIMIT),
        scratch_shapes=[pltpu.SemaphoreType.DMA((8 * fars * ms,))],
        cost_estimate=estimate(0, 4 * sum(math.prod(shape) for shape in shapes)),
        name=name,
    )(me, *parts)


def in_order(parts, wide_size, narrow_size, place_of):
    my_wide, my_narrow = lax.axis_index("wide"), lax.axis_index("narrow")
    ordered = [
        pick(parts, place_of(w ^ my_wide, n ^ my_narrow), 0) for w in range(wide_size) for n in range(narrow_size)
    ]
    return jnp.stack(ordered).reshape((wide_size, narrow_size) + parts.shape[1:])


def half_in_order(parts, half):
    wide_size, narrow_size = lax.axis_size("wide"), lax.axis_size("narrow")
    fars, ms = narrow_size // 2, wide_size // 2

    def place_of(wide_mask, narrow_mask):
        near, m, side, far = wide_mask & 1, wide_mask >> 1, narrow_mask & 1, narrow_mask >> 1
        outer = far * 2 + near if half == 0 else near * fars + far
        return side * (fars * 2 * ms) + outer * ms + m

    count = len(parts) // 2
    found = []
    for side in range(2):
        own = parts[side * count : (side + 1) * count]
        found += own[:fars] if half == 0 else own[fars:]
    found = [part.reshape((-1,) + part.shape[2:]) for part in found]
    return in_order(jnp.concatenate(found), wide_size, narrow_size, place_of)


def pick(value, index, axis):
    return lax.dynamic_index_in_dim(value, index, axis, keepdims=False)


def core_swap(send):
    return [swap(part, "narrow", 1) for part in send]


def cut_wide(send):
    count = min(4, send.shape[1] // 2)
    width = send.shape[1] // count
    return [lax.slice_in_dim(send, width * k, width * (k + 1), axis=1) for k in range(count)]


def far_all_to_all(pieces):
    groups = [list(range(near, lax.axis_size("wide"), 2)) for near in range(2)]
    return lax.all_to_all(pieces, "wide", 0, 0, axis_index_groups=groups)


class Stream:
    def __init__(self, keep, arrived, order, window=None):
        rest = keep.shape[2:]
        self.quarters, self.wide = len(arrived), keep.shape[1]
        self.window = window or (0, rest[0])
        self.rest = (self.window[1] - self.window[0],) + rest[1:]
        self.order = list(order)
        self.dims = {"y": keep.shape[0], "z": keep.shape[1] // 2, "x": 2}
        self.parts = [part.reshape((1, -1) + rest) for part in [keep] + arrived]

    def plan(self):
        by_all = self.order[0] == "a"
        axis = "z" if by_all else self.order[0]
        names = [name for name in ("y", "z", "x") if name in self.dims]
        sizes = [self.dims[name] for name in names]
        cut = names.index(axis)
        stride = math.prod(sizes[cut + 1 :])
        places = [
            outer * sizes[cut] * stride + inner for outer in range(math.prod(sizes[:cut])) for inner in range(stride)
        ]
        return by_all, axis, sizes[cut], stride, places

    def outputs(self):
        by_all, unused_axis, size, unused_stride, places = self.plan()
        shape = (len(places),) + self.rest
        return [(size,) + shape] if by_all else [(1,) + shape] * size

    def sent(self, pieces):
        axis = self.order.pop(0)
        self.quarters = 0
        del self.dims["z" if axis == "a" else axis]
        self.window = (0, self.rest[0])
        if axis == "a":
            self.parts = list(pieces)
        else:
            name, scale = ("narrow", 2) if axis == "y" else ("wide", 1 if axis == "x" else 2)
            self.parts = [pieces[0]] + [swap(piece, name, scale * m) for m, piece in enumerate(pieces) if m]

    def last(self):
        return [part.reshape((-1,) + self.rest) for part in self.parts]


def fold_kernel(plans, windows, quarters, firsts, me_ref, all_ins, all_outs):
    for (by_all, axis, size, stride, places), (low, high), parts, first, ins, outs in zip(
        plans, windows, quarters, firsts, all_ins, all_outs
    ):
        here = me_ref[1] >> 1 if axis == "y" else me_ref[0] & 1 if axis == "x" else me_ref[0] >> 1
        for step in range(size):
            at = step * stride if by_all else (here ^ step) * stride
            for k, base in enumerate(places):
                found = [(ref, source, base + at) for ref in (ins[:1] if parts else ins) for source in range(ref.shape[0])]
                if parts:
                    wide = parts[1]
                    width = wide // parts[0]
                    far, left = (here ^ step, base) if axis == "y" else (base // wide, base % wide)
                    inner = left % width if axis == "y" else left % width + at
                    found.append((ins[1 + left // width], 0, far * width + inner))
                total = sum(ref[source, place, low:high].astype(jnp.float32) for ref, source, place in found)
                out = outs[0].at[step, first + k] if by_all else outs[step].at[0, k]
                out[...] = total.astype(out.dtype)


def interleaved(kernel, before, extra, in_places, out_places):
    def run(*refs):
        ins, outs = refs[1:before], refs[before + extra :]
        return kernel(
            refs[0], [[ins[k] for k in places] for places in in_places], [[outs[k] for k in places] for places in out_places]
        )

    return run


def fold_streams(streams, me, after):
    plans = [stream.plan() for stream in streams]
    windows = [stream.window for stream in streams]
    quarters = [(stream.quarters, stream.wide) if stream.quarters else None for stream in streams]
    operands, in_places = [], []
    for stream in streams:
        known = [id(part) for part in operands]
        operands += [part for part in stream.parts if id(part) not in known]
        known = [id(part) for part in operands]
        in_places.append([known.index(id(part)) for part in stream.parts])
    shapes, out_places, firsts, joint, joint_at = [], [], [], 0, None
    for stream, plan in zip(streams, plans):
        firsts.append(joint)
        if plan[0] and joint_at is not None:
            out_places.append([joint_at])
        else:
            if plan[0]:
                joint_at = len(shapes)
            out_places.append(list(range(len(shapes), len(shapes) + len(stream.outputs()))))
            shapes += stream.outputs()
        if plan[0]:
            joint += len(plan[4])
    if joint_at is not None:
        shapes[joint_at] = (shapes[joint_at][0], joint) + shapes[joint_at][2:]
    kinds = [None] * len(shapes)
    for stream, places in zip(streams, out_places):
        for k in places:
            kinds[k] = stream.parts[0].dtype
    found = pl.pallas_call(
        interleaved(
            partial(fold_kernel, plans, windows, quarters, firsts), 1 + len(operands), len(after), in_places, out_places
        ),
        in_specs=[pl.BlockSpec(memory_space=pltpu.SMEM)] + [whole_plain(a) for a in operands] + [ANYWHERE] * len(after),
        out_shape=[jax.ShapeDtypeStruct(shape, kind) for shape, kind in zip(shapes, kinds)],
        compiler_params=pltpu.CompilerParams(vmem_limit_bytes=LIMIT),
        cost_estimate=estimate(1e6, 6e6),
        name="fold",
    )(me, *operands, *after)
    token = found[0]
    for stream, plan, places in zip(streams, plans, out_places):
        if not plan[0]:
            stream.sent([found[k] for k in places])
    if joint_at is not None:
        arrived = far_all_to_all(found[joint_at])
        for stream, plan, first in zip(streams, plans, firsts):
            if plan[0]:
                stream.sent([lax.slice_in_dim(arrived, first, first + len(plan[4]), axis=1)])
    return token


def narrow_sum(value):
    mask = 1
    while mask < lax.axis_size("narrow"):
        value = value + swap(value, "narrow", mask)
        mask *= 2
    return value


def exact(left, right, dims=(((1,), (0,)), ((), ()))):
    return lax.dot_general(left, right, dims, precision=PRECISE, preferred_element_type=jnp.float32)


def close(left, right):
    left_high, left_low = halves(left)
    right_high, right_low = halves(right)
    return mm(
        jnp.concatenate([left_high, left_low, left_high], axis=1), jnp.concatenate([right_high, right_high, right_low], axis=0)
    )


def diagonal_of(shape):
    return lax.broadcasted_iota(jnp.int32, shape, 0) == lax.broadcasted_iota(jnp.int32, shape, 1)


def ortho_scale(gram_mat):
    square_sum = jnp.where(diagonal_of(gram_mat.shape), gram_mat, 0.0)
    square_sum = jnp.sum(jnp.sum(square_sum, axis=1, keepdims=True), axis=0, keepdims=True)
    return 1.0 / (jnp.sqrt(square_sum) + ORTHO_EPS)


def sweeps(grams, factors, count, last):
    for left in reversed(range(count)):
        polys = [CUBIC_COEF * gram + QUINTIC_COEF * close(gram, gram) for gram in grams]
        polys = [jnp.where(diagonal_of(poly.shape), poly + LINEAR_COEF, poly) for poly in polys]
        if not left and last:
            return grams, [close(poly, factor) for poly, factor in zip(polys, factors)]
        if factors is None:
            factors, halfway = polys, [close(poly, gram) for poly, gram in zip(polys, grams)]
        else:
            both = [
                close(poly, jnp.concatenate([factor, gram], axis=1)) for poly, factor, gram in zip(polys, factors, grams)
            ]
            factors, halfway = zip(*[(pair[:, : pair.shape[0]], pair[:, pair.shape[0] :]) for pair in both])
        grams = [close(poly, half) for poly, half in zip(polys, halfway)]
    return grams, factors


def apply_factor(factor, block):
    rows = block.shape[0]
    return exact(factor[:rows, :rows], block)


def apply_factor_turned(factor, block):
    rows = block.shape[1]
    return close(block, factor) if rows % 128 == 0 else exact(block, factor[:rows, :rows])


def ortho_start(grams):
    scales = [ortho_scale(gram) for gram in grams]
    return [gram * scale * scale for gram, scale in zip(grams, scales)], scales


def block_pairs(count):
    return [(row, column) for row in range(count) for column in range(row + 1)]


def padded(size):
    return -(-size // 128) * 128


def store_padded(gram, out_ref):
    out_ref[...] = jnp.zeros(out_ref.shape, jnp.float32)
    out_ref[: gram.shape[0], : gram.shape[1]] = gram


def packed_blocks(small, large, out_ref):
    pairs = block_pairs(padded(large.shape[0]) // 128)
    for k, (row, column) in enumerate(pairs):
        store_padded(large[128 * row : 128 * (row + 1), 128 * column : 128 * (column + 1)], out_ref.at[k])
    store_padded(small, out_ref.at[len(pairs)])


def unpacked_blocks(blocks, count):
    pairs = block_pairs(count)
    found = {}
    for k, (row, column) in enumerate(pairs):
        found[row, column] = blocks[k]
        if row != column:
            found[column, row] = blocks[k].T
    large = [jnp.concatenate([found[row, column] for column in range(count)], axis=1) for row in range(count)]
    return blocks[len(pairs)], jnp.concatenate(large, axis=0)


def sweep_kernel(count, *refs):
    blocks, (small_ref, large_ref, small_factor_ref, large_factor_ref) = refs[:-4], refs[-4:]
    grams = unpacked_blocks(sum(ref[...] for ref in blocks), large_ref.shape[0] // 128)
    grams, scales = ortho_start(grams)
    grams, factors = sweeps(grams, None, count, False)
    for gram, factor, scale, gram_ref, factor_ref in zip(
        grams, factors, scales, (small_ref, large_ref), (small_factor_ref, large_factor_ref)
    ):
        gram_ref[...] = gram
        factor_ref[...] = factor * scale


def moment_step(gradient, moment_ref, grad_ref, new_ref, at=(), along=1):
    grad_ref[at + (slice(None), slice(None))] = gradient
    moment = MOMENT_DECAY * moment_ref[at + (slice(None), slice(None))] + gradient
    new_ref[at + (slice(None), slice(None))] = moment
    return exact(moment, moment, (((along,), (along,)), ((), ())))


def sum_of(refs):
    return sum(ref[k].astype(jnp.float32) for ref in refs for k in range(ref.shape[0]))


def take(refs, count):
    return refs[:count], refs[count:]


def attn_moment_kernel(counts, mqkv_ref, mout_ref, *refs):
    left, refs = take(refs, counts[0])
    right, refs = take(refs, counts[1])
    gqkv_ref, gout_ref, nqkv_ref, nout_ref, gram_ref = refs
    left, right = sum_of(left), sum_of(right)
    width = mout_ref.shape[1]
    store_padded(moment_step(left[:, :width], mqkv_ref, gqkv_ref, nqkv_ref, (0,)), gram_ref.at[0])
    store_padded(moment_step(left[:, width:], mqkv_ref, gqkv_ref, nqkv_ref, (1,)), gram_ref.at[1])
    store_padded(moment_step(right[:, :width], mqkv_ref, gqkv_ref, nqkv_ref, (2,)), gram_ref.at[2])
    store_padded(moment_step(right[:, width:], mout_ref, gout_ref, nout_ref), gram_ref.at[3])


def ffn_moment_kernel(counts, unit, min_ref, mback_ref, *refs):
    found = []
    for count in counts:
        part, refs = take(refs, count)
        found.append(sum_of(part))
    gin_ref, gback_ref, nin_ref, nback_ref, blocks_ref = refs
    rows = min_ref.shape[0]
    if len(found) * 128 == mback_ref.shape[1]:
        grad_in = [part[:rows] for part in found]
        turned = [jnp.concatenate([part[rows:, :128], part[rows:, 128:]], axis=0) for part in found]
        turned = jnp.concatenate(turned, axis=1)
    else:
        grad_in, turned = [found[0]], found[1]
    pieces = [part[:, at : at + unit] for at in range(0, grad_in[0].shape[1], unit) for part in grad_in]
    small = moment_step(jnp.concatenate(pieces, axis=1), min_ref, gin_ref, nin_ref)
    packed_blocks(small, moment_step(turned, mback_ref, gback_ref, nback_ref, (), 0), blocks_ref)


def with_own_columns(me_ref, old, width, use):
    for n in range(old.shape[-1] // width):
        pl.when(me_ref[1] == n)(partial(use, old[..., width * n : width * (n + 1)]))


def attn_ortho_kernel(rates, me_ref, *refs):
    parts, (nqkv_ref, nout_ref, wqkv_ref, wout_ref, vqkv_ref, vout_ref) = refs[:-6], refs[-6:]
    grams, scales = ortho_start([sum(ref[j] for ref in parts) for j in range(4)])
    factors = sweeps(grams, None, NS_ITERS, True)[1]
    for j in range(4):
        new, old, rate = (nqkv_ref[j], wqkv_ref[j], rates[0]) if j < 3 else (nout_ref[...], wout_ref[...], rates[1])
        ortho = apply_factor(factors[j] * scales[j], new)

        def store(own, j=j, rate=rate, ortho=ortho):
            value = own * (1.0 - rate * WEIGHT_DECAY) - rate * ortho
            if j < 3:
                vqkv_ref[j] = value
            else:
                vout_ref[...] = value

        with_own_columns(me_ref, old, ortho.shape[1], store)


def ffn_ortho_kernel(
    rates, count, me_ref, gin_ref, gback_ref, fin_ref, fback_ref, nin_ref, nback_ref, win_ref, wback_ref, vin_ref, vback_ref
):
    grams, factors = [gin_ref[...], gback_ref[...]], [fin_ref[...], fback_ref[...]]
    factors = sweeps(grams, factors, count, True)[1]
    ortho_in = apply_factor(factors[0], nin_ref[...])
    ortho_back = apply_factor_turned(factors[1], nback_ref[...])

    def store_in(own):
        vin_ref[...] = own * (1.0 - rates[0] * WEIGHT_DECAY) - rates[0] * ortho_in

    def store_back(own):
        vback_ref[...] = own.T * (1.0 - rates[1] * WEIGHT_DECAY) - rates[1] * ortho_back

    with_own_columns(me_ref, win_ref[...], ortho_in.shape[1], store_in)
    with_own_columns(me_ref, wback_ref[...], ortho_back.shape[0], store_back)


def simple_call(kernel, args, shapes, name, flops, after=()):
    def run(*refs):
        kernel(*refs[: len(args)], *refs[len(args) + len(after) :])

    return pl.pallas_call(
        run,
        in_specs=[whole_plain(a) for a in args] + [pl.BlockSpec(memory_space=pl.ANY)] * len(after),
        out_shape=[jax.ShapeDtypeStruct(shape, jnp.float32) for shape in shapes],
        compiler_params=pltpu.CompilerParams(vmem_limit_bytes=LIMIT),
        cost_estimate=estimate(flops, 4e6),
        name=name,
    )(*args, *after)


def whole_plain(array):
    return pl.BlockSpec(memory_space=pltpu.SMEM if array.dtype == jnp.int32 else pltpu.VMEM)


def adam_update(param, earlier_first, earlier_second, gradient):
    first_new = FIRST_DECAY * earlier_first + (1.0 - FIRST_DECAY) * gradient
    second_new = SECOND_DECAY * earlier_second + (1.0 - SECOND_DECAY) * gradient * gradient
    first_fix = 1.0 - FIRST_DECAY**ADAM_STEP
    second_fix = 1.0 - SECOND_DECAY**ADAM_STEP
    direction = first_new / first_fix / (jnp.sqrt(second_new / second_fix) + ADAM_EPS)
    return (first_new, second_new, param - VECTOR_RATE * (direction + WEIGHT_DECAY * param))


def per_device(
    block_in,
    out_grad,
    lengths,
    feature_proj,
    attn_in,
    attn_out,
    ffn_in,
    ffn_out,
    norm_params,
    bias_in,
    bias_out,
    mom_attn_in,
    mom_attn_out,
    mom_ffn_in,
    mom_ffn_out,
    first_norms,
    first_bias_in,
    first_bias_out,
    second_norms,
    second_bias_in,
    second_bias_out,
):
    seqs, length, unused_width = block_in.shape
    wide_size, narrow_size = lax.axis_size("wide"), lax.axis_size("narrow")
    column = lax.axis_index("narrow")
    own_rows, own_cols = D // wide_size, D // narrow_size
    ffn_rows = FF // wide_size
    tiles = ffn_rows // 128 if ffn_rows % 128 == 0 else 1
    unit = ffn_rows // tiles
    width = unit * wide_size
    copied = narrow_size == 4 and own_rows % 16 == 0 and unit % 32 == 0 and (width // narrow_size) % 128 == 0
    blocks = unit == 128 and width // narrow_size == 256 and own_cols == 2 * own_rows
    bf = jnp.bfloat16

    me = jnp.stack([lax.axis_index("wide"), column]).astype(jnp.int32)

    small = jnp.concatenate([norm_params.reshape(-1), bias_in, bias_out]).astype(bf)
    small_size = small.shape[0]
    part = 4 * D // narrow_size
    four = jnp.concatenate([attn_in.astype(bf), attn_out.astype(bf)[None]])
    if part == D:
        four = pick(four, column, 0)
    else:
        four = lax.dynamic_slice_in_dim(four.transpose(1, 0, 2).reshape(own_rows, 4 * D), column * part, part, 1)
    small = jnp.pad(small, (0, -small_size % (8 * part))).reshape(-1, part)
    split = own_rows // 2
    four_gather = Gather(far_wide(jnp.concatenate([four[:split], small, four[split:]])), split)

    in_part = width // narrow_size
    back_part = unit // narrow_size
    folds = D // in_part
    low_in = ffn_in.astype(bf).reshape(own_rows, wide_size, tiles, unit).transpose(2, 0, 1, 3).reshape(tiles, own_rows, width)
    low_in = lax.dynamic_slice_in_dim(low_in, column * in_part, in_part, 2)
    low_back = lax.dynamic_slice_in_dim(ffn_out.reshape(tiles, unit, D), column * back_part, back_part, 1).astype(bf)
    low_back = low_back.reshape(tiles, back_part, folds, in_part).transpose(0, 2, 1, 3).reshape(tiles, own_rows, in_part)
    low_ffn = jnp.concatenate([low_in, low_back], axis=1)

    def as_rows(piece):
        return piece.reshape(-1, folds, back_part, in_part).swapaxes(1, 2).reshape(-1, back_part, D)

    four_gather.near()
    ffn_far = far_wide(tie(low_ffn, *four_gather.pieces[1:]))
    middle_piece = len(ffn_far) // 2
    four_far = four_gather.far(ffn_far[middle_piece])
    four_gather.second_in = tie(four_gather.second_in, *ffn_far[1:])
    four_gather.core()
    ffn_gather = Gather(ffn_far, own_rows, as_rows)
    early = ffn_gather.near(*four_far)
    four_parts = four_gather.mine + four_gather.theirs
    ms = wide_size // 2
    small_all = in_order(
        four_gather.extra.reshape((-1,) + small.shape), wide_size, 1, lambda w, n: (w & 1) * ms + (w >> 1)
    )
    small_all = small_all.reshape(wide_size, -1)[:, :small_size].astype(jnp.float32)
    norm_all = small_all[:, : 4 * own_rows].reshape(wide_size, 4, own_rows).transpose(1, 0, 2).reshape(4, D)
    bias_in_all = small_all[:, 4 * own_rows : 4 * own_rows + ffn_rows].reshape(wide_size, tiles, unit)
    bias_in_all = bias_in_all.transpose(1, 0, 2).reshape(tiles, 1, width)
    bias_out_all = small_all[:, 4 * own_rows + ffn_rows :].reshape(1, D)
    vectors = jnp.concatenate([norm_all, bias_out_all, jnp.zeros((3, D), jnp.float32)])

    def four_copies(piece, outs, half, w, n):
        return [(piece, outs[0].at[n, pl.ds(w * own_rows + half * split, split)])]

    def ffn_copies(piece, outs, half, w, n):
        if half == 0:
            return [(piece, outs[0].at[:, pl.ds(w * own_rows, own_rows), pl.ds(n * in_part, in_part)])]
        return [(piece, outs[1].at[:, pl.ds(w * unit + n * back_part, back_part)])]

    if copied:
        (weights,) = place(me, four_parts, four_copies, [(4, D, D)], "place_four")
    else:
        weights = jnp.stack([half_in_order(four_parts, half) for half in range(2)], axis=2)
        weights = weights.transpose(0, 2, 3, 1, 4).reshape(D, 4, D).transpose(1, 0, 2)

    cosine, sine = rotary_blocks(length)
    proj, projt = projection_blocks(feature_proj)
    middle, h1, h2, *kept, mixed = attend(lengths, block_in, weights, vectors, proj, cosine, sine, early)
    ffn_gather.far()
    ffn_gather.core(middle)
    ffn_parts = ffn_gather.mine + ffn_gather.theirs
    if copied:
        w_in, w_back = place(me, ffn_parts, ffn_copies, [(tiles, D, width), (tiles, width, D)], "place_ffn")
    else:
        w_in = half_in_order(ffn_parts, 0).transpose(2, 0, 3, 1, 4).reshape(tiles, D, width)
        w_back = half_in_order(ffn_parts, 1).transpose(2, 0, 1, 3, 4).reshape(tiles, width, D)
    past, token = None, []
    streams, bias_sums = [], []
    orders = ["yzx", "yxa", "xya"]
    for tile in range(tiles):
        ffn, grad_h2, bias_sum, *grad_tile = ffn_tile(
            tile, h2, out_grad, w_in, w_back, bias_in_all[tile : tile + 1], me, past, wide_size, narrow_size, blocks, token
        )
        past = (ffn, grad_h2)
        bias_sums.append(bias_sum)
        token = [fold_streams(streams[:1], me, [bias_sum])] if tile == 1 else []
        if blocks:
            keep, *send = grad_tile
            streams.append(Stream(keep, core_swap(send), orders[tile % 3]))
        else:
            grad_in = grad_tile[0][0].reshape(wide_size, own_rows, narrow_size, in_part).transpose(2, 0, 1, 3)
            grad_back = grad_tile[0][1].reshape(narrow_size, own_cols, wide_size, unit).transpose(0, 2, 1, 3)
            for found, order in ((grad_in, "yxz"), (grad_back, "xyz")):
                found = found.reshape((narrow_size // 2, 2) + found.shape[1:])
                arrived = core_swap(cut_wide(pick(found, 1 - (column & 1), 1)))
                streams.append(Stream(pick(found, column & 1, 1), arrived, order))
    ffn = tie(ffn, *streams[0].parts[1:])
    grad_middle, gb, sums_two = middle_back(out_grad, grad_h2, middle, vectors, narrow_size)

    def fold_open(more, after):
        found = more + [stream for stream in streams if stream.order]
        done = [part for stream in streams if not stream.order for part in stream.parts]
        return fold_streams(found, me, after + done)

    token = fold_open([], [sums_two])
    gq, gk, gv = attend_back(lengths, grad_middle, weights, projt, cosine, sine, kept, narrow_size, [token])
    token = fold_open([], [gq])
    send = attn_weights(me, h1, mixed, (gq, gk, gv, gb), wide_size, 1, [token])
    (keep,) = attn_weights(me, h1, mixed, (gq, gk, gv, gb), wide_size, 0, send[:1])
    arrived = core_swap(send)
    left = Stream(keep, arrived, "xzy", (0, own_rows))
    right = Stream(keep, arrived, "yxz", (own_rows, 2 * own_rows))
    right.parts = left.parts
    token = fold_open([left, right], [keep])
    input_grad, sums_one = input_back(block_in, grad_middle, (gq, gk, gv), weights, vectors, [token])

    norm_sums = jnp.concatenate([sums_one[:2], sums_two[:2], sums_two[2:3]])
    inner_sums = jnp.concatenate(bias_sums).reshape(tiles, wide_size, unit).transpose(1, 0, 2)
    inner_sums = inner_sums.reshape(wide_size, narrow_size, ffn_rows // narrow_size)
    norm_part = own_rows // narrow_size
    norm_sums = norm_sums.reshape(5, wide_size, narrow_size, norm_part).transpose(1, 2, 0, 3).reshape(wide_size, narrow_size, -1)
    vector_parts = jnp.concatenate([norm_sums, inner_sums], axis=2).swapaxes(0, 1)
    vector_size = vector_parts.shape[2]
    vector_parts = jnp.pad(vector_parts, ((0, 0), (0, 0), (0, -vector_size % 128)))
    vector_parts = vector_parts.reshape(narrow_size // 2, 2, wide_size, 1, -1)
    vector_send = tie(pick(vector_parts, 1 - (column & 1), 1), *left.parts[1:], *right.parts[1:])
    vector = Stream(pick(vector_parts, column & 1, 1), core_swap([vector_send]), "yxz")
    token = fold_streams([left, right, vector], me, [sums_one])
    sum_parts = [stream.last() for stream in streams]
    small_size, large_size = padded(own_rows), padded(ffn_rows)
    block_count = len(block_pairs(large_size // 128)) + small_size // 128
    grad_in_w, grad_back_w, mom_in_new, mom_back_new, blocks_gram = simple_call(
        partial(ffn_moment_kernel, [len(parts) for parts in sum_parts], unit),
        [mom_ffn_in, mom_ffn_out.T] + sum(sum_parts, []),
        [mom_ffn_in.shape, mom_ffn_out.T.shape] * 2 + [(block_count, 128, 128)],
        "ffn_moment",
        1e9,
        [token],
    )
    block_out = layer_output(ffn, middle, vectors, [mom_in_new])
    token = fold_streams([left, right, vector], me, [mom_in_new, block_out])
    blocks_gram = tie(blocks_gram, token)
    blocks_near = blocks_gram + swap(blocks_gram, "narrow", 1)
    blocks_all = [blocks_near] + [swap(blocks_near, "narrow", mask) for mask in far_masks("narrow")]
    token = fold_streams([vector], me, [blocks_near])
    left_parts, right_parts = left.last(), right.last()
    def own_columns(weight):
        block_width = weight.shape[-1] // narrow_size
        return lax.dynamic_slice_in_dim(
            weight, column * block_width, block_width, axis=weight.ndim - 1
        )

    rate_qkv = MUON_SCALE
    rate_out = MUON_SCALE * math.sqrt(D / (D // 64))
    rate_in = MUON_SCALE * math.sqrt(FF / D)
    rate_back = MUON_SCALE * math.sqrt(D / FF)
    shapes = [mom_attn_in.shape, mom_attn_out.shape]
    grad_qkv, grad_out_w, mom_qkv_new, mom_out_new, gram_four = simple_call(
        partial(attn_moment_kernel, (len(left_parts), len(right_parts))),
        [mom_attn_in, mom_attn_out] + left_parts + right_parts,
        shapes + shapes + [(4, padded(own_rows), padded(own_rows))],
        "attn_moment",
        1e9,
        [token],
    )
    gram_near = gram_four + swap(gram_four, "narrow", 1)
    sweep_in, sweep_back, factor_in, factor_back = simple_call(
        partial(sweep_kernel, 2),
        blocks_all,
        [(small_size, small_size), (large_size, large_size)] * 2,
        "ffn_sweeps",
        1e10,
        [gram_four],
    )
    vector_sums = sum(jnp.sum(part, axis=0) for part in vector.last())[0, :vector_size]
    grad_norm_vals = vector_sums[: 4 * norm_part].reshape(4, norm_part)
    grad_bias_final = vector_sums[4 * norm_part : 5 * norm_part]
    grad_bias_inner = vector_sums[5 * norm_part :]
    gram_all = [gram_near] + [swap(gram_near, "narrow", mask) for mask in far_masks("narrow")]
    new_in, new_back = simple_call(
        partial(ffn_ortho_kernel, (rate_in, rate_back), NS_ITERS - 2),
        [me, sweep_in, sweep_back, factor_in, factor_back, mom_in_new, mom_back_new, ffn_in, ffn_out],
        [mom_ffn_in.shape, mom_ffn_out.T.shape],
        "ffn_ortho",
        1e10,
        [gram_near],
    )
    new_qkv, new_out = simple_call(
        partial(attn_ortho_kernel, (rate_qkv, rate_out)),
        [me, *gram_all, mom_qkv_new, mom_out_new, attn_in, attn_out],
        shapes,
        "attn_ortho",
        5e9,
        [new_in],
    )
    norm_first, norm_second, norm_new = adam_update(
        own_columns(norm_params), first_norms, second_norms, grad_norm_vals
    )
    inner_first, inner_second, inner_new = adam_update(
        own_columns(bias_in), first_bias_in, second_bias_in, grad_bias_inner
    )
    final_first, final_second, final_new = adam_update(
        own_columns(bias_out), first_bias_out, second_bias_out, grad_bias_final
    )
    return (
        block_out,
        input_grad,
        grad_qkv,
        grad_out_w,
        grad_in_w,
        grad_back_w.T,
        grad_norm_vals,
        grad_bias_inner,
        grad_bias_final,
        mom_qkv_new,
        mom_out_new,
        mom_in_new,
        mom_back_new.T,
        new_qkv,
        new_out,
        new_in,
        new_back.T,
        norm_first,
        inner_first,
        final_first,
        norm_second[:2],
        norm_second[2:],
        inner_second,
        final_second,
        norm_new,
        inner_new,
        final_new,
    )


def solution(mesh):
    in_specs = (
        P(("wide", "narrow"), None, None),
        P(("wide", "narrow"), None, None),
        P(("wide", "narrow")),
        P(),
        P(None, "wide", None),
        P("wide", None),
        P("wide", None),
        P("wide", None),
        P(None, "wide"),
        P("wide"),
        P("wide"),
        P(None, "wide", "narrow"),
        P("wide", "narrow"),
        P("wide", "narrow"),
        P("wide", "narrow"),
        P(None, ("wide", "narrow")),
        P(("wide", "narrow")),
        P(("wide", "narrow")),
        P(None, ("wide", "narrow")),
        P(("wide", "narrow")),
        P(("wide", "narrow")),
    )
    out_specs = (
        P(("wide", "narrow"), None, None),
        P(("wide", "narrow"), None, None),
        P(None, "wide", "narrow"),
        P("wide", "narrow"),
        P("wide", "narrow"),
        P("wide", "narrow"),
        P(None, ("wide", "narrow")),
        P(("wide", "narrow")),
        P(("wide", "narrow")),
        P(None, "wide", "narrow"),
        P("wide", "narrow"),
        P("wide", "narrow"),
        P("wide", "narrow"),
        P(None, "wide", "narrow"),
        P("wide", "narrow"),
        P("wide", "narrow"),
        P("wide", "narrow"),
        P(None, ("wide", "narrow")),
        P(("wide", "narrow")),
        P(("wide", "narrow")),
        P(None, ("wide", "narrow")),
        P(None, ("wide", "narrow")),
        P(("wide", "narrow")),
        P(("wide", "narrow")),
        P(None, ("wide", "narrow")),
        P(("wide", "narrow")),
        P(("wide", "narrow")),
    )
    return jax.shard_map(
        per_device, mesh=mesh, in_specs=in_specs, out_specs=out_specs, check_vma=False
    )
```

```python
from functools import partial
import math

import jax
import jax.numpy as jnp
from jax import lax
from jax.experimental import pallas as pl
from jax.experimental.pallas import tpu as pltpu
from jax.sharding import PartitionSpec as P

D = 768
FF = 3072
HEADS = 12
HDIM = 64
FEAT = 32
NS_ITERS = 5
ADAM_STEP = 10


PRECISE = lax.Precision.HIGHEST
NORM_EPS = 1e-05
ORTHO_EPS = 1e-07
ADAM_EPS = 1e-08
LINEAR_COEF = 3.4445
CUBIC_COEF = -4.775
QUINTIC_COEF = 2.0315
MOMENT_DECAY = 0.5
FIRST_DECAY = 0.5
SECOND_DECAY = 0.5
MUON_SCALE = 0.6
WEIGHT_DECAY = 0.01
VECTOR_RATE = 0.4
GROUP = 4
GROUPS = HEADS // GROUP
GE = GROUP * HDIM
GF = GROUP * FEAT


def mm(left, right):
    return jnp.dot(left, right, preferred_element_type=jnp.float32)


def mm_nt(left, right):
    return lax.dot_general(left, right, (((1,), (1,)), ((), ())), preferred_element_type=jnp.float32)


def mm_tn(left, right):
    return lax.dot_general(left, right, (((0,), (0,)), ((), ())), preferred_element_type=jnp.float32)


def halves(value):
    high = value.astype(jnp.bfloat16)
    return high, (value - high.astype(jnp.float32)).astype(jnp.bfloat16)


def normalise(rows):
    centered = rows - jnp.mean(rows, axis=-1, keepdims=True)
    inverse = lax.rsqrt(jnp.mean(centered * centered, axis=-1, keepdims=True) + NORM_EPS)
    return centered * inverse, inverse


def norm_pull(normed, inverse, grad, gain):
    scaled = grad * gain
    mean_plain = jnp.mean(scaled, axis=-1, keepdims=True)
    mean_prod = jnp.mean(scaled * normed, axis=-1, keepdims=True)
    return inverse * (scaled - mean_plain - normed * mean_prod)


def partner_of(values):
    lane = lax.broadcasted_iota(jnp.int32, (values.shape[0], 128), 1)
    first = (lane & (HDIM - 1)) < HDIM // 2
    parts = []
    for at in range(0, values.shape[1], 128):
        block = values[:, at : at + 128]
        ahead = pltpu.roll(block, 128 - HDIM // 2, 1)
        behind = pltpu.roll(block, HDIM // 2, 1)
        parts.append(jnp.where(first, ahead, behind))
    return jnp.concatenate(parts, axis=1)


def head_mask(rows, columns, row_width, column_width):
    row = lax.broadcasted_iota(jnp.int32, (rows, columns), 0) // row_width
    column = lax.broadcasted_iota(jnp.int32, (rows, columns), 1) // column_width
    return row == column


def store_columns(ref, values):
    width = ref.shape[3]
    for n in range(ref.shape[0]):
        ref[n, 0] = values[:, width * n : width * (n + 1)].astype(ref.dtype)


def load_columns(ref):
    return jnp.concatenate([ref[n, 0] for n in range(ref.shape[0])], axis=1)


def attend_kernel(
    lengths_ref, x_ref, w_ref, vec_ref, proj_ref, cos_ref, sin_ref,
    middle_ref, h1_ref, h2_ref, wq_ref, wk_ref, pq_ref, pk_ref, v_ref, state_ref, total_ref, att_ref, rden_ref, mixed_ref,
):
    rows = x_ref.shape[1]
    x = x_ref[0].astype(jnp.float32)
    h1 = (normalise(x)[0] * vec_ref[0:1, :] + vec_ref[1:2, :]).astype(jnp.bfloat16)
    h1_ref[0] = h1
    live = lax.broadcasted_iota(jnp.int32, (rows, 1), 0) < lengths_ref[pl.program_id(0)]
    live = live.astype(jnp.float32)
    cosine = jnp.concatenate([cos_ref[...]] * (D // 128), axis=1)
    sine = jnp.concatenate([sin_ref[...]] * (D // 128), axis=1)
    values = mm(h1, w_ref[2]).astype(jnp.bfloat16)
    v_ref[0] = values
    feats = []
    for j, (w_out, p_out) in enumerate(((wq_ref, pq_ref), (wk_ref, pk_ref))):
        heads = mm(h1, w_ref[j])
        unit = (heads * cosine + partner_of(heads) * sine) * HDIM ** (-0.25)
        w_out[0] = unit
        high, low = halves(unit)
        sq_high, sq_low = halves(unit * unit)
        parts = []
        for g in range(GROUPS):
            cut = slice(GE * g, GE * (g + 1))
            left = jnp.concatenate([high[:, cut], low[:, cut], high[:, cut], sq_high[:, cut], sq_low[:, cut]], axis=1)
            parts.append(jnp.exp(mm(left, proj_ref[g])) * FEAT ** (-0.5))
        phi = jnp.concatenate(parts, axis=1)
        p_out[0] = phi
        feats.append(phi)
    query_low = feats[0].astype(jnp.bfloat16)
    key_vals = feats[1].astype(jnp.bfloat16).astype(jnp.float32) * live
    key_low = key_vals.astype(jnp.bfloat16)
    total_ref[0] = jnp.sum(key_vals, axis=0, keepdims=True)
    mask = head_mask(GF, GE, FEAT, HDIM)
    ones = jnp.ones((rows, GE), jnp.bfloat16)
    attended, inverse_den = [], []
    for g in range(GROUPS):
        cut = slice(GE * g, GE * (g + 1))
        fcut = slice(GF * g, GF * (g + 1))
        both = mm_tn(key_low[:, fcut], jnp.concatenate([values[:, cut], ones], axis=1))
        state = jnp.where(mask, both[:, :GE], 0.0).astype(jnp.bfloat16)
        state_ref[0, g] = state
        tot_high, tot_low = halves(jnp.where(mask, both[:, GE:], 0.0))
        query = query_low[:, fcut]
        numer = mm(query, state)
        denom = mm(jnp.concatenate([query, query], axis=1), jnp.concatenate([tot_high, tot_low], axis=0))
        inverse = 1.0 / denom
        attended.append(numer * inverse)
        inverse_den.append(inverse)
    attended = jnp.concatenate(attended, axis=1)
    att_ref[0] = attended
    rden_ref[0] = jnp.concatenate(inverse_den, axis=1)
    mixed = attended.astype(jnp.bfloat16)
    mixed_ref[0] = mixed
    middle = x + mm(mixed, w_ref[3])
    middle_ref[0] = middle
    h2_ref[0] = (normalise(middle)[0] * vec_ref[2:3, :] + vec_ref[3:4, :]).astype(jnp.bfloat16)


def output_kernel(ffn_ref, middle_ref, vec_ref, out_ref):
    out_ref[0] = middle_ref[0] + (ffn_ref[0] + vec_ref[4:5, :])


def middle_back_kernel(og_ref, gh2_ref, middle_ref, vec_ref, gm_ref, gb_ref, sums_ref):
    og = og_ref[0].astype(jnp.float32)
    middle = middle_ref[0]
    grad_h2 = gh2_ref[0]
    normed, inverse = normalise(middle)
    grad_middle = og + norm_pull(normed, inverse, grad_h2, vec_ref[2:3, :])
    gm_ref[0] = grad_middle
    store_columns(gb_ref, grad_middle)

    @pl.when(pl.program_id(0) == 0)
    def _():
        sums_ref[...] = jnp.zeros_like(sums_ref)

    sums_ref[0:1, :] += jnp.sum(grad_h2 * normed, axis=0, keepdims=True)
    sums_ref[1:2, :] += jnp.sum(grad_h2, axis=0, keepdims=True)
    sums_ref[2:3, :] += jnp.sum(og, axis=0, keepdims=True)


def attend_back_kernel(
    lengths_ref, gm_ref, w_ref, projt_ref, cos_ref, sin_ref,
    wq_ref, wk_ref, pq_ref, pk_ref, v_ref, state_ref, total_ref, att_ref, rden_ref,
    gq_ref, gk_ref, gv_ref,
):
    rows = gm_ref.shape[1]
    branch = gm_ref[0].astype(jnp.bfloat16)
    grad_numer = mm_nt(branch, w_ref[0]) * rden_ref[0]
    gn_high, gn_low = halves(grad_numer)
    pr_high, pr_low = halves(grad_numer * att_ref[0])
    live = (lax.broadcasted_iota(jnp.int32, (rows, 1), 0) < lengths_ref[pl.program_id(0)]).astype(jnp.float32)
    query_low = pq_ref[0].astype(jnp.bfloat16)
    key_low = (pk_ref[0].astype(jnp.bfloat16).astype(jnp.float32) * live).astype(jnp.bfloat16)
    mask = head_mask(GF, GE, FEAT, HDIM)
    spread = head_mask(GE, GF, HDIM, FEAT).astype(jnp.float32).astype(jnp.bfloat16)
    spread2 = jnp.concatenate([spread, spread], axis=0)
    gather = mask.astype(jnp.float32).astype(jnp.bfloat16)
    gather2 = jnp.concatenate([gather, gather], axis=0)
    grad_u = ([], [])
    grad_v = []
    for g in range(GROUPS):
        cut = slice(GE * g, GE * (g + 1))
        fcut = slice(GF * g, GF * (g + 1))
        query, key, values = query_low[:, fcut], key_low[:, fcut], v_ref[0, :, cut]
        state = state_ref[0, g]
        grad_denom = -mm(jnp.concatenate([pr_high[:, cut], pr_low[:, cut]], axis=1), spread2)
        two = jnp.concatenate([gn_high[:, cut], gn_low[:, cut]], axis=1)
        grad_qfeat = mm_nt(two, jnp.concatenate([state, state], axis=1)) + grad_denom * total_ref[0, :, fcut]
        pair = mm_tn(query, two)
        grad_state = jnp.where(mask, pair[:, :GE] + pair[:, GE:], 0.0)
        grad_total = jnp.sum(grad_denom * query.astype(jnp.float32), axis=0, keepdims=True)
        gs_high, gs_low = halves(grad_state)
        grad_kfeat = mm_nt(
            jnp.concatenate([values, values], axis=1), jnp.concatenate([gs_high, gs_low], axis=1)
        )
        grad_kfeat = (grad_kfeat + grad_total) * live
        grad_v.append(mm(jnp.concatenate([key, key], axis=1), jnp.concatenate([gs_high, gs_low], axis=0)))
        for j, (grad_feat, p_in, w_in) in enumerate(((grad_qfeat, pq_ref, wq_ref), (grad_kfeat, pk_ref, wk_ref))):
            t_high, t_low = halves(grad_feat * p_in[0, :, fcut])
            pulled = mm(jnp.concatenate([t_high, t_low, t_high], axis=1), projt_ref[g])
            weight = mm(jnp.concatenate([t_high, t_low], axis=1), gather2)
            grad_u[j].append((pulled - weight * w_in[0, :, cut]) * HDIM ** (-0.25))
    cosine = jnp.concatenate([cos_ref[...]] * (D // 128), axis=1)
    sine = jnp.concatenate([sin_ref[...]] * (D // 128), axis=1)
    for grads, ref in zip(grad_u, (gq_ref, gk_ref)):
        turned = jnp.concatenate(grads, axis=1)
        store_columns(ref, turned * cosine - partner_of(turned) * sine)
    store_columns(gv_ref, jnp.concatenate(grad_v, axis=1))


def input_back_kernel(x_ref, gm_ref, gq_ref, gk_ref, gv_ref, w_ref, vec_ref, out_ref, sums_ref):
    grad_h1 = sum(mm_nt(load_columns(ref), w_ref[j]) for j, ref in enumerate((gq_ref, gk_ref, gv_ref)))
    normed, inverse = normalise(x_ref[0].astype(jnp.float32))
    out_ref[0] = gm_ref[0] + norm_pull(normed, inverse, grad_h1, vec_ref[0:1, :])

    @pl.when(pl.program_id(0) == 0)
    def _():
        sums_ref[...] = jnp.zeros_like(sums_ref)

    sums_ref[0:1, :] += jnp.sum(grad_h1 * normed, axis=0, keepdims=True)
    sums_ref[1:2, :] += jnp.sum(grad_h1, axis=0, keepdims=True)


def attn_weight_kernel(me_ref, h1_ref, mixed_ref, gq_ref, gk_ref, gv_ref, gb_ref, *out_refs):
    width, rows = out_refs[0].shape[1], out_refs[0].shape[2] // 2
    h1 = h1_ref[...]
    left = mm_tn(h1, jnp.concatenate([gq_ref[...], gk_ref[...]], axis=1)).astype(jnp.bfloat16)
    right = jnp.concatenate([mm_tn(h1, gv_ref[...]), mm_tn(mixed_ref[...], gb_ref[...])], axis=1).astype(jnp.bfloat16)
    for w in range(width * len(out_refs)):
        out_refs[w // width][0, w % width, :rows] = left[rows * w : rows * (w + 1)]
        out_refs[w // width][0, w % width, rows:] = right[rows * w : rows * (w + 1)]


def ffn_kernel(has_past, blocks, h2_ref, og_ref, win_ref, wback_ref, bias_ref, me_ref, *rest):
    if has_past:
        out_past_ref, gh2_past_ref, *rest = rest
    if blocks:
        out_ref, gh2_ref, bsum_ref, keep_ref, *send_refs, act_ref, gi_ref, gw_ref = rest
    else:
        out_ref, gh2_ref, bsum_ref, gw_ref, act_ref, gi_ref = rest
    seqs, rows = out_ref.shape[0], out_ref.shape[1]
    step = pl.program_id(0)
    win, wback = win_ref[...], wback_ref[...]
    bias = bias_ref[...]

    def part(s, carry):
        span = pl.ds(pl.multiple_of(s * rows, rows), rows)
        inner = mm(h2_ref[s], win) + bias
        grad_act = mm_nt(og_ref[s], wback)
        cdf = 0.5 * (1.0 + lax.erf(inner * (2.0**-0.5)))
        pdf = jnp.exp(-0.5 * inner * inner) * (2.0 * math.pi) ** -0.5
        act = (inner * cdf).astype(jnp.bfloat16)
        grad_inner = (grad_act * (cdf + inner * pdf)).astype(jnp.bfloat16)
        act_ref[span, :] = act
        gi_ref[span, :] = grad_inner
        out_part = mm(act, wback)
        gh2_part = mm_nt(grad_inner, win)

        @pl.when(step == 0)
        def _():
            if has_past:
                out_ref[s] = out_past_ref[s] + out_part
                gh2_ref[s] = gh2_past_ref[s] + gh2_part
            else:
                out_ref[s] = out_part
                gh2_ref[s] = gh2_part

        @pl.when(step > 0)
        def _():
            out_ref[s] += out_part
            gh2_ref[s] += gh2_part

        return carry + jnp.sum(grad_inner.astype(jnp.float32), axis=0, keepdims=True)

    bsum_ref[...] = lax.fori_loop(0, seqs, part, jnp.zeros(bias.shape, jnp.float32), unroll=True)
    h2 = h2_ref[...].reshape(seqs * rows, D)
    og = og_ref[...].reshape(seqs * rows, D)
    grad_in = mm_tn(h2, gi_ref[...]).astype(jnp.bfloat16)
    grad_back = mm_tn(og, act_ref[...]).astype(jnp.bfloat16)
    if not blocks:
        gw_ref[0] = grad_in
        gw_ref[1] = grad_back
        return
    narrow, wide = gw_ref.shape[0], gw_ref.shape[1]
    in_rows, in_cols = D // wide, gw_ref.shape[3]
    width = grad_in.shape[1]
    for k in range(width // in_cols):
        for w in range(wide):
            gw_ref[step * (width // in_cols) + k, w, :in_rows, :] = grad_in[
                in_rows * w : in_rows * (w + 1), in_cols * k : in_cols * (k + 1)
            ]
    back_rows = D // narrow
    half = back_rows // 2
    for k in range(width // 128):
        for n in range(narrow):
            for h in range(2):
                gw_ref[n, step * (width // 128) + k, in_rows:, 128 * h : 128 * (h + 1)] = grad_back[
                    back_rows * n + half * h : back_rows * n + half * (h + 1), 128 * k : 128 * (k + 1)
                ]

    @pl.when(step == pl.num_programs(0) - 1)
    def _():
        side = me_ref[1] & 1
        for far in range(narrow // 2):
            for w in range(wide):
                keep_ref[far, w] = gw_ref[2 * far + side, w]
                width = wide // len(send_refs)
                send_refs[w // width][far, w % width] = gw_ref[2 * far + (1 - side), w]


def spec(shape, index):
    return pl.BlockSpec(shape, index)


LIMIT = 60 * 1024 * 1024
ANYWHERE = pl.BlockSpec(memory_space=pl.ANY)


def skipping(kernel, before, extra):
    def run(*refs):
        return kernel(*refs[:before], *refs[before + extra :])

    return run


def estimate(flops, moved, transcendentals=0):
    return pl.CostEstimate(flops=int(flops), bytes_accessed=int(moved), transcendentals=int(transcendentals))


def whole(array):
    rank = array.ndim
    return pl.BlockSpec(array.shape, lambda *unused: (0,) * rank)


def by_seq(shape):
    rank = len(shape)
    return pl.BlockSpec((1,) + tuple(shape[1:]), lambda s, *unused: (s,) + (0,) * (rank - 1))


def by_seq_second(shape):
    rank = len(shape)
    return pl.BlockSpec((shape[0], 1) + tuple(shape[2:]), lambda s, *unused: (0, s) + (0,) * (rank - 2))


def attend(lengths, x, weights, vectors, proj, cosine, sine, after):
    seqs, rows, unused_width = x.shape
    bf, f4 = jnp.bfloat16, jnp.float32
    shapes = [
        ((seqs, rows, D), f4), ((seqs, rows, D), bf), ((seqs, rows, D), bf), ((seqs, rows, D), f4), ((seqs, rows, D), f4),
        ((seqs, rows, HEADS * FEAT), f4), ((seqs, rows, HEADS * FEAT), f4), ((seqs, rows, D), bf),
        ((seqs, GROUPS, GF, GE), bf), ((seqs, 1, HEADS * FEAT), f4), ((seqs, rows, D), f4), ((seqs, rows, D), f4),
        ((seqs, rows, D), bf),
    ]
    return pl.pallas_call(
        skipping(attend_kernel, 7, len(after)),
        grid_spec=pltpu.PrefetchScalarGridSpec(
            num_scalar_prefetch=1,
            grid=(seqs,),
            in_specs=[by_seq(x.shape)] + [whole(a) for a in (weights, vectors, proj, cosine, sine)]
            + [ANYWHERE] * len(after),
            out_specs=[by_seq(shape) for shape, unused in shapes],
        ),
        out_shape=[jax.ShapeDtypeStruct(shape, dtype) for shape, dtype in shapes],
        compiler_params=pltpu.CompilerParams(vmem_limit_bytes=LIMIT),
        cost_estimate=estimate(seqs * rows * D * D * 6, 20e6),
        name="attend",
    )(lengths, x, weights, vectors, proj, cosine, sine, *after)


def layer_output(ffn, middle, vectors, after):
    return pl.pallas_call(
        skipping(output_kernel, 3, len(after)),
        grid=(ffn.shape[0],),
        in_specs=[by_seq(ffn.shape)] * 2 + [whole(vectors)] + [ANYWHERE] * len(after),
        out_specs=by_seq(ffn.shape),
        out_shape=jax.ShapeDtypeStruct(ffn.shape, jnp.float32),
        compiler_params=pltpu.CompilerParams(vmem_limit_bytes=LIMIT),
        cost_estimate=estimate(1e6, 8e6),
        name="layer_output",
    )(ffn, middle, vectors, *after)


def middle_back(og, grad_h2, middle, vectors, narrow_size):
    seqs, rows, unused_width = og.shape
    blocked = (narrow_size, seqs, rows, D // narrow_size)
    full = jax.ShapeDtypeStruct(og.shape, jnp.float32)
    return pl.pallas_call(
        middle_back_kernel,
        grid=(seqs,),
        in_specs=[by_seq(og.shape)] * 3 + [whole(vectors)],
        out_specs=[by_seq(og.shape)] + [by_seq_second(blocked), pl.BlockSpec((8, D), lambda s: (0, 0))],
        out_shape=[full, jax.ShapeDtypeStruct(blocked, jnp.bfloat16), jax.ShapeDtypeStruct((8, D), jnp.float32)],
        compiler_params=pltpu.CompilerParams(vmem_limit_bytes=LIMIT),
        cost_estimate=estimate(1e7, 16e6),
        name="middle_back",
    )(og, grad_h2, middle, vectors)


def attend_back(lengths, grad_middle, weights, projt, cosine, sine, kept, narrow_size, after):
    seqs, rows, unused_width = grad_middle.shape
    blocked = (narrow_size, seqs, rows, D // narrow_size)
    count = 6 + len(kept)
    return pl.pallas_call(
        skipping(attend_back_kernel, count, len(after)),
        grid_spec=pltpu.PrefetchScalarGridSpec(
            num_scalar_prefetch=1,
            grid=(seqs,),
            in_specs=[by_seq(grad_middle.shape), pl.BlockSpec((1, D, D), lambda s, *unused: (3, 0, 0))]
            + [whole(a) for a in (projt, cosine, sine)]
            + [by_seq(a.shape) for a in kept]
            + [ANYWHERE] * len(after),
            out_specs=[by_seq_second(blocked)] * 3,
        ),
        out_shape=[jax.ShapeDtypeStruct(blocked, jnp.bfloat16)] * 3,
        compiler_params=pltpu.CompilerParams(vmem_limit_bytes=LIMIT),
        cost_estimate=estimate(seqs * rows * D * D * 8, 40e6),
        name="attend_back",
    )(lengths, grad_middle, weights, projt, cosine, sine, *kept, *after)


def input_back(x, grad_middle, grads, weights, vectors, after):
    seqs, rows, unused_width = x.shape
    return pl.pallas_call(
        skipping(input_back_kernel, 4 + len(grads), len(after)),
        grid=(seqs,),
        in_specs=[by_seq(x.shape), by_seq(x.shape)] + [by_seq_second(a.shape) for a in grads] + [whole(weights), whole(vectors)] + [ANYWHERE] * len(after),
        out_specs=[by_seq(x.shape), pl.BlockSpec((8, D), lambda s: (0, 0))],
        out_shape=[jax.ShapeDtypeStruct(x.shape, jnp.float32), jax.ShapeDtypeStruct((8, D), jnp.float32)],
        compiler_params=pltpu.CompilerParams(vmem_limit_bytes=LIMIT),
        cost_estimate=estimate(seqs * rows * D * D * 6, 15e6),
        name="input_back",
    )(x, grad_middle, *grads, weights, vectors, *after)


def attn_weights(me, h1, mixed, grads, wide_size, side, after):
    narrow_size, seqs, rows, width = grads[0].shape
    tokens = seqs * rows
    flat = [a.reshape(narrow_size, tokens, width) for a in grads]
    h1, mixed = h1.reshape(tokens, D), mixed.reshape(tokens, D)
    count = 2 if side else 1
    shape = (narrow_size // 2, wide_size // count, 2 * D // wide_size, 2 * width)

    def block_at(i, me_ref):
        return (2 * i + ((me_ref[1] & 1) ^ side), 0, 0)

    return pl.pallas_call(
        skipping(attn_weight_kernel, 7, len(after)),
        grid_spec=pltpu.PrefetchScalarGridSpec(
            num_scalar_prefetch=1,
            grid=(narrow_size // 2,),
            in_specs=[whole(h1), whole(mixed)] + [pl.BlockSpec((None, tokens, width), block_at)] * 4 + [ANYWHERE] * len(after),
            out_specs=[pl.BlockSpec((1,) + shape[1:], lambda i, *unused: (i, 0, 0, 0))] * count,
        ),
        out_shape=[jax.ShapeDtypeStruct(shape, jnp.bfloat16)] * count,
        compiler_params=pltpu.CompilerParams(vmem_limit_bytes=LIMIT),
        cost_estimate=estimate(tokens * D * D * 4, 8e6),
        name="attn_weights",
    )(me, h1, mixed, *flat, *after)


def ffn_tile(tile, h2, og, w_in, w_back, bias, me, past, wide_size, narrow_size, blocks, after):
    seqs, rows, unused_width = h2.shape
    width = w_in.shape[2]
    step = 1024 if width % 1024 == 0 else width
    tokens = jax.ShapeDtypeStruct(h2.shape, jnp.float32)
    out_specs = [whole(h2), whole(h2), pl.BlockSpec((1, step), lambda i: (0, i))]
    out_shape = [tokens, tokens, jax.ShapeDtypeStruct((1, width), jnp.float32)]
    scratch = [pltpu.VMEM((seqs * rows, step), jnp.bfloat16)] * 2
    if blocks:
        block = (2 * D // wide_size, width // narrow_size)
        half = jax.ShapeDtypeStruct((narrow_size // 2, wide_size) + block, jnp.bfloat16)
        part = jax.ShapeDtypeStruct((narrow_size // 2, wide_size // 4) + block, jnp.bfloat16)
        out_specs += [whole(half)] + [whole(part)] * 4
        out_shape += [half] + [part] * 4
        scratch.append(pltpu.VMEM((narrow_size, wide_size) + block, jnp.bfloat16))
    else:
        out_specs.append(pl.BlockSpec((2, D, step), lambda i: (0, 0, i)))
        out_shape.append(jax.ShapeDtypeStruct((2, D, width), jnp.bfloat16))
    return pl.pallas_call(
        skipping(partial(ffn_kernel, past is not None, blocks), 6 + len(past or ()), len(after)),
        grid=(width // step,),
        in_specs=[
            whole(h2),
            whole(og),
            pl.BlockSpec((None, D, step), lambda i: (tile, 0, i)),
            pl.BlockSpec((None, step, D), lambda i: (tile, i, 0)),
            pl.BlockSpec((None, 1, step), lambda i: (0, 0, i)),
            pl.BlockSpec(memory_space=pltpu.SMEM),
        ]
        + [whole(a) for a in past or ()]
        + [ANYWHERE] * len(after),
        out_specs=out_specs,
        out_shape=out_shape,
        scratch_shapes=scratch,
        compiler_params=pltpu.CompilerParams(vmem_limit_bytes=LIMIT),
        cost_estimate=estimate(seqs * rows * D * width * 12, 20e6, seqs * rows * width * 2),
        name="ffn_tile",
    )(h2, og, w_in, w_back, bias, me, *(past or ()), *after)


def rotary_blocks(length):
    half = HDIM // 2
    frequency = jnp.exp(jnp.arange(half, dtype=jnp.float32) * (-2.0 * math.log(10000.0) / HDIM))
    angles = jnp.arange(length, dtype=jnp.float32)[:, None] * frequency[None, :]
    cosine, sine = jnp.cos(angles), jnp.sin(angles)
    return jnp.tile(cosine, (1, 4)), jnp.tile(jnp.concatenate([-sine, sine], axis=1), (1, 2))


def projection_blocks(feature_proj):
    rows = jnp.arange(GF)[:, None] // FEAT
    columns = jnp.arange(GE)[None, :] // HDIM
    mask = (rows == columns).astype(jnp.float32)
    tall = jnp.tile(feature_proj.reshape(GROUPS, GF, HDIM), (1, 1, GROUP)) * mask
    high, low = halves(tall)
    square = jnp.broadcast_to(-0.5 * mask, tall.shape).astype(jnp.bfloat16)
    turned = [a.swapaxes(1, 2) for a in (high, high, low, square, square)]
    return jnp.concatenate(turned, axis=1), jnp.concatenate([high, high, low], axis=1)


def xor_pairs(size, mask):
    return [(index, index ^ mask) for index in range(size)]


def tie(value, *earlier):
    return lax.optimization_barrier((value, earlier))[0]


def swap(value, axis_name, mask):
    return lax.ppermute(value, axis_name, xor_pairs(lax.axis_size(axis_name), mask))


def far_masks(axis_name):
    return [2 * m for m in range(1, lax.axis_size(axis_name) // 2)]


class Gather:
    def __init__(self, pieces, cut, turn=None):
        self.cut = cut
        self.turn = turn or (lambda piece: piece)
        self.pieces = pieces

    def near(self, *earlier):
        self.pieces = [tie(piece, *earlier) for piece in self.pieces] if earlier else self.pieces
        self.first = jnp.stack([piece[..., : -self.cut, :] for piece in self.pieces])
        self.second = jnp.stack([self.turn(piece[..., -self.cut :, :]) for piece in self.pieces])
        self.first_in = swap(self.first, "wide", 1)
        self.second_in = [swap(self.second, "narrow", mask) for mask in far_masks("narrow")]
        return [self.first_in] + self.second_in

    def far(self, *earlier):
        if earlier:
            self.first_in = tie(self.first_in, *earlier)
        self.first = jnp.stack([self.first, self.first_in])
        self.extra = self.first[..., self.cut :, :]
        self.first = self.first[..., : self.cut, :]
        self.second = jnp.stack([self.second] + (list(tie(tuple(self.second_in), *earlier)) if earlier else self.second_in))
        self.first_in = [swap(self.first, "narrow", mask) for mask in far_masks("narrow")]
        self.second_in = swap(self.second, "wide", 1)
        return self.first_in + [self.second_in]

    def core(self, *earlier):
        if earlier:
            late = tie((tuple(self.first_in), self.second_in), *earlier)
            self.first_in, self.second_in = list(late[0]), late[1]
        self.mine = [self.first] + self.first_in + [self.second, self.second_in]
        self.theirs = [swap(part, "narrow", 1) for part in self.mine]
        return self.theirs


def far_wide(piece):
    return [piece] + [swap(piece, "wide", mask) for mask in far_masks("wide")]


def gathered_at(part, index, side, fars, ms):
    m, index = index % ms, index // ms
    half, near, far = (0, index, part) if part < fars else (1, part - fars, index)
    return half, 2 * m + near, 2 * far + side


def placing(copies, fars, ms, me_ref, refs, outs, sems):
    found = []
    for k, ref in enumerate(refs):
        side, part = divmod(k, fars + 2)
        for index in range(ref.shape[0] * ms):
            half, wide_mask, narrow_mask = gathered_at(part, index, side, fars, ms)
            wide, narrow = me_ref[0] ^ wide_mask, me_ref[1] ^ narrow_mask
            for source, target in copies(ref.at[index // ms, index % ms], outs, half, wide, narrow):
                found.append(pltpu.make_async_copy(source, target, sems.at[len(found)]))
    return found


def place_kernel(copies, fars, ms, me_ref, *rest):
    count = 2 * (fars + 2)
    found = placing(copies, fars, ms, me_ref, rest[:count], rest[count:-1], rest[-1])
    for copy in found:
        copy.start()
    for copy in found:
        copy.wait()


def place(me, parts, copies, shapes, name):
    fars, ms = lax.axis_size("narrow") // 2, lax.axis_size("wide") // 2
    return pl.pallas_call(
        partial(place_kernel, copies, fars, ms),
        out_shape=[jax.ShapeDtypeStruct(shape, parts[0].dtype) for shape in shapes],
        in_specs=[pl.BlockSpec(memory_space=pltpu.SMEM)] + [ANYWHERE] * len(parts),
        out_specs=[pl.BlockSpec(memory_space=pltpu.VMEM)] * len(shapes),
        compiler_params=pltpu.CompilerParams(vmem_limit_bytes=LIMIT),
        scratch_shapes=[pltpu.SemaphoreType.DMA((8 * fars * ms,))],
        cost_estimate=estimate(0, 4 * sum(math.prod(shape) for shape in shapes)),
        name=name,
    )(me, *parts)


def in_order(parts, wide_size, narrow_size, place_of):
    my_wide, my_narrow = lax.axis_index("wide"), lax.axis_index("narrow")
    ordered = [
        pick(parts, place_of(w ^ my_wide, n ^ my_narrow), 0) for w in range(wide_size) for n in range(narrow_size)
    ]
    return jnp.stack(ordered).reshape((wide_size, narrow_size) + parts.shape[1:])


def half_in_order(parts, half):
    wide_size, narrow_size = lax.axis_size("wide"), lax.axis_size("narrow")
    fars, ms = narrow_size // 2, wide_size // 2

    def place_of(wide_mask, narrow_mask):
        near, m, side, far = wide_mask & 1, wide_mask >> 1, narrow_mask & 1, narrow_mask >> 1
        outer = far * 2 + near if half == 0 else near * fars + far
        return side * (fars * 2 * ms) + outer * ms + m

    count = len(parts) // 2
    found = []
    for side in range(2):
        own = parts[side * count : (side + 1) * count]
        found += own[:fars] if half == 0 else own[fars:]
    found = [part.reshape((-1,) + part.shape[2:]) for part in found]
    return in_order(jnp.concatenate(found), wide_size, narrow_size, place_of)


def pick(value, index, axis):
    return lax.dynamic_index_in_dim(value, index, axis, keepdims=False)


def core_swap(send):
    return [swap(part, "narrow", 1) for part in send]


def cut_wide(send):
    count = min(4, send.shape[1] // 2)
    width = send.shape[1] // count
    return [lax.slice_in_dim(send, width * k, width * (k + 1), axis=1) for k in range(count)]


def far_all_to_all(pieces):
    groups = [list(range(near, lax.axis_size("wide"), 2)) for near in range(2)]
    return lax.all_to_all(pieces, "wide", 0, 0, axis_index_groups=groups)


class Stream:
    def __init__(self, keep, arrived, order, window=None):
        rest = keep.shape[2:]
        self.quarters, self.wide = len(arrived), keep.shape[1]
        self.window = window or (0, rest[0])
        self.rest = (self.window[1] - self.window[0],) + rest[1:]
        self.order = list(order)
        self.dims = {"y": keep.shape[0], "z": keep.shape[1] // 2, "x": 2}
        self.parts = [part.reshape((1, -1) + rest) for part in [keep] + arrived]

    def plan(self):
        by_all = self.order[0] == "a"
        axis = "z" if by_all else self.order[0]
        names = [name for name in ("y", "z", "x") if name in self.dims]
        sizes = [self.dims[name] for name in names]
        cut = names.index(axis)
        stride = math.prod(sizes[cut + 1 :])
        places = [
            outer * sizes[cut] * stride + inner for outer in range(math.prod(sizes[:cut])) for inner in range(stride)
        ]
        return by_all, axis, sizes[cut], stride, places

    def outputs(self):
        by_all, unused_axis, size, unused_stride, places = self.plan()
        shape = (len(places),) + self.rest
        return [(size,) + shape] if by_all else [(1,) + shape] * size

    def sent(self, pieces):
        axis = self.order.pop(0)
        self.quarters = 0
        del self.dims["z" if axis == "a" else axis]
        self.window = (0, self.rest[0])
        if axis == "a":
            self.parts = list(pieces)
        else:
            name, scale = ("narrow", 2) if axis == "y" else ("wide", 1 if axis == "x" else 2)
            self.parts = [pieces[0]] + [swap(piece, name, scale * m) for m, piece in enumerate(pieces) if m]

    def last(self):
        return [part.reshape((-1,) + self.rest) for part in self.parts]


def fold_kernel(plans, windows, quarters, firsts, me_ref, all_ins, all_outs):
    for (by_all, axis, size, stride, places), (low, high), parts, first, ins, outs in zip(
        plans, windows, quarters, firsts, all_ins, all_outs
    ):
        here = me_ref[1] >> 1 if axis == "y" else me_ref[0] & 1 if axis == "x" else me_ref[0] >> 1
        for step in range(size):
            at = step * stride if by_all else (here ^ step) * stride
            for k, base in enumerate(places):
                found = [(ref, source, base + at) for ref in (ins[:1] if parts else ins) for source in range(ref.shape[0])]
                if parts:
                    wide = parts[1]
                    width = wide // parts[0]
                    far, left = (here ^ step, base) if axis == "y" else (base // wide, base % wide)
                    inner = left % width if axis == "y" else left % width + at
                    found.append((ins[1 + left // width], 0, far * width + inner))
                total = sum(ref[source, place, low:high].astype(jnp.float32) for ref, source, place in found)
                out = outs[0].at[step, first + k] if by_all else outs[step].at[0, k]
                out[...] = total.astype(out.dtype)


def interleaved(kernel, before, extra, in_places, out_places):
    def run(*refs):
        ins, outs = refs[1:before], refs[before + extra :]
        return kernel(
            refs[0], [[ins[k] for k in places] for places in in_places], [[outs[k] for k in places] for places in out_places]
        )

    return run


def fold_streams(streams, me, after):
    plans = [stream.plan() for stream in streams]
    windows = [stream.window for stream in streams]
    quarters = [(stream.quarters, stream.wide) if stream.quarters else None for stream in streams]
    operands, in_places = [], []
    for stream in streams:
        known = [id(part) for part in operands]
        operands += [part for part in stream.parts if id(part) not in known]
        known = [id(part) for part in operands]
        in_places.append([known.index(id(part)) for part in stream.parts])
    shapes, out_places, firsts, joint, joint_at = [], [], [], 0, None
    for stream, plan in zip(streams, plans):
        firsts.append(joint)
        if plan[0] and joint_at is not None:
            out_places.append([joint_at])
        else:
            if plan[0]:
                joint_at = len(shapes)
            out_places.append(list(range(len(shapes), len(shapes) + len(stream.outputs()))))
            shapes += stream.outputs()
        if plan[0]:
            joint += len(plan[4])
    if joint_at is not None:
        shapes[joint_at] = (shapes[joint_at][0], joint) + shapes[joint_at][2:]
    kinds = [None] * len(shapes)
    for stream, places in zip(streams, out_places):
        for k in places:
            kinds[k] = stream.parts[0].dtype
    found = pl.pallas_call(
        interleaved(
            partial(fold_kernel, plans, windows, quarters, firsts), 1 + len(operands), len(after), in_places, out_places
        ),
        in_specs=[pl.BlockSpec(memory_space=pltpu.SMEM)] + [whole_plain(a) for a in operands] + [ANYWHERE] * len(after),
        out_shape=[jax.ShapeDtypeStruct(shape, kind) for shape, kind in zip(shapes, kinds)],
        compiler_params=pltpu.CompilerParams(vmem_limit_bytes=LIMIT),
        cost_estimate=estimate(1e6, 6e6),
        name="fold",
    )(me, *operands, *after)
    token = found[0]
    for stream, plan, places in zip(streams, plans, out_places):
        if not plan[0]:
            stream.sent([found[k] for k in places])
    if joint_at is not None:
        arrived = far_all_to_all(found[joint_at])
        for stream, plan, first in zip(streams, plans, firsts):
            if plan[0]:
                stream.sent([lax.slice_in_dim(arrived, first, first + len(plan[4]), axis=1)])
    return token


def narrow_sum(value):
    mask = 1
    while mask < lax.axis_size("narrow"):
        value = value + swap(value, "narrow", mask)
        mask *= 2
    return value


def exact(left, right, dims=(((1,), (0,)), ((), ()))):
    return lax.dot_general(left, right, dims, precision=PRECISE, preferred_element_type=jnp.float32)


def close(left, right):
    left_high, left_low = halves(left)
    right_high, right_low = halves(right)
    return mm(
        jnp.concatenate([left_high, left_low, left_high], axis=1), jnp.concatenate([right_high, right_high, right_low], axis=0)
    )


def diagonal_of(shape):
    return lax.broadcasted_iota(jnp.int32, shape, 0) == lax.broadcasted_iota(jnp.int32, shape, 1)


def ortho_scale(gram_mat):
    square_sum = jnp.where(diagonal_of(gram_mat.shape), gram_mat, 0.0)
    square_sum = jnp.sum(jnp.sum(square_sum, axis=1, keepdims=True), axis=0, keepdims=True)
    return 1.0 / (jnp.sqrt(square_sum) + ORTHO_EPS)


def sweeps(grams, factors, count, last):
    for left in reversed(range(count)):
        polys = [CUBIC_COEF * gram + QUINTIC_COEF * close(gram, gram) for gram in grams]
        polys = [jnp.where(diagonal_of(poly.shape), poly + LINEAR_COEF, poly) for poly in polys]
        if not left and last:
            return grams, [close(poly, factor) for poly, factor in zip(polys, factors)]
        if factors is None:
            factors, halfway = polys, [close(poly, gram) for poly, gram in zip(polys, grams)]
        else:
            both = [
                close(poly, jnp.concatenate([factor, gram], axis=1)) for poly, factor, gram in zip(polys, factors, grams)
            ]
            factors, halfway = zip(*[(pair[:, : pair.shape[0]], pair[:, pair.shape[0] :]) for pair in both])
        grams = [close(poly, half) for poly, half in zip(polys, halfway)]
    return grams, factors


def apply_factor(factor, block):
    rows = block.shape[0]
    return exact(factor[:rows, :rows], block)


def apply_factor_turned(factor, block):
    rows = block.shape[1]
    return close(block, factor) if rows % 128 == 0 else exact(block, factor[:rows, :rows])


def ortho_start(grams):
    scales = [ortho_scale(gram) for gram in grams]
    return [gram * scale * scale for gram, scale in zip(grams, scales)], scales


def block_pairs(count):
    return [(row, column) for row in range(count) for column in range(row + 1)]


def padded(size):
    return -(-size // 128) * 128


def store_padded(gram, out_ref):
    out_ref[...] = jnp.zeros(out_ref.shape, jnp.float32)
    out_ref[: gram.shape[0], : gram.shape[1]] = gram


def packed_blocks(small, large, out_ref):
    pairs = block_pairs(padded(large.shape[0]) // 128)
    for k, (row, column) in enumerate(pairs):
        store_padded(large[128 * row : 128 * (row + 1), 128 * column : 128 * (column + 1)], out_ref.at[k])
    store_padded(small, out_ref.at[len(pairs)])


def unpacked_blocks(blocks, count):
    pairs = block_pairs(count)
    found = {}
    for k, (row, column) in enumerate(pairs):
        found[row, column] = blocks[k]
        if row != column:
            found[column, row] = blocks[k].T
    large = [jnp.concatenate([found[row, column] for column in range(count)], axis=1) for row in range(count)]
    return blocks[len(pairs)], jnp.concatenate(large, axis=0)


def sweep_kernel(count, *refs):
    blocks, (small_ref, large_ref, small_factor_ref, large_factor_ref) = refs[:-4], refs[-4:]
    grams = unpacked_blocks(sum(ref[...] for ref in blocks), large_ref.shape[0] // 128)
    grams, scales = ortho_start(grams)
    grams, factors = sweeps(grams, None, count, False)
    for gram, factor, scale, gram_ref, factor_ref in zip(
        grams, factors, scales, (small_ref, large_ref), (small_factor_ref, large_factor_ref)
    ):
        gram_ref[...] = gram
        factor_ref[...] = factor * scale


def moment_step(gradient, moment_ref, grad_ref, new_ref, at=(), along=1):
    grad_ref[at + (slice(None), slice(None))] = gradient
    moment = MOMENT_DECAY * moment_ref[at + (slice(None), slice(None))] + gradient
    new_ref[at + (slice(None), slice(None))] = moment
    return exact(moment, moment, (((along,), (along,)), ((), ())))


def sum_of(refs):
    return sum(ref[k].astype(jnp.float32) for ref in refs for k in range(ref.shape[0]))


def take(refs, count):
    return refs[:count], refs[count:]


def attn_moment_kernel(counts, mqkv_ref, mout_ref, *refs):
    left, refs = take(refs, counts[0])
    right, refs = take(refs, counts[1])
    gqkv_ref, gout_ref, nqkv_ref, nout_ref, gram_ref = refs
    left, right = sum_of(left), sum_of(right)
    width = mout_ref.shape[1]
    store_padded(moment_step(left[:, :width], mqkv_ref, gqkv_ref, nqkv_ref, (0,)), gram_ref.at[0])
    store_padded(moment_step(left[:, width:], mqkv_ref, gqkv_ref, nqkv_ref, (1,)), gram_ref.at[1])
    store_padded(moment_step(right[:, :width], mqkv_ref, gqkv_ref, nqkv_ref, (2,)), gram_ref.at[2])
    store_padded(moment_step(right[:, width:], mout_ref, gout_ref, nout_ref), gram_ref.at[3])


def ffn_moment_kernel(counts, unit, min_ref, mback_ref, *refs):
    found = []
    for count in counts:
        part, refs = take(refs, count)
        found.append(sum_of(part))
    gin_ref, gback_ref, nin_ref, nback_ref, blocks_ref = refs
    rows = min_ref.shape[0]
    if len(found) * 128 == mback_ref.shape[1]:
        grad_in = [part[:rows] for part in found]
        turned = [jnp.concatenate([part[rows:, :128], part[rows:, 128:]], axis=0) for part in found]
        turned = jnp.concatenate(turned, axis=1)
    else:
        grad_in, turned = [found[0]], found[1]
    pieces = [part[:, at : at + unit] for at in range(0, grad_in[0].shape[1], unit) for part in grad_in]
    small = moment_step(jnp.concatenate(pieces, axis=1), min_ref, gin_ref, nin_ref)
    packed_blocks(small, moment_step(turned, mback_ref, gback_ref, nback_ref, (), 0), blocks_ref)


def with_own_columns(me_ref, old, width, use):
    for n in range(old.shape[-1] // width):
        pl.when(me_ref[1] == n)(partial(use, old[..., width * n : width * (n + 1)]))


def ortho_kernel(attn_rates, ffn_rates, done, me_ref, *refs):
    parts, refs = refs[:-16], refs[-16:]
    nqkv_ref, nout_ref, wqkv_ref, wout_ref, gin_ref, gback_ref, fin_ref, fback_ref = refs[:8]
    nin_ref, nback_ref, win_ref, wback_ref, vqkv_ref, vout_ref, vin_ref, vback_ref = refs[8:]
    grams, scales = ortho_start([sum(ref[j] for ref in parts) for j in range(4)])
    grams, factors = sweeps(grams, None, done, False)
    grams, factors = list(grams) + [gin_ref[...], gback_ref[...]], list(factors) + [fin_ref[...], fback_ref[...]]
    factors = sweeps(grams, factors, NS_ITERS - done, True)[1]
    ortho_in = apply_factor(factors[4], nin_ref[...])
    ortho_back = apply_factor_turned(factors[5], nback_ref[...])
    for j in range(4):
        new, old, rate = (nqkv_ref[j], wqkv_ref[j], attn_rates[0]) if j < 3 else (nout_ref[...], wout_ref[...], attn_rates[1])
        ortho = apply_factor(factors[j] * scales[j], new)

        def store(own, j=j, rate=rate, ortho=ortho):
            value = own * (1.0 - rate * WEIGHT_DECAY) - rate * ortho
            if j < 3:
                vqkv_ref[j] = value
            else:
                vout_ref[...] = value

        with_own_columns(me_ref, old, ortho.shape[1], store)

    def store_in(own):
        vin_ref[...] = own * (1.0 - ffn_rates[0] * WEIGHT_DECAY) - ffn_rates[0] * ortho_in

    def store_back(own):
        vback_ref[...] = own.T * (1.0 - ffn_rates[1] * WEIGHT_DECAY) - ffn_rates[1] * ortho_back

    with_own_columns(me_ref, win_ref[...], ortho_in.shape[1], store_in)
    with_own_columns(me_ref, wback_ref[...], ortho_back.shape[0], store_back)


def simple_call(kernel, args, shapes, name, flops, after=()):
    def run(*refs):
        kernel(*refs[: len(args)], *refs[len(args) + len(after) :])

    return pl.pallas_call(
        run,
        in_specs=[whole_plain(a) for a in args] + [pl.BlockSpec(memory_space=pl.ANY)] * len(after),
        out_shape=[jax.ShapeDtypeStruct(shape, jnp.float32) for shape in shapes],
        compiler_params=pltpu.CompilerParams(vmem_limit_bytes=LIMIT),
        cost_estimate=estimate(flops, 4e6),
        name=name,
    )(*args, *after)


def whole_plain(array):
    return pl.BlockSpec(memory_space=pltpu.SMEM if array.dtype == jnp.int32 else pltpu.VMEM)


def adam_update(param, earlier_first, earlier_second, gradient):
    first_new = FIRST_DECAY * earlier_first + (1.0 - FIRST_DECAY) * gradient
    second_new = SECOND_DECAY * earlier_second + (1.0 - SECOND_DECAY) * gradient * gradient
    first_fix = 1.0 - FIRST_DECAY**ADAM_STEP
    second_fix = 1.0 - SECOND_DECAY**ADAM_STEP
    direction = first_new / first_fix / (jnp.sqrt(second_new / second_fix) + ADAM_EPS)
    return (first_new, second_new, param - VECTOR_RATE * (direction + WEIGHT_DECAY * param))


def per_device(
    block_in,
    out_grad,
    lengths,
    feature_proj,
    attn_in,
    attn_out,
    ffn_in,
    ffn_out,
    norm_params,
    bias_in,
    bias_out,
    mom_attn_in,
    mom_attn_out,
    mom_ffn_in,
    mom_ffn_out,
    first_norms,
    first_bias_in,
    first_bias_out,
    second_norms,
    second_bias_in,
    second_bias_out,
):
    seqs, length, unused_width = block_in.shape
    wide_size, narrow_size = lax.axis_size("wide"), lax.axis_size("narrow")
    column = lax.axis_index("narrow")
    own_rows, own_cols = D // wide_size, D // narrow_size
    ffn_rows = FF // wide_size
    tiles = ffn_rows // 128 if ffn_rows % 128 == 0 else 1
    unit = ffn_rows // tiles
    width = unit * wide_size
    copied = narrow_size == 4 and own_rows % 16 == 0 and unit % 32 == 0 and (width // narrow_size) % 128 == 0
    blocks = unit == 128 and width // narrow_size == 256 and own_cols == 2 * own_rows
    bf = jnp.bfloat16

    me = jnp.stack([lax.axis_index("wide"), column]).astype(jnp.int32)

    small = jnp.concatenate([norm_params.reshape(-1), bias_in, bias_out]).astype(bf)
    small_size = small.shape[0]
    part = 4 * D // narrow_size
    four = jnp.concatenate([attn_in.astype(bf), attn_out.astype(bf)[None]])
    if part == D:
        four = pick(four, column, 0)
    else:
        four = lax.dynamic_slice_in_dim(four.transpose(1, 0, 2).reshape(own_rows, 4 * D), column * part, part, 1)
    small = jnp.pad(small, (0, -small_size % (8 * part))).reshape(-1, part)
    split = own_rows // 2
    four_gather = Gather(far_wide(jnp.concatenate([four[:split], small, four[split:]])), split)

    in_part = width // narrow_size
    back_part = unit // narrow_size
    folds = D // in_part
    low_in = ffn_in.astype(bf).reshape(own_rows, wide_size, tiles, unit).transpose(2, 0, 1, 3).reshape(tiles, own_rows, width)
    low_in = lax.dynamic_slice_in_dim(low_in, column * in_part, in_part, 2)
    low_back = lax.dynamic_slice_in_dim(ffn_out.reshape(tiles, unit, D), column * back_part, back_part, 1).astype(bf)
    low_back = low_back.reshape(tiles, back_part, folds, in_part).transpose(0, 2, 1, 3).reshape(tiles, own_rows, in_part)
    low_ffn = jnp.concatenate([low_in, low_back], axis=1)

    def as_rows(piece):
        return piece.reshape(-1, folds, back_part, in_part).swapaxes(1, 2).reshape(-1, back_part, D)

    four_gather.near()
    ffn_far = far_wide(tie(low_ffn, *four_gather.pieces[1:]))
    middle_piece = len(ffn_far) // 2
    four_far = four_gather.far(ffn_far[middle_piece])
    four_gather.second_in = tie(four_gather.second_in, *ffn_far[1:])
    four_gather.core()
    ffn_gather = Gather(ffn_far, own_rows, as_rows)
    early = ffn_gather.near(*four_far)
    four_parts = four_gather.mine + four_gather.theirs
    ms = wide_size // 2
    small_all = in_order(
        four_gather.extra.reshape((-1,) + small.shape), wide_size, 1, lambda w, n: (w & 1) * ms + (w >> 1)
    )
    small_all = small_all.reshape(wide_size, -1)[:, :small_size].astype(jnp.float32)
    norm_all = small_all[:, : 4 * own_rows].reshape(wide_size, 4, own_rows).transpose(1, 0, 2).reshape(4, D)
    bias_in_all = small_all[:, 4 * own_rows : 4 * own_rows + ffn_rows].reshape(wide_size, tiles, unit)
    bias_in_all = bias_in_all.transpose(1, 0, 2).reshape(tiles, 1, width)
    bias_out_all = small_all[:, 4 * own_rows + ffn_rows :].reshape(1, D)
    vectors = jnp.concatenate([norm_all, bias_out_all, jnp.zeros((3, D), jnp.float32)])

    def four_copies(piece, outs, half, w, n):
        return [(piece, outs[0].at[n, pl.ds(w * own_rows + half * split, split)])]

    def ffn_copies(piece, outs, half, w, n):
        if half == 0:
            return [(piece, outs[0].at[:, pl.ds(w * own_rows, own_rows), pl.ds(n * in_part, in_part)])]
        return [(piece, outs[1].at[:, pl.ds(w * unit + n * back_part, back_part)])]

    if copied:
        (weights,) = place(me, four_parts, four_copies, [(4, D, D)], "place_four")
    else:
        weights = jnp.stack([half_in_order(four_parts, half) for half in range(2)], axis=2)
        weights = weights.transpose(0, 2, 3, 1, 4).reshape(D, 4, D).transpose(1, 0, 2)

    cosine, sine = rotary_blocks(length)
    proj, projt = projection_blocks(feature_proj)
    middle, h1, h2, *kept, mixed = attend(lengths, block_in, weights, vectors, proj, cosine, sine, early)
    ffn_gather.far()
    ffn_gather.core(middle)
    ffn_parts = ffn_gather.mine + ffn_gather.theirs
    if copied:
        w_in, w_back = place(me, ffn_parts, ffn_copies, [(tiles, D, width), (tiles, width, D)], "place_ffn")
    else:
        w_in = half_in_order(ffn_parts, 0).transpose(2, 0, 3, 1, 4).reshape(tiles, D, width)
        w_back = half_in_order(ffn_parts, 1).transpose(2, 0, 1, 3, 4).reshape(tiles, width, D)
    past, token = None, []
    streams, bias_sums = [], []
    orders = ["yzx", "yxa", "xya"]
    for tile in range(tiles):
        ffn, grad_h2, bias_sum, *grad_tile = ffn_tile(
            tile, h2, out_grad, w_in, w_back, bias_in_all[tile : tile + 1], me, past, wide_size, narrow_size, blocks, token
        )
        past = (ffn, grad_h2)
        bias_sums.append(bias_sum)
        token = [fold_streams(streams[:1], me, [bias_sum])] if tile == 1 else []
        if blocks:
            keep, *send = grad_tile
            streams.append(Stream(keep, core_swap(send), orders[tile % 3]))
        else:
            grad_in = grad_tile[0][0].reshape(wide_size, own_rows, narrow_size, in_part).transpose(2, 0, 1, 3)
            grad_back = grad_tile[0][1].reshape(narrow_size, own_cols, wide_size, unit).transpose(0, 2, 1, 3)
            for found, order in ((grad_in, "yxz"), (grad_back, "xyz")):
                found = found.reshape((narrow_size // 2, 2) + found.shape[1:])
                arrived = core_swap(cut_wide(pick(found, 1 - (column & 1), 1)))
                streams.append(Stream(pick(found, column & 1, 1), arrived, order))
    ffn = tie(ffn, *streams[0].parts[1:])
    grad_middle, gb, sums_two = middle_back(out_grad, grad_h2, middle, vectors, narrow_size)

    def fold_open(more, after):
        found = more + [stream for stream in streams if stream.order]
        done = [part for stream in streams if not stream.order for part in stream.parts]
        return fold_streams(found, me, after + done)

    token = fold_open([], [sums_two])
    gq, gk, gv = attend_back(lengths, grad_middle, weights, projt, cosine, sine, kept, narrow_size, [token])
    token = fold_open([], [gq])
    send = attn_weights(me, h1, mixed, (gq, gk, gv, gb), wide_size, 1, [token])
    (keep,) = attn_weights(me, h1, mixed, (gq, gk, gv, gb), wide_size, 0, send[:1])
    arrived = core_swap(send)
    left = Stream(keep, arrived, "xzy", (0, own_rows))
    right = Stream(keep, arrived, "yxz", (own_rows, 2 * own_rows))
    right.parts = left.parts
    token = fold_open([left, right], [keep])
    input_grad, sums_one = input_back(block_in, grad_middle, (gq, gk, gv), weights, vectors, [token])

    norm_sums = jnp.concatenate([sums_one[:2], sums_two[:2], sums_two[2:3]])
    inner_sums = jnp.concatenate(bias_sums).reshape(tiles, wide_size, unit).transpose(1, 0, 2)
    inner_sums = inner_sums.reshape(wide_size, narrow_size, ffn_rows // narrow_size)
    norm_part = own_rows // narrow_size
    norm_sums = norm_sums.reshape(5, wide_size, narrow_size, norm_part).transpose(1, 2, 0, 3).reshape(wide_size, narrow_size, -1)
    vector_parts = jnp.concatenate([norm_sums, inner_sums], axis=2).swapaxes(0, 1)
    vector_size = vector_parts.shape[2]
    vector_parts = jnp.pad(vector_parts, ((0, 0), (0, 0), (0, -vector_size % 128)))
    vector_parts = vector_parts.reshape(narrow_size // 2, 2, wide_size, 1, -1)
    vector_send = tie(pick(vector_parts, 1 - (column & 1), 1), *left.parts[1:], *right.parts[1:])
    vector = Stream(pick(vector_parts, column & 1, 1), core_swap([vector_send]), "yxz")
    token = fold_streams([left, right, vector], me, [sums_one])
    sum_parts = [stream.last() for stream in streams]
    small_size, large_size = padded(own_rows), padded(ffn_rows)
    block_count = len(block_pairs(large_size // 128)) + small_size // 128
    grad_in_w, grad_back_w, mom_in_new, mom_back_new, blocks_gram = simple_call(
        partial(ffn_moment_kernel, [len(parts) for parts in sum_parts], unit),
        [mom_ffn_in, mom_ffn_out.T] + sum(sum_parts, []),
        [mom_ffn_in.shape, mom_ffn_out.T.shape] * 2 + [(block_count, 128, 128)],
        "ffn_moment",
        1e9,
        [token],
    )
    block_out = layer_output(ffn, middle, vectors, [mom_in_new])
    token = fold_streams([left, right, vector], me, [mom_in_new, block_out])
    blocks_gram = tie(blocks_gram, token)
    blocks_near = blocks_gram + swap(blocks_gram, "narrow", 1)
    blocks_all = [blocks_near] + [swap(blocks_near, "narrow", mask) for mask in far_masks("narrow")]
    token = fold_streams([vector], me, [blocks_near])
    left_parts, right_parts = left.last(), right.last()
    def own_columns(weight):
        block_width = weight.shape[-1] // narrow_size
        return lax.dynamic_slice_in_dim(
            weight, column * block_width, block_width, axis=weight.ndim - 1
        )

    rate_qkv = MUON_SCALE
    rate_out = MUON_SCALE * math.sqrt(D / (D // 64))
    rate_in = MUON_SCALE * math.sqrt(FF / D)
    rate_back = MUON_SCALE * math.sqrt(D / FF)
    shapes = [mom_attn_in.shape, mom_attn_out.shape]
    grad_qkv, grad_out_w, mom_qkv_new, mom_out_new, gram_four = simple_call(
        partial(attn_moment_kernel, (len(left_parts), len(right_parts))),
        [mom_attn_in, mom_attn_out] + left_parts + right_parts,
        shapes + shapes + [(4, padded(own_rows), padded(own_rows))],
        "attn_moment",
        1e9,
        [token],
    )
    gram_near = gram_four + swap(gram_four, "narrow", 1)
    sweep_in, sweep_back, factor_in, factor_back = simple_call(
        partial(sweep_kernel, 2),
        blocks_all,
        [(small_size, small_size), (large_size, large_size)] * 2,
        "ffn_sweeps",
        1e10,
        [gram_four],
    )
    vector_sums = sum(jnp.sum(part, axis=0) for part in vector.last())[0, :vector_size]
    grad_norm_vals = vector_sums[: 4 * norm_part].reshape(4, norm_part)
    grad_bias_final = vector_sums[4 * norm_part : 5 * norm_part]
    grad_bias_inner = vector_sums[5 * norm_part :]
    gram_all = [gram_near] + [swap(gram_near, "narrow", mask) for mask in far_masks("narrow")]
    new_qkv, new_out, new_in, new_back = simple_call(
        partial(ortho_kernel, (rate_qkv, rate_out), (rate_in, rate_back), 2),
        [me, *gram_all, mom_qkv_new, mom_out_new, attn_in, attn_out]
        + [sweep_in, sweep_back, factor_in, factor_back, mom_in_new, mom_back_new, ffn_in, ffn_out],
        [mom_attn_in.shape, mom_attn_out.shape, mom_ffn_in.shape, mom_ffn_out.T.shape],
        "ortho",
        1e10,
    )
    norm_first, norm_second, norm_new = adam_update(
        own_columns(norm_params), first_norms, second_norms, grad_norm_vals
    )
    inner_first, inner_second, inner_new = adam_update(
        own_columns(bias_in), first_bias_in, second_bias_in, grad_bias_inner
    )
    final_first, final_second, final_new = adam_update(
        own_columns(bias_out), first_bias_out, second_bias_out, grad_bias_final
    )
    return (
        block_out,
        input_grad,
        grad_qkv,
        grad_out_w,
        grad_in_w,
        grad_back_w.T,
        grad_norm_vals,
        grad_bias_inner,
        grad_bias_final,
        mom_qkv_new,
        mom_out_new,
        mom_in_new,
        mom_back_new.T,
        new_qkv,
        new_out,
        new_in,
        new_back.T,
        norm_first,
        inner_first,
        final_first,
        norm_second[:2],
        norm_second[2:],
        inner_second,
        final_second,
        norm_new,
        inner_new,
        final_new,
    )


def solution(mesh):
    in_specs = (
        P(("wide", "narrow"), None, None),
        P(("wide", "narrow"), None, None),
        P(("wide", "narrow")),
        P(),
        P(None, "wide", None),
        P("wide", None),
        P("wide", None),
        P("wide", None),
        P(None, "wide"),
        P("wide"),
        P("wide"),
        P(None, "wide", "narrow"),
        P("wide", "narrow"),
        P("wide", "narrow"),
        P("wide", "narrow"),
        P(None, ("wide", "narrow")),
        P(("wide", "narrow")),
        P(("wide", "narrow")),
        P(None, ("wide", "narrow")),
        P(("wide", "narrow")),
        P(("wide", "narrow")),
    )
    out_specs = (
        P(("wide", "narrow"), None, None),
        P(("wide", "narrow"), None, None),
        P(None, "wide", "narrow"),
        P("wide", "narrow"),
        P("wide", "narrow"),
        P("wide", "narrow"),
        P(None, ("wide", "narrow")),
        P(("wide", "narrow")),
        P(("wide", "narrow")),
        P(None, "wide", "narrow"),
        P("wide", "narrow"),
        P("wide", "narrow"),
        P("wide", "narrow"),
        P(None, "wide", "narrow"),
        P("wide", "narrow"),
        P("wide", "narrow"),
        P("wide", "narrow"),
        P(None, ("wide", "narrow")),
        P(("wide", "narrow")),
        P(("wide", "narrow")),
        P(None, ("wide", "narrow")),
        P(None, ("wide", "narrow")),
        P(("wide", "narrow")),
        P(("wide", "narrow")),
        P(None, ("wide", "narrow")),
        P(("wide", "narrow")),
        P(("wide", "narrow")),
    )
    return jax.shard_map(
        per_device, mesh=mesh, in_specs=in_specs, out_specs=out_specs, check_vma=False
    )
```
